32 devices in a mesh: batch: 4 (over z), ha: 4 (over y, x), wa: 2 (over core).
Axes of the slice: x: 2, y: 2, z: 4, core: 2. Of those that a mesh axis runs over, the one named last changes fastest.
Arguments:
- block_input: bfloat16 [32, 8, 12, 10, 256], P('batch', None, 'ha', 'wa'), may hold values from -6 to 6
- cotangent: bfloat16 [32, 8, 12, 10, 256], P('batch', None, 'ha', 'wa'), may hold values from -6 to 6
- frame_sides: int32 [4], P('batch'), may hold values from 7 to 10, as said below
- owner_list: int32 [1728, 1], replicated, may hold values from 0 to 31; in each aligned block of 1728 rows (0 to 1727, 1728 to 3455, ...) at most 55 rows name the same one
- master_slots: float32 [1760, 2048], P(('batch', 'ha', 'wa')), may hold values from -0.125 to 0.125
- first_slots: float32 [1760, 2048], P(('batch', 'ha', 'wa')), may hold values from -320 to 320
- second_slots: float32 [1760, 2048], P(('batch', 'ha', 'wa')), may hold values from 3072 to 12288
- norm_gains: float32 [1664], replicated, may hold values from 0.25 to 1.75
- norm_biases: float32 [1664], replicated, may hold values from -3 to 3
- norm_first: float32 [2, 1664], replicated, may hold values from -320 to 320
- norm_second: float32 [2, 1664], replicated, may hold values from 3072 to 12288
Outputs:
- block_output: float32 [32, 8, 12, 10, 256], P('batch', None, 'ha', 'wa')
- input_grad: float32 [32, 8, 12, 10, 256], P('batch', None, 'ha', 'wa')
- master_new: float32 [1760, 2048], P(('batch', 'ha', 'wa'))
- first_new: float32 [1760, 2048], P(('batch', 'ha', 'wa'))
- second_new: float32 [1760, 2048], P(('batch', 'ha', 'wa'))
- weight_copy: bfloat16 [1760, 2048], P(('batch', 'ha', 'wa'))
- norm_first_new: float32 [2, 1664], replicated
- norm_second_new: float32 [2, 1664], replicated
- norm_new: float32 [2, 1664], replicated
The draws below stay inside these ranges and needn't reach their ends.
Inputs may be any that keep to these rules, and one draw needn't show every extreme that they name: `owner_list`: every device owns at least one piece and at most 55; some device owns exactly 55. `frame_sides`: each entry is 7 or 10, and both occur.
All inputs are finite; a program needn't handle non-finite values.
Results may differ from the reference program's by a relative error of at most 0.012.
The reference program's roundings to bfloat16 on the way count: a program that leaves them out, or rounds other values in their place, can miss the bound.
Values may be sent and summed in bfloat16 or wider, within the bound.
No kernel may reach another device: no remote copies, remote signals or barrier semaphores. Data moves between devices by JAX's collectives and lax.ppermute only.
A program may use at most 192 MiB of HBM per device.

```python
import math
from functools import partial
import jax
import jax.numpy as jnp
import numpy as np
from jax import lax

D = 256
MID = 576
CLIPS = 8
FRAMES = 8
TH = 3
TW = 5
PIECE = 2048
STEP = 5
SHARDS = 4
CLIPS_ALL = 32
GH = 12
GW = 10
PIECES = 1728
SLOTS = 55
NORMS = 1664
N_BATCH = 4
N_HA = 4
N_WA = 2
DEVICES = 32


def draw_frame_sides(key, part):
    key = jax.random.fold_in(key, 11)
    flip_key = jax.random.fold_in(key, 1)
    order_key = jax.random.fold_in(key, 2)
    coin_flips = jax.random.randint(flip_key, (SHARDS,), 0, 2)
    shuffled = jax.random.permutation(order_key, SHARDS)
    coin_flips = coin_flips.at[shuffled[0]].set(1).at[shuffled[1]].set(0)
    return (7 + 3 * coin_flips).astype(jnp.int32)


def level_of(own_key, extent, cuts, smallest, top_value):
    loudness = 1.0
    for position, blocks in cuts:
        heights = jax.random.uniform(jax.random.fold_in(jax.random.fold_in(own_key, 6), position), (blocks,), jnp.float32, smallest / len(cuts), top_value / len(cuts))
        loudness = loudness * jnp.repeat(jnp.exp(heights), extent[position] // blocks).reshape((-1,) + (1,) * (len(extent) - 1 - position))
    return loudness


def routed_block(key, own, number, rows, number_of, top, reach, slope):
    sequence = jax.random.permutation(key, number_of)
    crowded, common = portions_of(number_of, rows * top, reach, slope, True), portions_of(number_of, rows * top, reach, slope, False)
    places = jnp.arange(number_of)

    def named(lengths, turn):
        used = int((lengths > 0).sum())
        fixed = max(1, used // 4)
        passed = fixed + (places - fixed + turn * (used - fixed)) % max(1, number_of - fixed)
        return jnp.zeros((number_of,), jnp.int32).at[sequence[jnp.where(places < fixed, places, passed)]].set(jnp.asarray(lengths, jnp.int32))

    lengths = jnp.where(number % 4 == 0, named(crowded, number // 4), named(common, number - number // 4 - 1))
    mixed = jax.random.permutation(jax.random.fold_in(own, 3), number_of)
    source_of, sink = mixed[0:number_of // 2 * 2:2], mixed[1:number_of // 2 * 2:2]
    slack = jnp.minimum(lengths[source_of] - 1, reach - lengths[sink]) // 2
    slack = jnp.where((source_of == sequence[0]) | (sink == sequence[0]) | (lengths[sink] == 0), 0, jnp.maximum(slack, 0))
    passed = jax.random.randint(jax.random.fold_in(own, 4), (number_of // 2,), 0, 1 << 20) % (slack + 1)
    lengths = lengths.at[source_of].add(-passed).at[sink].add(passed)
    members = jnp.searchsorted(jnp.cumsum(lengths), jnp.arange(rows * top), side="right").astype(jnp.int32)
    table = members.reshape(top, rows).T
    table = table[jax.random.permutation(jax.random.fold_in(own, 1), rows)]
    turn = jax.random.randint(jax.random.fold_in(own, 2), (rows, 1), 0, top)
    return jnp.take_along_axis(table, (jnp.arange(top)[None, :] + turn) % top, axis=1)


def portions_of(amount, total, limit, lean, full):
    loads = [(1 << 20) // math.isqrt(grade ** lean) + 1 for grade in range(1, amount + 1)]
    largest = limit if full else min(limit, max(-(-total // amount), total * loads[0] // sum(loads)))
    least = 1 if total - largest >= amount - 1 else 0
    counts, rest = [largest] + [least] * (amount - 1), total - largest - least * (amount - 1)
    while rest > 0:
        free = [i for i in range(1, amount) if counts[i] < largest] or [i for i in range(1, amount) if counts[i] < limit]
        whole, left = sum([loads[i] for i in free]), rest
        for i in free:
            extra = min(limit - counts[i], max(1, left * loads[i] // whole), rest)
            counts[i] = counts[i] + extra
            rest = rest - extra
    return np.array(counts)


def bell_draw(rng, extent, width, most, split=(), held_as=jnp.bfloat16):
    gain = level_of(rng, extent, split, -0.22, 0.18) if split else 1.0
    entries = jax.random.normal(rng, extent, jnp.float32) * width * gain
    return jnp.minimum(jnp.maximum(entries, -most), most).astype(held_as)


def setup_inputs(seed: int = 0) -> dict:
    key_of = jax.random.split(jax.random.key(seed), 12)
    block_input = bell_draw(key_of[0], (CLIPS_ALL, FRAMES, GH, GW, D), 1.0, 6.0, ((0, 4), (2, 4), (3, 2)))
    cotangent = bell_draw(key_of[1], (CLIPS_ALL, FRAMES, GH, GW, D), 1.0, 6.0, ((0, 4), (2, 4), (3, 2)))
    frame_sides = draw_frame_sides(jax.random.fold_in(key_of[11], 71), 0)
    owner_list_keys = jax.random.split(jax.random.fold_in(key_of[3], 1), PIECES // PIECES)
    owner_list_turns = jax.random.permutation(jax.random.fold_in(key_of[3], 3), PIECES // PIECES)
    owner_list = jax.vmap(lambda own, number: routed_block(jax.random.fold_in(key_of[3], 2), own, number, PIECES, DEVICES, 1, SLOTS, 2))(owner_list_keys, owner_list_turns).reshape((PIECES, 1))
    master_slots = bell_draw(key_of[4], (DEVICES * SLOTS, PIECE), (9 * D) ** -0.5, 0.125, ((0, 32),), jnp.float32)
    first_slots = bell_draw(key_of[5], (DEVICES * SLOTS, PIECE), (0.4 * (SHARDS * CLIPS * FRAMES * 75) ** 0.5), 320.0, ((0, 32),), jnp.float32)
    second_slots = jnp.clip(jnp.exp(math.log(12288.0) - 1.3862944 * jax.random.uniform(key_of[6], (DEVICES * SLOTS, PIECE), jnp.float32) ** level_of(key_of[6], (DEVICES * SLOTS, PIECE), ((0, 32),), -0.2, 0.2)), 3072.0, 12288.0)
    norm_gains = jnp.clip(1.0 + 0.15 * jax.random.normal(key_of[7], (NORMS,), jnp.float32), 0.25, 1.75)
    norm_biases = bell_draw(key_of[8], (NORMS,), 0.5, 3.0, (), jnp.float32)
    norm_first = bell_draw(key_of[9], (2, NORMS), (0.4 * (SHARDS * CLIPS * FRAMES * 75) ** 0.5), 320.0, (), jnp.float32)
    norm_second = jnp.clip(jnp.exp(jax.random.uniform(key_of[10], (2, NORMS), jnp.float32, math.log(3072.0), math.log(12288.0))), 3072.0, 12288.0)
    return {"block_input": block_input, "cotangent": cotangent, "frame_sides": frame_sides, "owner_list": owner_list, "master_slots": master_slots, "first_slots": first_slots, "second_slots": second_slots, "norm_gains": norm_gains, "norm_biases": norm_biases, "norm_first": norm_first, "norm_second": norm_second}


@jax.custom_vjp
def low(v):
    return lax.optimization_barrier(v.astype(jnp.bfloat16)).astype(jnp.float32)

@jax.custom_vjp
def low_back(v):
    return v

def low_keep(v):
    return (low(v), None)

def low_pass(kept, grad):
    return (grad,)

def back_keep(v):
    return (v, None)

def back_low(kept, grad):
    return (low(grad),)
low.defvjp(low_keep, low_pass)
low_back.defvjp(back_keep, back_low)
EPSILON = 1e-05
ADAM_EPSILON = 1e-08
DECAY_RATE = 0.1
NORM_RATE = 0.3
HIGHEST_PRECISION = lax.Precision.HIGHEST

def slot_of_pieces(owner_list, slot_count, device_total):
    owner_ids = owner_list[:, 0].astype(jnp.int32)
    onehot = (owner_ids[:, None] == jnp.arange(device_total, dtype=jnp.int32)[None, :]).astype(jnp.int32)
    earlier = jnp.cumsum(onehot, axis=0) - onehot
    ranking = lax.optimization_barrier(jnp.sum(earlier * onehot, axis=1))
    return (owner_ids * slot_count + ranking).astype(jnp.int32)

def spatial_conv(values, weight):
    in_width = values.shape[-1]
    kernel = weight.reshape(3, 3, in_width, weight.shape[1])
    padded = jnp.pad(values, ((0, 0), (0, 0), (1, 1), (1, 1), (0, 0)))
    height = values.shape[2]
    breadth = values.shape[3]
    result = None
    for row_tap in range(3):
        for col_tap in range(3):
            window = padded[:, :, row_tap:row_tap + height, col_tap:col_tap + breadth, :]
            term = jnp.einsum('bfhwc,co->bfhwo', window, kernel[row_tap, col_tap], precision=HIGHEST_PRECISION)
            result = term if result is None else result + term
    return result

def temporal_conv(values, weight):
    in_width = values.shape[-1]
    kernel = weight.reshape(3, in_width, weight.shape[1])
    padded = jnp.pad(values, ((0, 0), (1, 1), (0, 0), (0, 0), (0, 0)))
    frames = values.shape[1]
    result = None
    for offset in range(3):
        window = padded[:, offset:offset + frames]
        term = jnp.einsum('bfhwc,co->bfhwo', window, kernel[offset], precision=HIGHEST_PRECISION)
        result = term if result is None else result + term
    return result

def batch_norm(values, valid_mask, cell_count, norm_gain, norm_bias):
    channel_mean = lax.optimization_barrier(jnp.sum(values * valid_mask, axis=(0, 1, 2, 3))) / cell_count
    centered = (values - channel_mean) * valid_mask
    variance = lax.optimization_barrier(jnp.sum(centered * centered, axis=(0, 1, 2, 3))) / cell_count
    return (values - channel_mean) * lax.rsqrt(variance + EPSILON) * norm_gain + norm_bias

def block_forward(inputs, spatial_one, temporal_one, spatial_two, temporal_two, norm_pair, valid_mask, cell_count):
    middle = spatial_one.shape[1]
    model_width = temporal_one.shape[1]
    bounds = [0, middle, middle + model_width, 2 * middle + model_width, 2 * middle + 2 * model_width]

    def norm_at(values, index):
        return batch_norm(values, valid_mask, cell_count, norm_pair[0, bounds[index]:bounds[index + 1]], norm_pair[1, bounds[index]:bounds[index + 1]])

    def unit(values, spatial_w, temporal_w, index):
        spatial = low_back(spatial_conv(low(values), spatial_w))
        inner = jax.nn.silu(norm_at(spatial, index)) * valid_mask
        temporal = low_back(temporal_conv(low(inner), temporal_w))
        return norm_at(temporal, index + 1)
    start = inputs * valid_mask
    first = jax.nn.silu(unit(start, spatial_one, temporal_one, 0)) * valid_mask
    second = unit(first, spatial_two, temporal_two, 2)
    return jax.nn.silu(second + start) * valid_mask

def reference(block_input, cotangent, frame_sides, owner_list, master_slots, first_slots, second_slots, norm_gains, norm_biases, norm_first, norm_second):
    device_total = N_BATCH * N_HA * N_WA
    slot_count = master_slots.shape[0] // device_total
    grid_rows = TH * N_HA
    grid_cols = TW * N_WA
    clip_sides = jnp.repeat(frame_sides.astype(jnp.int32), CLIPS)
    row_ids = jnp.arange(grid_rows, dtype=jnp.int32)
    col_ids = jnp.arange(grid_cols, dtype=jnp.int32)
    valid_rows = row_ids[None, :, None] >= (grid_rows - clip_sides)[:, None, None]
    valid_cols = col_ids[None, None, :] >= (grid_cols - clip_sides)[:, None, None]
    valid_mask = (valid_rows & valid_cols).astype(jnp.float32)[:, None, :, :, None]
    cell_count = FRAMES * jnp.sum(valid_mask)
    slot_index = slot_of_pieces(owner_list, slot_count, device_total)
    low_weights = master_slots.astype(jnp.bfloat16).astype(jnp.float32)[slot_index].reshape(-1)
    spatial_len = 9 * D * MID
    temporal_len = 3 * MID * D
    spatial_one = low_weights[:spatial_len].reshape(9 * D, MID)
    temporal_one = low_weights[spatial_len:spatial_len + temporal_len].reshape(3 * MID, D)
    second_base = spatial_len + temporal_len
    spatial_two = low_weights[second_base:second_base + spatial_len].reshape(9 * D, MID)
    temporal_two = low_weights[second_base + spatial_len:2 * second_base].reshape(3 * MID, D)
    norm_pair = jnp.stack([norm_gains, norm_biases])
    forward = partial(block_forward, valid_mask=valid_mask, cell_count=cell_count)
    block_output, pullback = jax.vjp(forward, block_input.astype(jnp.float32), spatial_one, temporal_one, spatial_two, temporal_two, norm_pair)
    grads = pullback(cotangent.astype(jnp.float32))
    grad_flat = jnp.concatenate([grads[1].reshape(-1, PIECE), grads[2].reshape(-1, PIECE), grads[3].reshape(-1, PIECE), grads[4].reshape(-1, PIECE)], axis=0)
    grad_slots = jnp.zeros((device_total * slot_count, PIECE), jnp.float32).at[slot_index].set(grad_flat)
    correction = 1.0 - 0.5 ** STEP
    step_rate = 1.8 / (9.0 * D) ** 0.5
    first_new = 0.5 * first_slots + 0.5 * grad_slots
    second_new = 0.5 * second_slots + 0.5 * grad_slots * grad_slots
    master_new = master_slots - step_rate * (first_new / correction / (jnp.sqrt(second_new / correction) + ADAM_EPSILON) + DECAY_RATE * master_slots)
    weight_copy = master_new.astype(jnp.bfloat16)
    norm_grad = grads[5]
    norm_first_new = 0.5 * norm_first + 0.5 * norm_grad
    norm_second_new = 0.5 * norm_second + 0.5 * norm_grad * norm_grad
    norm_new = norm_pair - NORM_RATE * (norm_first_new / correction) / (jnp.sqrt(norm_second_new / correction) + ADAM_EPSILON)
    return (block_output, grads[0], master_new, first_new, second_new, weight_copy, norm_first_new, norm_second_new, norm_new)
```

```python
import functools
import math

import jax
import jax.numpy as jnp
from jax import lax
from jax.experimental import pallas as pl
from jax.experimental.pallas import tpu as pltpu
from jax.sharding import PartitionSpec as P

STEP = 5
EPSILON = 1e-05
ADAM_EPSILON = 1e-08
DECAY_RATE = 0.1
NORM_RATE = 0.3

AXES = ("batch", "ha", "wa")
F32 = jnp.float32
BF16 = jnp.bfloat16
VMEM = pl.BlockSpec(memory_space=pltpu.VMEM)
SMEM = pl.BlockSpec(memory_space=pltpu.SMEM)
CELL = 64
LANES = 128
PIECE_ROWS = 16


def sigmoid(v):
    return 1.0 / (1.0 + jnp.exp(-v))


def cell_rows(index, count=1):
    return pl.ds(pl.multiple_of(index * CELL, CELL), count * CELL)


def block_rows(index, size):
    return pl.ds(pl.multiple_of(index * size, size), size)


def fold8(block):
    return jnp.sum(block.reshape(-1, 8, block.shape[-1]), axis=0)


def widen(lane_block, width):
    return jnp.concatenate([lane_block] * (width // LANES), axis=1)


def valid_rows(valid_ref, cells):
    total = valid_ref[0]
    for cell in range(1, cells):
        total = total + valid_ref[cell]
    return total * CELL


def send_stats(values_ref, valid_ref, msg_ref):
    rows, width = values_ref.shape
    cells = rows // CELL
    count = valid_rows(valid_ref, cells)

    def add(cell, total):
        return total + valid_ref[cell] * fold8(values_ref[cell_rows(cell), :])

    total = lax.fori_loop(0, cells, add, jnp.zeros((8, width), F32))
    total = jnp.sum(total, axis=0, keepdims=True)
    mean = total / jnp.maximum(jnp.full((1, width), count, F32), 1.0)

    def add_squares(cell, squares):
        centered = values_ref[cell_rows(cell), :] - mean
        return squares + valid_ref[cell] * fold8(centered * centered)

    squares = lax.fori_loop(0, cells, add_squares, jnp.zeros((8, width), F32))
    squares = jnp.sum(squares, axis=0, keepdims=True)
    message = jnp.concatenate([total, squares, jnp.full((1, LANES), count, F32)], axis=1)
    msg_ref[...] = jnp.broadcast_to(message[None], msg_ref.shape)


def receive_stats(msg_ref):
    devices, _, length = msg_ref.shape
    width = (length - LANES) // 2

    def add(i, carry):
        total, count = carry
        return (total + msg_ref[i, :, :width], count + msg_ref[i, :, 2 * width :])

    total, count = lax.fori_loop(
        0, devices, add, (jnp.zeros((1, width), F32), jnp.zeros((1, LANES), F32)), unroll=4
    )
    count = widen(count, width)
    mean = total / count

    def add_squares(i, squares):
        own = widen(msg_ref[i, :, 2 * width :], width)
        offset = msg_ref[i, :, :width] / jnp.maximum(own, 1.0) - mean
        return squares + msg_ref[i, :, width : 2 * width] + own * offset * offset

    squares = lax.fori_loop(0, devices, add_squares, jnp.zeros((1, width), F32), unroll=4)
    return mean, lax.rsqrt(squares / count + EPSILON), count


def keep_stats(stats_ref, mean, rstd, count):
    stats_ref[0:1, :] = mean
    stats_ref[1:2, :] = rstd
    stats_ref[2:3, :] = count


def receive_sums(msg_ref):
    devices, _, length = msg_ref.shape
    total = lax.fori_loop(
        0, devices, lambda i, t: t + msg_ref[i], jnp.zeros((1, length), F32), unroll=4
    )
    return total[:, : length // 2], total[:, length // 2 :]


def send_sums(bias, gain, msg_ref):
    message = jnp.concatenate(
        [jnp.sum(bias, axis=0, keepdims=True), jnp.sum(gain, axis=0, keepdims=True)], axis=1
    )
    msg_ref[...] = jnp.broadcast_to(message[None], msg_ref.shape)


def later_frame(block):
    return jnp.concatenate([block[8:], jnp.zeros((8, block.shape[1]), block.dtype)], axis=0)


def earlier_frame(block):
    return jnp.concatenate([jnp.zeros((8, block.shape[1]), block.dtype), block[:-8]], axis=0)


def unpack_weights_kernel(slot_ref, all_ref, ws_ref, wt_ref, stage, turn, *, base):
    low = lax.broadcasted_iota(jnp.int32, (8, LANES), 1) < 64
    zero = jnp.zeros((8, LANES), F32)
    spatial_groups = ws_ref.shape[0] // 32

    def load_piece(number):
        start = pl.multiple_of(slot_ref[number] * PIECE_ROWS, PIECE_ROWS)
        return all_ref[pl.ds(start, PIECE_ROWS), :].astype(F32)

    def spatial_group(g, _):
        for q in range(9):
            stage[16 * q : 16 * q + 16, :] = load_piece(base + 9 * g + q)
        for i in range(2):
            a = [stage[pl.ds(72 * i + j, 8, stride=9), :] for j in range(9)]
            r = [pltpu.roll(a[4 + j], 64, axis=1) for j in range(5)]
            even = a[:4] + [jnp.where(low, a[4], zero)]
            odd = [jnp.where(low, r[j], r[j + 1]) for j in range(4)] + [jnp.where(low, r[4], zero)]
            for j in range(5):
                turn[j, pl.ds(16 * i, 8, stride=2), :] = even[j]
                turn[j, pl.ds(16 * i + 1, 8, stride=2), :] = odd[j]
        rows = block_rows(g, 32)
        for j in range(5):
            ws_ref[rows, LANES * j : LANES * (j + 1)] = turn[j].astype(BF16)
        return 0

    lax.fori_loop(0, spatial_groups, spatial_group, 0)
    temporal_base = base + 9 * spatial_groups
    padded = wt_ref.shape[0] // 3
    pairs = (9 * spatial_groups) // 3 // 6
    for tap in range(3):

        def temporal_pair(k, _):
            first = temporal_base + tap * 2 * pairs + 2 * k
            stage[0:16, :] = load_piece(first)
            stage[16:32, :] = load_piece(first + 1)
            rows = pl.ds(pl.multiple_of(tap * padded + k * 16, 16), 16)
            for h in range(2):
                wt_ref[rows, LANES * h : LANES * (h + 1)] = stage[pl.ds(h, 16, stride=2), :].astype(
                    BF16
                )
            return 0

        lax.fori_loop(0, pairs, temporal_pair, 0)
        wt_ref[tap * padded + 16 * pairs : (tap + 1) * padded, :] = jnp.zeros(
            (padded - 16 * pairs, wt_ref.shape[1]), BF16
        )


def pack_grads_kernel(slot_ref, ws_ref, wt_ref, ws2_ref, wt2_ref, out_ref, stage, turn):
    low = lax.broadcasted_iota(jnp.int32, (8, LANES), 1) < 64
    spatial_groups = ws_ref.shape[0] // 32
    padded = wt_ref.shape[0] // 3
    pairs = (9 * spatial_groups) // 3 // 6

    def clear(i, _):
        out_ref[block_rows(i, 32), :] = jnp.zeros((32, LANES), BF16)
        return 0

    lax.fori_loop(0, out_ref.shape[0] // 32, clear, 0)

    def store_piece(number, rows16):
        start = pl.multiple_of(slot_ref[number] * PIECE_ROWS, PIECE_ROWS)
        out_ref[pl.ds(start, PIECE_ROWS), :] = rows16.astype(BF16)

    base = 0
    for spatial, temporal in ((ws_ref, wt_ref), (ws2_ref, wt2_ref)):

        def spatial_group(g, _):
            rows = block_rows(g, 32)
            for j in range(5):
                turn[j] = spatial[rows, LANES * j : LANES * (j + 1)]
            for i in range(2):
                even = [turn[j, pl.ds(16 * i, 8, stride=2), :] for j in range(5)]
                odd = [turn[j, pl.ds(16 * i + 1, 8, stride=2), :] for j in range(5)]
                r = [pltpu.roll(odd[j], 64, axis=1) for j in range(5)]
                flat = even[:4] + [jnp.where(low, even[4], r[0])]
                flat += [jnp.where(low, r[j], r[j + 1]) for j in range(4)]
                for j in range(9):
                    stage[pl.ds(72 * i + j, 8, stride=9), :] = flat[j]
            for q in range(9):
                store_piece(base + 9 * g + q, stage[16 * q : 16 * q + 16, :])
            return 0

        lax.fori_loop(0, spatial_groups, spatial_group, 0)
        base += 9 * spatial_groups
        for tap in range(3):

            def temporal_pair(k, _):
                first = base + tap * 2 * pairs + 2 * k
                rows = pl.ds(pl.multiple_of(tap * padded + k * 16, 16), 16)
                for h in range(2):
                    stage[pl.ds(h, 16, stride=2), :] = temporal[rows, LANES * h : LANES * (h + 1)]
                store_piece(first, stage[0:16, :])
                store_piece(first + 1, stage[16:32, :])
                return 0

            lax.fori_loop(0, pairs, temporal_pair, 0)
        base += 6 * pairs


def fill_padded(place_ref, padded_ref, tile_ref, halo_refs):
    up, down, side, corner_up, corner_down = halo_refs
    rows, cols = tile_ref.shape[:2]
    padded_ref[1 : rows + 1, 1 : cols + 1] = tile_ref[...]
    padded_ref[0, 1 : cols + 1] = up[...]
    padded_ref[rows + 1, 1 : cols + 1] = down[...]
    for core in range(2):
        near, far = (cols + 1, 0) if core == 0 else (0, cols + 1)

        @pl.when(place_ref[0] == core)
        def _():
            padded_ref[1 : rows + 1, near] = side[...]
            padded_ref[0, near] = corner_up[...]
            padded_ref[rows + 1, near] = corner_down[...]
            padded_ref[:, far] = jnp.zeros((rows + 2,) + tile_ref.shape[2:], BF16)


def write_edges(place_ref, tile_ref, edge_refs):
    top, bottom, side, corner_top, corner_bottom = edge_refs
    rows, cols = tile_ref.shape[:2]
    top[...] = tile_ref[0]
    bottom[...] = tile_ref[rows - 1]
    edge = jnp.where(place_ref[0] == 0, cols - 1, 0)
    side[...] = tile_ref[:, edge]
    corner_top[...] = tile_ref[0, edge]
    corner_bottom[...] = tile_ref[rows - 1, edge]


def spatial_kernel(
    place_ref, valid_ref, tile_ref, up, down, side, cup, cdown, ws_ref, padded_ref, s_ref, msg_ref
):
    rows, cols, cell, width = tile_ref.shape
    fill_padded(place_ref, padded_ref, tile_ref, (up, down, side, cup, cdown))

    def one_row(r, _):
        windows = []
        for row_tap in range(3):
            for col_tap in range(3):
                window = padded_ref[r + row_tap, col_tap : col_tap + cols]
                windows.append(window.reshape(cols * cell, width))
        s_ref[block_rows(r, cols * cell), :] = jnp.dot(
            jnp.concatenate(windows, axis=1), ws_ref[...], preferred_element_type=F32
        )
        return 0

    lax.fori_loop(0, rows, one_row, 0)
    send_stats(s_ref, valid_ref, msg_ref)


def spatial_back(padded_ref, ws_ref, r, cols, cell, width):
    total = None
    for row_tap in range(3):
        for col_tap in range(3):
            window = padded_ref[r + 2 - row_tap, 2 - col_tap : 2 - col_tap + cols]
            tap = 3 * row_tap + col_tap
            term = lax.dot_general(
                window.reshape(cols * cell, window.shape[-1]),
                ws_ref[tap * width : (tap + 1) * width, :],
                (((1,), (1,)), ((), ())),
                preferred_element_type=F32,
            )
            total = term if total is None else total + term
    return total


def spatial_weight_kernel(padded_ref, ds_ref, grad_ref):
    rows, cols, cell, middle = ds_ref.shape
    width = padded_ref.shape[-1]
    grads = ds_ref[...].reshape(rows * cols * cell, middle)
    for row_tap in range(3):
        for col_tap in range(3):
            window = padded_ref[row_tap : row_tap + rows, col_tap : col_tap + cols]
            tap = 3 * row_tap + col_tap
            grad_ref[tap * width : (tap + 1) * width, :] = lax.dot_general(
                window.reshape(rows * cols * cell, width),
                grads,
                (((0,), (0,)), ((), ())),
                preferred_element_type=F32,
            )


def spatial_grad_kernel(
    place_ref, valid_ref, ds_ref, up, down, side, cup, cdown, ws_ref, t_ref, stats_ref, gb_ref,
    e_ref, msg_ref, padded_ref, *, index,
):
    rows, cols, cell, middle = ds_ref.shape
    width = e_ref.shape[1]
    fill_padded(place_ref, padded_ref, ds_ref, (up, down, side, cup, cdown))
    mean, rstd = stats_ref[0:1, :], stats_ref[1:2, :]
    gain, bias = gb_ref[2 * index : 2 * index + 1, :width], gb_ref[2 * index + 1 : 2 * index + 2, :width]

    def one_row(r, carry):
        grad = spatial_back(padded_ref, ws_ref, r, cols, cell, width)
        e_ref[block_rows(r, cols * cell), :] = grad
        return carry

    lax.fori_loop(0, rows, one_row, 0)

    def one_cell(c, carry):
        bias_sum, gain_sum = carry
        normal = (t_ref[cell_rows(c), :] - mean) * rstd
        value = normal * gain + bias
        sigma = sigmoid(value)
        e = e_ref[cell_rows(c), :] * valid_ref[c] * (sigma * (1.0 + value * (1.0 - sigma)))
        e_ref[cell_rows(c), :] = e
        return (bias_sum + fold8(e), gain_sum + fold8(e * normal))

    start = jnp.zeros((8, width), F32)
    bias_sum, gain_sum = lax.fori_loop(0, rows * cols, one_cell, (start, start))
    send_sums(bias_sum, gain_sum, msg_ref)


def input_grad_kernel(
    place_ref, valid_ref, ds_ref, up, down, side, cup, cdown, ws_ref, dpre_ref, out_ref, padded_ref
):
    rows, cols, cell, middle = ds_ref.shape
    width = out_ref.shape[1]
    fill_padded(place_ref, padded_ref, ds_ref, (up, down, side, cup, cdown))

    def one_row(r, carry):
        grad = spatial_back(padded_ref, ws_ref, r, cols, cell, width)
        for c in range(cols):
            rows_of = cell_rows(r * cols + c)
            out_ref[rows_of, :] = (grad[c * cell : (c + 1) * cell] + dpre_ref[rows_of, :]) * valid_ref[
                r * cols + c
            ]
        return carry

    lax.fori_loop(0, rows, one_row, 0)


def temporal_kernel(
    valid_ref, s_ref, msg_ref, gb_ref, wt_ref, columns_ref, t_ref, stats_ref, out_ref, *, index
):
    rows, middle = s_ref.shape
    mean, rstd, count = receive_stats(msg_ref)
    keep_stats(stats_ref, mean, rstd, count)
    gain, bias = gb_ref[2 * index : 2 * index + 1, :], gb_ref[2 * index + 1 : 2 * index + 2, :]

    def one_cell(c, _):
        value = (s_ref[cell_rows(c), :] - mean) * rstd * gain + bias
        inner = value * sigmoid(value) * valid_ref[c]
        columns_ref[cell_rows(c), 0:middle] = earlier_frame(inner).astype(BF16)
        columns_ref[cell_rows(c), middle : 2 * middle] = inner.astype(BF16)
        columns_ref[cell_rows(c), 2 * middle : 3 * middle] = later_frame(inner).astype(BF16)
        return 0

    lax.fori_loop(0, rows // CELL, one_cell, 0)

    def one_block(i, _):
        t_ref[block_rows(i, 320), :] = jnp.dot(
            columns_ref[block_rows(i, 320), :], wt_ref[...], preferred_element_type=F32
        )
        return 0

    lax.fori_loop(0, rows // 320, one_block, 0)
    send_stats(t_ref, valid_ref, out_ref)


def middle_kernel(
    place_ref, valid_ref, t_ref, msg_ref, gb_ref, stats_ref, tile_ref, top, bottom, side, ctop, cbottom,
    *, index,
):
    width = t_ref.shape[1]
    rows, cols = tile_ref.shape[:2]
    mean, rstd, count = receive_stats(msg_ref)
    keep_stats(stats_ref, mean, rstd, count)
    gain, bias = gb_ref[2 * index : 2 * index + 1, :width], gb_ref[2 * index + 1 : 2 * index + 2, :width]
    for r in range(rows):
        for c in range(cols):
            number = r * cols + c
            value = (t_ref[number * CELL : (number + 1) * CELL, :] - mean) * rstd * gain + bias
            tile_ref[r, c] = (value * sigmoid(value) * valid_ref[number]).astype(BF16)
    write_edges(place_ref, tile_ref, (top, bottom, side, ctop, cbottom))


def top_kernel(
    valid_ref, t_ref, msg_ref, gb_ref, x_ref, cot_ref, stats_ref, out_ref, dpre_ref, msg_out, *, index
):
    rows, width = t_ref.shape
    mean, rstd, count = receive_stats(msg_ref)
    keep_stats(stats_ref, mean, rstd, count)
    gain, bias = gb_ref[2 * index : 2 * index + 1, :width], gb_ref[2 * index + 1 : 2 * index + 2, :width]

    def one_cell(c, carry):
        bias_sum, gain_sum = carry
        normal = (t_ref[cell_rows(c), :] - mean) * rstd
        pre = normal * gain + bias + x_ref[cell_rows(c), :].astype(F32)
        sigma = sigmoid(pre)
        valid = valid_ref[c]
        out_ref[cell_rows(c), :] = pre * sigma * valid
        dpre = cot_ref[cell_rows(c), :].astype(F32) * valid * (sigma * (1.0 + pre * (1.0 - sigma)))
        dpre_ref[cell_rows(c), :] = dpre
        return (bias_sum + fold8(dpre), gain_sum + fold8(dpre * normal))

    start = jnp.zeros((8, width), F32)
    bias_sum, gain_sum = lax.fori_loop(0, rows // CELL, one_cell, (start, start))
    send_sums(bias_sum, gain_sum, msg_out)


def temporal_grad_kernel(
    valid_ref, e_ref, t_ref, tstats_ref, msg_ref, s_ref, sstats_ref, gb_ref, wt_ref,
    dt_ref, en_ref, sums_ref, msg_out, columns_ref, *, index,
):
    rows, width = e_ref.shape
    middle = s_ref.shape[1]
    bias_grad, gain_grad = receive_sums(msg_ref)
    sums_ref[0:1, :] = gain_grad
    sums_ref[1:2, :] = bias_grad
    mean, rstd, count = tstats_ref[0:1, :], tstats_ref[1:2, :], tstats_ref[2:3, :]
    gain = gb_ref[2 * index + 2 : 2 * index + 3, :width]

    def one_cell(c, _):
        normal = (t_ref[cell_rows(c), :] - mean) * rstd
        dt = (rstd * gain) * (
            e_ref[cell_rows(c), :] - valid_ref[c] * ((bias_grad + normal * gain_grad) / count)
        )
        dt_ref[cell_rows(c), :] = dt.astype(BF16)
        columns_ref[cell_rows(c), 0:width] = later_frame(dt).astype(BF16)
        columns_ref[cell_rows(c), width : 2 * width] = dt.astype(BF16)
        columns_ref[cell_rows(c), 2 * width : 3 * width] = earlier_frame(dt).astype(BF16)
        return 0

    lax.fori_loop(0, rows // CELL, one_cell, 0)

    def one_block(i, _):
        total = None
        for tap in range(3):
            term = lax.dot_general(
                columns_ref[block_rows(i, 320), tap * width : (tap + 1) * width],
                wt_ref[tap * middle : (tap + 1) * middle, :],
                (((1,), (1,)), ((), ())),
                preferred_element_type=F32,
            )
            total = term if total is None else total + term
        en_ref[block_rows(i, 320), :] = total
        return 0

    lax.fori_loop(0, rows // 320, one_block, 0)
    mean_s, rstd_s = sstats_ref[0:1, :], sstats_ref[1:2, :]
    gain_s, bias_s = gb_ref[2 * index : 2 * index + 1, :], gb_ref[2 * index + 1 : 2 * index + 2, :]

    def one_mid_cell(c, carry):
        bias_sum, gain_sum = carry
        normal = (s_ref[cell_rows(c), :] - mean_s) * rstd_s
        value = normal * gain_s + bias_s
        sigma = sigmoid(value)
        e = en_ref[cell_rows(c), :] * valid_ref[c] * (sigma * (1.0 + value * (1.0 - sigma)))
        en_ref[cell_rows(c), :] = e
        return (bias_sum + fold8(e), gain_sum + fold8(e * normal))

    start = jnp.zeros((8, middle), F32)
    bias_sum, gain_sum = lax.fori_loop(0, rows // CELL, one_mid_cell, (start, start))
    send_sums(bias_sum, gain_sum, msg_out)


def temporal_weight_kernel(columns_ref, dt_ref, grad_ref):
    middle = columns_ref.shape[1] // 3
    for tap in range(3):
        grad_ref[tap * middle : (tap + 1) * middle, :] = lax.dot_general(
            columns_ref[:, tap * middle : (tap + 1) * middle],
            dt_ref[...],
            (((0,), (0,)), ((), ())),
            preferred_element_type=F32,
        )


def ds_kernel(
    place_ref, valid_ref, en_ref, s_ref, stats_ref, msg_ref, gb_ref,
    sums_ref, tile_ref, top, bottom, side, ctop, cbottom, *, index,
):
    rows, cols = tile_ref.shape[:2]
    bias_grad, gain_grad = receive_sums(msg_ref)
    sums_ref[0:1, :] = gain_grad
    sums_ref[1:2, :] = bias_grad
    mean, rstd, count = stats_ref[0:1, :], stats_ref[1:2, :], stats_ref[2:3, :]
    scale = rstd * gb_ref[2 * index : 2 * index + 1, :]
    for r in range(rows):
        for c in range(cols):
            number = r * cols + c
            block = slice(number * CELL, (number + 1) * CELL)
            normal = (s_ref[block, :] - mean) * rstd
            tile_ref[r, c] = (
                scale
                * (en_ref[block, :] - valid_ref[number] * ((bias_grad + normal * gain_grad) / count))
            ).astype(BF16)
    write_edges(place_ref, tile_ref, (top, bottom, side, ctop, cbottom))


def run(kernel, ins, outs, scratch=(), scalars=0, **settings):
    return pl.pallas_call(
        functools.partial(kernel, **settings),
        out_shape=[jax.ShapeDtypeStruct(shape, dtype) for shape, dtype in outs],
        in_specs=[SMEM] * scalars + [VMEM] * (len(ins) - scalars),
        out_specs=[VMEM] * len(outs),
        scratch_shapes=list(scratch),
        compiler_params=pltpu.CompilerParams(vmem_limit_bytes=56 * 2**20),
    )(*ins)


def slot_of_pieces(owner_list, slot_count, device_total):
    owner_ids = owner_list[:, 0]
    onehot = (owner_ids[:, None] == jnp.arange(device_total, dtype=jnp.int32)[None, :]).astype(
        jnp.int32
    )
    earlier = jnp.cumsum(onehot, axis=0) - onehot
    ranking = jnp.sum(earlier * onehot, axis=1)
    return owner_ids * slot_count + ranking


def exchange(message):
    return lax.all_to_all(message, AXES, 0, 0, tiled=True)


def swap_edges(edges):
    top, bottom, side, corner_top, corner_bottom = edges
    count = lax.axis_size("ha")
    cores = lax.axis_size("wa")
    forward = [(i, i + 1) for i in range(count - 1)]
    backward = [(i + 1, i) for i in range(count - 1)]
    across = [(0, 1), (1, 0)]

    def both(moves):
        return [(a * cores + i, b * cores + j) for a, b in moves for i, j in across]

    up = lax.ppermute(bottom, "ha", forward)
    down = lax.ppermute(top, "ha", backward)
    corner_up = lax.ppermute(corner_bottom, ("ha", "wa"), both(forward))
    corner_down = lax.ppermute(corner_top, ("ha", "wa"), both(backward))
    beside = lax.ppermute(side, "wa", across)
    return [up, down, beside, corner_up, corner_down]


def per_device(
    block_input,
    cotangent,
    frame_sides,
    owner_list,
    master_slots,
    first_slots,
    second_slots,
    norm_gains,
    norm_biases,
    norm_first,
    norm_second,
):
    clip_count, frames, tile_rows, tile_cols, width = block_input.shape
    devices = lax.axis_size(AXES)
    slot_count, piece_len = master_slots.shape
    middle = norm_gains.shape[0] // 2 - width
    middle_pad = -(-middle // LANES) * LANES
    rows = clip_count * frames * tile_rows * tile_cols

    low_slots = master_slots.astype(BF16).reshape(slot_count * PIECE_ROWS, LANES)
    all_weights = lax.all_gather(low_slots, AXES, axis=0, tiled=True)

    own_side = frame_sides[0]
    row_ids = lax.axis_index("ha") * tile_rows + jnp.arange(tile_rows, dtype=jnp.int32)
    col_ids = lax.axis_index("wa") * tile_cols + jnp.arange(tile_cols, dtype=jnp.int32)
    grid_rows = tile_rows * lax.axis_size("ha")
    grid_cols = tile_cols * lax.axis_size("wa")
    valid = (
        (row_ids[:, None] >= grid_rows - own_side) & (col_ids[None, :] >= grid_cols - own_side)
    ).astype(F32)
    valid_flat = valid.reshape(-1)
    place = lax.axis_index("wa").reshape(1)
    slot_index = slot_of_pieces(owner_list, slot_count, devices)
    batches, heights, cores = (lax.axis_size(axis) for axis in AXES)
    owner, ranking = slot_index // slot_count, slot_index % slot_count
    turned = (owner % cores * heights + owner // cores % heights) * batches + owner // (cores * heights)
    grad_slots = turned * slot_count + ranking

    bounds = [0, middle, middle + width, 2 * middle + width, 2 * middle + 2 * width]
    gb = []
    for i in range(4):
        for vector in (norm_gains, norm_biases):
            part = vector[bounds[i] : bounds[i + 1]]
            gb.append(jnp.pad(part, (0, middle_pad - part.shape[0])))
    gb = jnp.stack(gb)

    def to_tile(array):
        return jnp.transpose(array, (2, 3, 1, 0, 4)).reshape(tile_rows, tile_cols, CELL, width)

    x_tile = to_tile(block_input) * valid[:, :, None, None].astype(BF16)
    cot_tile = to_tile(cotangent)
    edge = jnp.where(place[0] == 0, tile_cols - 1, 0)
    x_side = lax.dynamic_index_in_dim(x_tile, edge, axis=1, keepdims=False)
    x_halo = swap_edges([x_tile[0], x_tile[-1], x_side, x_side[0], x_side[-1]])

    tap_rows = 9 * width
    stage = [pltpu.VMEM((144, LANES), F32), pltpu.VMEM((5, 32, LANES), F32)]
    half = tap_rows * middle // piece_len + 3 * middle * width // piece_len
    weight_shapes = [((tap_rows, middle_pad), BF16), ((3 * middle_pad, width), BF16)]
    weights = []
    for unit in range(2):
        weights.append(
            run(unpack_weights_kernel, [slot_index, all_weights], weight_shapes, stage, 1, base=unit * half)
        )

    tile_shape = (tile_rows, tile_cols, CELL, width)
    mid_tile = (tile_rows, tile_cols, CELL, middle_pad)
    padded_tile = (tile_rows + 2, tile_cols + 2, CELL, width)
    padded_mid = (tile_rows + 2, tile_cols + 2, CELL, middle_pad)
    stats_mid = (devices, 1, 2 * middle_pad + LANES)
    stats_wide = (devices, 1, 2 * width + LANES)

    def edge_shapes(lanes):
        row, col = (tile_cols, CELL, lanes), (tile_rows, CELL, lanes)
        return [(row, BF16), (row, BF16), (col, BF16), ((CELL, lanes), BF16), ((CELL, lanes), BF16)]

    def unit_forward(tile, halo, ws, wt, index):
        padded, s, msg = run(
            spatial_kernel,
            [place, valid_flat, tile, *halo, ws],
            [(padded_tile, BF16), ((rows, middle_pad), F32), (stats_mid, F32)],
            scalars=2,
        )
        columns, t, s_stats, msg = run(
            temporal_kernel,
            [valid_flat, s, exchange(msg), gb, wt],
            [
                ((rows, 3 * middle_pad), BF16),
                ((rows, width), F32),
                ((8, middle_pad), F32),
                (stats_wide, F32),
            ],
            scalars=1,
            index=index,
        )
        return padded, s, s_stats, columns, t, exchange(msg)

    (ws1, wt1), (ws2, wt2) = weights
    padded1, s1, s_stats1, columns1, t1, msg = unit_forward(x_tile, x_halo, ws1, wt1, 0)
    t_stats1, y_tile, *edges = run(
        middle_kernel,
        [place, valid_flat, t1, msg, gb],
        [((8, width), F32), (tile_shape, BF16)] + edge_shapes(width),
        scalars=2,
        index=1,
    )
    padded2, s2, s_stats2, columns2, t2, msg = unit_forward(y_tile, swap_edges(edges), ws2, wt2, 2)
    t_stats2, block_output, dpre, msg = run(
        top_kernel,
        [valid_flat, t2, msg, gb, x_tile.reshape(rows, width), cot_tile.reshape(rows, width)],
        [((8, width), F32), ((rows, width), F32), ((rows, width), F32), ((devices, 1, 2 * width), F32)],
        scalars=1,
        index=3,
    )

    def unit_backward(e, msg, t, t_stats, s, s_stats, columns, padded, wt, index):
        dt, en, t_sums, msg = run(
            temporal_grad_kernel,
            [valid_flat, e, t, t_stats, exchange(msg), s, s_stats, gb, wt],
            [
                ((rows, width), BF16),
                ((rows, middle_pad), F32),
                ((2, width), F32),
                ((devices, 1, 2 * middle_pad), F32),
            ],
            [pltpu.VMEM((rows, 3 * width), BF16)],
            scalars=1,
            index=index,
        )
        s_sums, ds, *edges = run(
            ds_kernel,
            [place, valid_flat, en, s, s_stats, exchange(msg), gb],
            [((2, middle_pad), F32), (mid_tile, BF16)] + edge_shapes(middle_pad),
            scalars=2,
            index=index,
        )
        halo = swap_edges(edges)
        (wt_grad,) = run(temporal_weight_kernel, [columns, dt], [((3 * middle_pad, width), F32)])
        (ws_grad,) = run(spatial_weight_kernel, [padded, ds], [((tap_rows, middle_pad), F32)])
        return ds, halo, ws_grad, wt_grad, s_sums, t_sums

    ds, halo, ws_grad2, wt_grad2, s_sums2, t_sums2 = unit_backward(
        dpre, msg, t2, t_stats2, s2, s_stats2, columns2, padded2, wt2, 2
    )
    e1, msg = run(
        spatial_grad_kernel,
        [place, valid_flat, ds, *halo, ws2, t1, t_stats1, gb],
        [((rows, width), F32), ((devices, 1, 2 * width), F32)],
        [pltpu.VMEM(padded_mid, BF16)],
        scalars=2,
        index=1,
    )
    ds, halo, ws_grad1, wt_grad1, s_sums1, t_sums1 = unit_backward(
        e1, msg, t1, t_stats1, s1, s_stats1, columns1, padded1, wt1, 0
    )
    (packed,) = run(
        pack_grads_kernel,
        [grad_slots, ws_grad1, wt_grad1, ws_grad2, wt_grad2],
        [((devices * slot_count * PIECE_ROWS, LANES), BF16)],
        stage,
        scalars=1,
    )
    grad_mine = packed
    for axis in ("wa", "ha", "batch"):
        grad_mine = lax.psum_scatter(grad_mine, axis, scatter_dimension=0, tiled=True)
    (input_grad,) = run(
        input_grad_kernel,
        [place, valid_flat, ds, *halo, ws1, dpre],
        [((rows, width), F32)],
        [pltpu.VMEM(padded_mid, BF16)],
        scalars=2,
    )

    def from_tile(array):
        array = array.reshape(tile_rows, tile_cols, frames, clip_count, width)
        return jnp.transpose(array, (3, 2, 0, 1, 4))

    grad_mine = grad_mine.astype(F32).reshape(slot_count, piece_len)
    correction = 1.0 - 0.5**STEP
    step_rate = 1.8 / math.sqrt(9.0 * width)
    first_new = 0.5 * first_slots + 0.5 * grad_mine
    second_new = 0.5 * second_slots + 0.5 * grad_mine * grad_mine
    master_new = master_slots - step_rate * (
        first_new / correction / (jnp.sqrt(second_new / correction) + ADAM_EPSILON)
        + DECAY_RATE * master_slots
    )
    weight_copy = master_new.astype(BF16)
    norm_grad = jnp.concatenate([s_sums1[:, :middle], t_sums1, s_sums2[:, :middle], t_sums2], axis=1)
    norm_pair = jnp.stack([norm_gains, norm_biases])
    norm_first_new = 0.5 * norm_first + 0.5 * norm_grad
    norm_second_new = 0.5 * norm_second + 0.5 * norm_grad * norm_grad
    norm_new = norm_pair - NORM_RATE * (norm_first_new / correction) / (
        jnp.sqrt(norm_second_new / correction) + ADAM_EPSILON
    )
    return (
        from_tile(block_output),
        from_tile(input_grad),
        master_new,
        first_new,
        second_new,
        weight_copy,
        norm_first_new,
        norm_second_new,
        norm_new,
    )


def solution(mesh):
    wide = P("batch", None, "ha", "wa", None)
    owned = P(AXES, None)
    return jax.shard_map(
        per_device,
        mesh=mesh,
        in_specs=(wide, wide, P("batch"), P(), owned, owned, owned, P(), P(), P(), P()),
        out_specs=(wide, wide, owned, owned, owned, owned, P(), P(), P()),
        check_vma=False,
    )
```

```python
import functools
import math

import jax
import jax.numpy as jnp
from jax import lax
from jax.experimental import pallas as pl
from jax.experimental.pallas import tpu as pltpu
from jax.sharding import PartitionSpec as P

STEP = 5
EPSILON = 1e-05
ADAM_EPSILON = 1e-08
DECAY_RATE = 0.1
NORM_RATE = 0.3

AXES = ("batch", "ha", "wa")
F32 = jnp.float32
BF16 = jnp.bfloat16
VMEM = pl.BlockSpec(memory_space=pltpu.VMEM)
SMEM = pl.BlockSpec(memory_space=pltpu.SMEM)
CELL = 64
LANES = 128
PIECE_ROWS = 16


def sigmoid(v):
    return 1.0 / (1.0 + jnp.exp(-v))


def cell_rows(index, count=1):
    return pl.ds(pl.multiple_of(index * CELL, CELL), count * CELL)


def block_rows(index, size):
    return pl.ds(pl.multiple_of(index * size, size), size)


def fold8(block):
    return jnp.sum(block.reshape(-1, 8, block.shape[-1]), axis=0)


def widen(lane_block, width):
    return jnp.concatenate([lane_block] * (width // LANES), axis=1)


def valid_rows(valid_ref, cells):
    total = valid_ref[0]
    for cell in range(1, cells):
        total = total + valid_ref[cell]
    return total * CELL


def send_stats(values_ref, valid_ref, msg_ref):
    rows, width = values_ref.shape
    cells = rows // CELL
    count = valid_rows(valid_ref, cells)

    def add(cell, total):
        return total + valid_ref[cell] * fold8(values_ref[cell_rows(cell), :])

    total = lax.fori_loop(0, cells, add, jnp.zeros((8, width), F32))
    total = jnp.sum(total, axis=0, keepdims=True)
    mean = total / jnp.maximum(jnp.full((1, width), count, F32), 1.0)

    def add_squares(cell, squares):
        centered = values_ref[cell_rows(cell), :] - mean
        return squares + valid_ref[cell] * fold8(centered * centered)

    squares = lax.fori_loop(0, cells, add_squares, jnp.zeros((8, width), F32))
    squares = jnp.sum(squares, axis=0, keepdims=True)
    message = jnp.concatenate([total, squares, jnp.full((1, LANES), count, F32)], axis=1)
    msg_ref[...] = jnp.broadcast_to(message[None], msg_ref.shape)


def receive_stats(msg_ref):
    devices, _, length = msg_ref.shape
    width = (length - LANES) // 2

    def add(i, carry):
        total, count = carry
        return (total + msg_ref[i, :, :width], count + msg_ref[i, :, 2 * width :])

    total, count = lax.fori_loop(
        0, devices, add, (jnp.zeros((1, width), F32), jnp.zeros((1, LANES), F32)), unroll=4
    )
    count = widen(count, width)
    mean = total / count

    def add_squares(i, squares):
        own = widen(msg_ref[i, :, 2 * width :], width)
        offset = msg_ref[i, :, :width] / jnp.maximum(own, 1.0) - mean
        return squares + msg_ref[i, :, width : 2 * width] + own * offset * offset

    squares = lax.fori_loop(0, devices, add_squares, jnp.zeros((1, width), F32), unroll=4)
    return mean, lax.rsqrt(squares / count + EPSILON), count


def keep_stats(stats_ref, mean, rstd, count):
    stats_ref[0:1, :] = mean
    stats_ref[1:2, :] = rstd
    stats_ref[2:3, :] = count


def receive_sums(msg_ref):
    devices, _, length = msg_ref.shape
    total = lax.fori_loop(
        0, devices, lambda i, t: t + msg_ref[i], jnp.zeros((1, length), F32), unroll=4
    )
    return total[:, : length // 2], total[:, length // 2 :]


def send_sums(bias, gain, msg_ref):
    message = jnp.concatenate(
        [jnp.sum(bias, axis=0, keepdims=True), jnp.sum(gain, axis=0, keepdims=True)], axis=1
    )
    msg_ref[...] = jnp.broadcast_to(message[None], msg_ref.shape)


def later_frame(block):
    return jnp.concatenate([block[8:], jnp.zeros((8, block.shape[1]), block.dtype)], axis=0)


def earlier_frame(block):
    return jnp.concatenate([jnp.zeros((8, block.shape[1]), block.dtype), block[:-8]], axis=0)


UNROLL = 4


def gather_weights_kernel(*refs):
    parts, all_ref, sems = refs[:-2], refs[-2], refs[-1]
    rows = parts[0].shape[0]
    copies = [
        pltpu.make_async_copy(part, all_ref.at[i * rows : (i + 1) * rows, :], sems.at[i])
        for i, part in enumerate(parts)
    ]
    for copy in copies:
        copy.start()
    for copy in copies:
        copy.wait()


def unpack_weights_kernel(slot_ref, all_ref, ws_ref, wt_ref, stage, turn, *, base):
    low = lax.broadcasted_iota(jnp.int32, (8, LANES), 1) < 64
    zero = jnp.zeros((8, LANES), F32)
    spatial_groups = ws_ref.shape[0] // 32

    def load_piece(number):
        start = pl.multiple_of(slot_ref[number] * PIECE_ROWS, PIECE_ROWS)
        return all_ref[pl.ds(start, PIECE_ROWS), :].astype(F32)

    def spatial_groups_at(k, _):
        first = k * UNROLL
        for u in range(UNROLL):
            for q in range(9):
                stage[u, 16 * q : 16 * q + 16, :] = load_piece(base + 9 * (first + u) + q)
        for u in range(UNROLL):
            for i in range(2):
                a = [stage[u, pl.ds(72 * i + j, 8, stride=9), :] for j in range(9)]
                r = [pltpu.roll(a[4 + j], 64, axis=1) for j in range(5)]
                even = a[:4] + [jnp.where(low, a[4], zero)]
                odd = [jnp.where(low, r[j], r[j + 1]) for j in range(4)]
                odd += [jnp.where(low, r[4], zero)]
                for j in range(5):
                    turn[u, j, pl.ds(16 * i, 8, stride=2), :] = even[j]
                    turn[u, j, pl.ds(16 * i + 1, 8, stride=2), :] = odd[j]
        for u in range(UNROLL):
            rows = block_rows(first + u, 32)
            for j in range(5):
                ws_ref[rows, LANES * j : LANES * (j + 1)] = turn[u, j].astype(BF16)
        return 0

    lax.fori_loop(0, spatial_groups // UNROLL, spatial_groups_at, 0)
    temporal_base = base + 9 * spatial_groups
    padded = wt_ref.shape[0] // 3
    pairs = (9 * spatial_groups) // 3 // 6
    for tap in range(3):

        def temporal_pairs(k, _):
            for u in range(UNROLL):
                first = temporal_base + tap * 2 * pairs + 2 * (k * UNROLL + u)
                stage[u, 0:16, :] = load_piece(first)
                stage[u, 16:32, :] = load_piece(first + 1)
            for u in range(UNROLL):
                start = tap * padded + (k * UNROLL + u) * 16
                rows = pl.ds(pl.multiple_of(start, 16), 16)
                for h in range(2):
                    half = stage[u, pl.ds(h, 16, stride=2), :]
                    wt_ref[rows, LANES * h : LANES * (h + 1)] = half.astype(BF16)
            return 0

        lax.fori_loop(0, pairs // UNROLL, temporal_pairs, 0)
        wt_ref[tap * padded + 16 * pairs : (tap + 1) * padded, :] = jnp.zeros(
            (padded - 16 * pairs, wt_ref.shape[1]), BF16
        )


def pack_grads_kernel(slot_ref, spatial, temporal, out_ref, stage, turn):
    low = lax.broadcasted_iota(jnp.int32, (8, LANES), 1) < 64
    spatial_groups = spatial.shape[0] // 32
    padded = temporal.shape[0] // 3
    pairs = (9 * spatial_groups) // 3 // 6

    def clear(i, _):
        out_ref[block_rows(i, 128), :] = jnp.zeros((128, LANES), BF16)
        return 0

    lax.fori_loop(0, out_ref.shape[0] // 128, clear, 0)

    def store_piece(number, rows16):
        start = pl.multiple_of(slot_ref[number] * PIECE_ROWS, PIECE_ROWS)
        out_ref[pl.ds(start, PIECE_ROWS), :] = rows16.astype(BF16)

    def spatial_groups_at(k, _):
        first = k * UNROLL
        for u in range(UNROLL):
            rows = block_rows(first + u, 32)
            for j in range(5):
                turn[u, j] = spatial[rows, LANES * j : LANES * (j + 1)]
        for u in range(UNROLL):
            for i in range(2):
                even = [turn[u, j, pl.ds(16 * i, 8, stride=2), :] for j in range(5)]
                odd = [turn[u, j, pl.ds(16 * i + 1, 8, stride=2), :] for j in range(5)]
                r = [pltpu.roll(odd[j], 64, axis=1) for j in range(5)]
                flat = even[:4] + [jnp.where(low, even[4], r[0])]
                flat += [jnp.where(low, r[j], r[j + 1]) for j in range(4)]
                for j in range(9):
                    stage[u, pl.ds(72 * i + j, 8, stride=9), :] = flat[j]
        for u in range(UNROLL):
            for q in range(9):
                store_piece(9 * (first + u) + q, stage[u, 16 * q : 16 * q + 16, :])
        return 0

    lax.fori_loop(0, spatial_groups // UNROLL, spatial_groups_at, 0)
    base = 9 * spatial_groups
    for tap in range(3):

        def temporal_pairs(k, _):
            for u in range(UNROLL):
                start = tap * padded + (k * UNROLL + u) * 16
                rows = pl.ds(pl.multiple_of(start, 16), 16)
                for h in range(2):
                    stage[u, pl.ds(h, 16, stride=2), :] = temporal[
                        rows, LANES * h : LANES * (h + 1)
                    ]
            for u in range(UNROLL):
                first = base + tap * 2 * pairs + 2 * (k * UNROLL + u)
                store_piece(first, stage[u, 0:16, :])
                store_piece(first + 1, stage[u, 16:32, :])
            return 0

        lax.fori_loop(0, pairs // UNROLL, temporal_pairs, 0)


def fill_padded(place_ref, padded_ref, tile_ref, halo_refs):
    up, down, side, corner_up, corner_down = halo_refs
    rows, cols = tile_ref.shape[:2]
    padded_ref[1 : rows + 1, 1 : cols + 1] = tile_ref[...]
    padded_ref[0, 1 : cols + 1] = up[...]
    padded_ref[rows + 1, 1 : cols + 1] = down[...]
    for core in range(2):
        near, far = (cols + 1, 0) if core == 0 else (0, cols + 1)

        @pl.when(place_ref[0] == core)
        def _():
            padded_ref[1 : rows + 1, near] = side[...]
            padded_ref[0, near] = corner_up[...]
            padded_ref[rows + 1, near] = corner_down[...]
            padded_ref[:, far] = jnp.zeros((rows + 2,) + tile_ref.shape[2:], BF16)


def write_edges(place_ref, tile_ref, edge_refs):
    top, bottom, side, corner_top, corner_bottom = edge_refs
    rows, cols = tile_ref.shape[:2]
    top[...] = tile_ref[0]
    bottom[...] = tile_ref[rows - 1]
    edge = jnp.where(place_ref[0] == 0, cols - 1, 0)
    side[...] = tile_ref[:, edge]
    corner_top[...] = tile_ref[0, edge]
    corner_bottom[...] = tile_ref[rows - 1, edge]


def spatial_kernel(
    place_ref, valid_ref, tile_ref, up, down, side, cup, cdown, ws_ref, padded_ref, s_ref, msg_ref
):
    rows, cols, cell, width = tile_ref.shape
    fill_padded(place_ref, padded_ref, tile_ref, (up, down, side, cup, cdown))

    def one_row(r, _):
        windows = []
        for row_tap in range(3):
            for col_tap in range(3):
                window = padded_ref[r + row_tap, col_tap : col_tap + cols]
                windows.append(window.reshape(cols * cell, width))
        s_ref[block_rows(r, cols * cell), :] = jnp.dot(
            jnp.concatenate(windows, axis=1), ws_ref[...], preferred_element_type=F32
        )
        return 0

    lax.fori_loop(0, rows, one_row, 0)
    send_stats(s_ref, valid_ref, msg_ref)


def weight_back(window, ws_ref, tap, width):
    return lax.dot_general(
        window.reshape(-1, window.shape[-1]),
        ws_ref[block_rows(tap, width), :],
        (((1,), (1,)), ((), ())),
        preferred_element_type=F32,
    )


def edge_grads(place_ref, ds_ref, ws_ref, edge_refs, row_ref):
    top, bottom, side, corner_top, corner_bottom = edge_refs
    width = top.shape[-1]
    cols, cell = top.shape[:2]
    rows = side.shape[0]
    core = place_ref[0]
    for row, row_tap, out, corner in ((0, 0, top, corner_top), (rows - 1, 2, bottom, corner_bottom)):
        total = None
        for col_tap in range(3):
            window = ds_ref[row, pl.ds(3 - core - col_tap, cols + 1)]
            term = weight_back(window, ws_ref, 3 * row_tap + col_tap, width)
            total = term if total is None else total + term
        row_ref[...] = total.astype(BF16).reshape(row_ref.shape)
        out[...] = row_ref[pl.ds(core, cols)]
        corner[...] = row_ref[cols * (1 - core)]
    column = ds_ref[:, jnp.where(core == 0, cols + 1, 2)]
    above, level, below = [
        weight_back(column, ws_ref, 3 * row_tap + 2 - 2 * core, width) for row_tap in range(3)
    ]
    empty = jnp.zeros((cell, width), F32)
    total = level + jnp.concatenate([above[cell:], empty]) + jnp.concatenate([empty, below[:-cell]])
    side[...] = total.astype(BF16).reshape(side.shape)


def spatial_grad_kernel(ds_ref, ws_ref, grad_ref):
    rows, cols, cell = ds_ref.shape[0], ds_ref.shape[1] - 4, ds_ref.shape[2]
    width = grad_ref.shape[1]
    for row in range(rows):
        total = None
        for row_tap in range(3):
            if not 0 <= row + 1 - row_tap < rows:
                continue
            for col_tap in range(3):
                window = ds_ref[row + 1 - row_tap, 3 - col_tap : 3 - col_tap + cols]
                term = weight_back(window, ws_ref, 3 * row_tap + col_tap, width)
                total = term if total is None else total + term
        grad_ref[row * cols * cell : (row + 1) * cols * cell, :] = total


def add_halo(place_ref, grad_ref, out_ref, halo_refs):
    up, down, side, corner_up, corner_down = halo_refs
    rows, cols = side.shape[0], up.shape[0]
    edge = jnp.where(place_ref[0] == 0, cols - 1, 0)
    out_ref[...] = grad_ref[...]
    last = (rows - 1) * cols
    for c in range(cols):
        out_ref[cell_rows(c), :] += up[c].astype(F32)
        out_ref[cell_rows(last + c), :] += down[c].astype(F32)
    for r in range(rows):
        out_ref[cell_rows(r * cols + edge), :] += side[r].astype(F32)
    out_ref[cell_rows(edge), :] += corner_up[...].astype(F32)
    out_ref[cell_rows(last + edge), :] += corner_down[...].astype(F32)


def spatial_weight_kernel(padded_ref, ds_ref, grad_ref):
    rows, cols, cell, middle = ds_ref.shape
    cols = cols - 4
    width = padded_ref.shape[-1]
    grads = ds_ref[:, 2 : cols + 2].reshape(rows * cols * cell, middle)
    for row_tap in range(3):
        for col_tap in range(3):
            window = padded_ref[row_tap : row_tap + rows, col_tap : col_tap + cols]
            tap = 3 * row_tap + col_tap
            grad_ref[tap * width : (tap + 1) * width, :] = lax.dot_general(
                window.reshape(rows * cols * cell, width),
                grads,
                (((0,), (0,)), ((), ())),
                preferred_element_type=F32,
            )


def between_kernel(
    place_ref, valid_ref, grad_ref, up, down, side, cup, cdown, t_ref, stats_ref, gb_ref,
    e_ref, msg_ref, *, index,
):
    rows, width = e_ref.shape
    add_halo(place_ref, grad_ref, e_ref, (up, down, side, cup, cdown))
    mean, rstd = stats_ref[0:1, :], stats_ref[1:2, :]
    gain, bias = gb_ref[2 * index : 2 * index + 1, :width], gb_ref[2 * index + 1 : 2 * index + 2, :width]

    def one_cell(c, carry):
        bias_sum, gain_sum = carry
        normal = (t_ref[cell_rows(c), :] - mean) * rstd
        value = normal * gain + bias
        sigma = sigmoid(value)
        e = e_ref[cell_rows(c), :] * valid_ref[c] * (sigma * (1.0 + value * (1.0 - sigma)))
        e_ref[cell_rows(c), :] = e
        return (bias_sum + fold8(e), gain_sum + fold8(e * normal))

    start = jnp.zeros((8, width), F32)
    bias_sum, gain_sum = lax.fori_loop(0, rows // CELL, one_cell, (start, start))
    send_sums(bias_sum, gain_sum, msg_ref)


def input_grad_kernel(
    place_ref, valid_ref, grad_ref, up, down, side, cup, cdown, dpre_ref, out_ref
):
    add_halo(place_ref, grad_ref, out_ref, (up, down, side, cup, cdown))

    def one_cell(c, carry):
        rows = cell_rows(c)
        out_ref[rows, :] = (out_ref[rows, :] + dpre_ref[rows, :]) * valid_ref[c]
        return carry

    lax.fori_loop(0, out_ref.shape[0] // CELL, one_cell, 0)


def temporal_kernel(
    valid_ref, s_ref, msg_ref, gb_ref, wt_ref, columns_ref, t_ref, stats_ref, out_ref, *, index
):
    rows, middle = s_ref.shape
    mean, rstd, count = receive_stats(msg_ref)
    keep_stats(stats_ref, mean, rstd, count)
    gain, bias = gb_ref[2 * index : 2 * index + 1, :], gb_ref[2 * index + 1 : 2 * index + 2, :]

    def one_cell(c, _):
        value = (s_ref[cell_rows(c), :] - mean) * rstd * gain + bias
        inner = value * sigmoid(value) * valid_ref[c]
        columns_ref[cell_rows(c), 0:middle] = earlier_frame(inner).astype(BF16)
        columns_ref[cell_rows(c), middle : 2 * middle] = inner.astype(BF16)
        columns_ref[cell_rows(c), 2 * middle : 3 * middle] = later_frame(inner).astype(BF16)
        return 0

    lax.fori_loop(0, rows // CELL, one_cell, 0)

    def one_block(i, _):
        t_ref[block_rows(i, 320), :] = jnp.dot(
            columns_ref[block_rows(i, 320), :], wt_ref[...], preferred_element_type=F32
        )
        return 0

    lax.fori_loop(0, rows // 320, one_block, 0)
    send_stats(t_ref, valid_ref, out_ref)


def middle_kernel(
    place_ref, valid_ref, t_ref, msg_ref, gb_ref, stats_ref, tile_ref, top, bottom, side, ctop, cbottom,
    *, index,
):
    width = t_ref.shape[1]
    rows, cols = tile_ref.shape[:2]
    mean, rstd, count = receive_stats(msg_ref)
    keep_stats(stats_ref, mean, rstd, count)
    gain, bias = gb_ref[2 * index : 2 * index + 1, :width], gb_ref[2 * index + 1 : 2 * index + 2, :width]
    for r in range(rows):
        for c in range(cols):
            number = r * cols + c
            value = (t_ref[number * CELL : (number + 1) * CELL, :] - mean) * rstd * gain + bias
            tile_ref[r, c] = (value * sigmoid(value) * valid_ref[number]).astype(BF16)
    write_edges(place_ref, tile_ref, (top, bottom, side, ctop, cbottom))


def top_kernel(
    valid_ref, t_ref, msg_ref, gb_ref, x_ref, cot_ref, stats_ref, out_ref, dpre_ref, msg_out, *, index
):
    rows, width = t_ref.shape
    mean, rstd, count = receive_stats(msg_ref)
    keep_stats(stats_ref, mean, rstd, count)
    gain, bias = gb_ref[2 * index : 2 * index + 1, :width], gb_ref[2 * index + 1 : 2 * index + 2, :width]

    def one_cell(c, carry):
        bias_sum, gain_sum = carry
        normal = (t_ref[cell_rows(c), :] - mean) * rstd
        pre = normal * gain + bias + x_ref[cell_rows(c), :].astype(F32)
        sigma = sigmoid(pre)
        valid = valid_ref[c]
        out_ref[cell_rows(c), :] = pre * sigma * valid
        dpre = cot_ref[cell_rows(c), :].astype(F32) * valid * (sigma * (1.0 + pre * (1.0 - sigma)))
        dpre_ref[cell_rows(c), :] = dpre
        return (bias_sum + fold8(dpre), gain_sum + fold8(dpre * normal))

    start = jnp.zeros((8, width), F32)
    bias_sum, gain_sum = lax.fori_loop(0, rows // CELL, one_cell, (start, start))
    send_sums(bias_sum, gain_sum, msg_out)


def temporal_grad_kernel(
    valid_ref, e_ref, t_ref, tstats_ref, msg_ref, s_ref, sstats_ref, gb_ref, wt_ref,
    dt_ref, en_ref, sums_ref, msg_out, columns_ref, *, index,
):
    rows, width = e_ref.shape
    middle = s_ref.shape[1]
    bias_grad, gain_grad = receive_sums(msg_ref)
    sums_ref[0:1, :] = gain_grad
    sums_ref[1:2, :] = bias_grad
    mean, rstd, count = tstats_ref[0:1, :], tstats_ref[1:2, :], tstats_ref[2:3, :]
    gain = gb_ref[2 * index + 2 : 2 * index + 3, :width]

    def one_cell(c, _):
        normal = (t_ref[cell_rows(c), :] - mean) * rstd
        dt = (rstd * gain) * (
            e_ref[cell_rows(c), :] - valid_ref[c] * ((bias_grad + normal * gain_grad) / count)
        )
        dt_ref[cell_rows(c), :] = dt.astype(BF16)
        columns_ref[cell_rows(c), 0:width] = later_frame(dt).astype(BF16)
        columns_ref[cell_rows(c), width : 2 * width] = dt.astype(BF16)
        columns_ref[cell_rows(c), 2 * width : 3 * width] = earlier_frame(dt).astype(BF16)
        return 0

    lax.fori_loop(0, rows // CELL, one_cell, 0)

    def one_block(i, _):
        total = None
        for tap in range(3):
            term = lax.dot_general(
                columns_ref[block_rows(i, 320), tap * width : (tap + 1) * width],
                wt_ref[tap * middle : (tap + 1) * middle, :],
                (((1,), (1,)), ((), ())),
                preferred_element_type=F32,
            )
            total = term if total is None else total + term
        en_ref[block_rows(i, 320), :] = total
        return 0

    lax.fori_loop(0, rows // 320, one_block, 0)
    mean_s, rstd_s = sstats_ref[0:1, :], sstats_ref[1:2, :]
    gain_s, bias_s = gb_ref[2 * index : 2 * index + 1, :], gb_ref[2 * index + 1 : 2 * index + 2, :]

    def one_mid_cell(c, carry):
        bias_sum, gain_sum = carry
        normal = (s_ref[cell_rows(c), :] - mean_s) * rstd_s
        value = normal * gain_s + bias_s
        sigma = sigmoid(value)
        e = en_ref[cell_rows(c), :] * valid_ref[c] * (sigma * (1.0 + value * (1.0 - sigma)))
        en_ref[cell_rows(c), :] = e
        return (bias_sum + fold8(e), gain_sum + fold8(e * normal))

    start = jnp.zeros((8, middle), F32)
    bias_sum, gain_sum = lax.fori_loop(0, rows // CELL, one_mid_cell, (start, start))
    send_sums(bias_sum, gain_sum, msg_out)


def temporal_weight_kernel(columns_ref, dt_ref, grad_ref):
    middle = columns_ref.shape[1] // 3
    for tap in range(3):
        grad_ref[tap * middle : (tap + 1) * middle, :] = lax.dot_general(
            columns_ref[:, tap * middle : (tap + 1) * middle],
            dt_ref[...],
            (((0,), (0,)), ((), ())),
            preferred_element_type=F32,
        )


def ds_kernel(
    place_ref, valid_ref, en_ref, s_ref, stats_ref, msg_ref, gb_ref, ws_ref,
    sums_ref, ds_ref, top, bottom, side, ctop, cbottom, row_ref, *, index,
):
    rows, cols = ds_ref.shape[0], ds_ref.shape[1] - 4
    bias_grad, gain_grad = receive_sums(msg_ref)
    sums_ref[0:1, :] = gain_grad
    sums_ref[1:2, :] = bias_grad
    mean, rstd, count = stats_ref[0:1, :], stats_ref[1:2, :], stats_ref[2:3, :]
    scale = rstd * gb_ref[2 * index : 2 * index + 1, :]
    for r in range(rows):
        for c in (0, 1, cols + 2, cols + 3):
            ds_ref[r, c] = jnp.zeros(ds_ref.shape[2:], BF16)
        for c in range(cols):
            number = r * cols + c
            block = slice(number * CELL, (number + 1) * CELL)
            normal = (s_ref[block, :] - mean) * rstd
            ds_ref[r, c + 2] = (
                scale
                * (en_ref[block, :] - valid_ref[number] * ((bias_grad + normal * gain_grad) / count))
            ).astype(BF16)
    edge_grads(place_ref, ds_ref, ws_ref, (top, bottom, side, ctop, cbottom), row_ref)


def run(kernel, ins, outs, scratch=(), scalars=0, us=1.0, extra=8, loose=(), spec=VMEM, **settings):
    held = sum(
        math.prod(x.shape) * jnp.dtype(x.dtype).itemsize
        for x in scratch
        if x.memory_space == pltpu.VMEM
    )
    return pl.pallas_call(
        functools.partial(kernel, **settings),
        out_shape=[
            jax.ShapeDtypeStruct(shape, dtype) if i in loose else pltpu.VMEM(shape, dtype)
            for i, (shape, dtype) in enumerate(outs)
        ],
        in_specs=[SMEM] * scalars + [spec] * (len(ins) - scalars),
        out_specs=[VMEM] * len(outs),
        scratch_shapes=list(scratch),
        cost_estimate=pl.CostEstimate(
            flops=int(us * 1.1e9), bytes_accessed=1000, transcendentals=0
        ),
        compiler_params=pltpu.CompilerParams(vmem_limit_bytes=held + extra * 2**20),
    )(*ins)


def ranks_of_pieces(owner_ids, devices):
    block = 64
    onehot = (owner_ids.reshape(-1, block, 1) == jnp.arange(devices, dtype=jnp.int32)).astype(BF16)
    earlier = jnp.tril(jnp.ones((block, block), BF16), -1)
    within = jnp.einsum("ij,bjd->bid", earlier, onehot, preferred_element_type=F32)
    sums = jnp.sum(onehot.astype(F32), axis=1)
    blocks = jnp.tril(jnp.ones((sums.shape[0],) * 2, F32), -1)
    before = jnp.sum(blocks[:, :, None] * sums[None], axis=1)
    ranking = jnp.sum(onehot.astype(F32) * (within + before[:, None, :]), axis=-1)
    return ranking.reshape(-1).astype(jnp.int32)


def moved_by(step, size):
    return [(i, (i + step) % size) for i in range(size)]


def mirrored(bit, size):
    return [(i, i ^ bit) for i in range(size)]


def gather_parts(own, beside):
    batches, heights = lax.axis_size("batch"), lax.axis_size("ha")
    steps = [own] + [
        lax.ppermute(own, "batch", moved_by(k, batches)) for k in range(1, batches)
    ]
    half = batches // 2
    one, two = jnp.concatenate(steps[:half]), jnp.concatenate(steps[half:])
    one = jnp.concatenate([one, lax.ppermute(one, "ha", mirrored(1, heights))])
    two = jnp.concatenate([two, lax.ppermute(two, "ha", mirrored(2, heights))])
    one, two, beside = together(one, two, beside)
    parts = [
        one,
        lax.ppermute(one, "ha", mirrored(2, heights)),
        two,
        lax.ppermute(two, "ha", mirrored(1, heights)),
    ]
    return parts + [lax.ppermute(part, "wa", mirrored(1, 2)) for part in parts], beside


def part_position(owner_ids, place):
    batches, heights, cores = (lax.axis_size(axis) for axis in AXES)
    z, h, w = place
    core = (owner_ids % cores) ^ w
    turn = (owner_ids // cores % heights) ^ h
    step = (z - owner_ids // (cores * heights)) % batches
    half = batches // 2
    swapped = jnp.where(turn == 1, 2, jnp.where(turn == 2, 1, turn))
    block = jnp.where(
        step < half, turn * half + step, heights * half + swapped * half + step - half
    )
    return core * batches * heights + block


def target_position(owner_ids, place):
    batches, heights, cores = (lax.axis_size(axis) for axis in AXES)
    z, h, w = place
    core = (owner_ids % cores) ^ w
    turn = (owner_ids // cores % heights) ^ h
    step = (owner_ids // (cores * heights) - z) % batches
    return (core * heights + turn) * batches + step


def add_low(a, b):
    return (a.astype(F32) + b.astype(F32)).astype(BF16)


def sum_cores(packed):
    heights = lax.axis_size("ha")
    rows = packed.shape[0] // (2 * heights)
    other = lax.ppermute(packed[heights * rows :], "wa", mirrored(1, 2))
    return add_low(packed[: heights * rows], other).reshape(heights, rows, LANES)


def sum_chips_first(both):
    heights, rows = both.shape[:2]
    half = rows // 2
    one, two = both[:, :half], both[:, half:]
    one_in = lax.ppermute(jnp.concatenate([one[1], one[3]]), "ha", mirrored(1, heights))
    two_in = lax.ppermute(jnp.concatenate([two[2], two[3]]), "ha", mirrored(2, heights))
    return [
        add_low(one[0], one_in[:half]),
        add_low(one[2], one_in[half:]),
        add_low(two[0], two_in[:half]),
        add_low(two[1], two_in[half:]),
    ]


def sum_chips_second(sums):
    one, one_out, two, two_out = sums
    heights, batches = lax.axis_size("ha"), lax.axis_size("batch")
    one_in = lax.ppermute(one_out, "ha", mirrored(2, heights))
    two_in = lax.ppermute(two_out, "ha", mirrored(1, heights))
    own = jnp.concatenate([add_low(one, one_in), add_low(two, two_in)])
    return own.reshape(batches, -1, LANES)


def sum_batch(own):
    batches = own.shape[0]
    total = own[0].astype(F32)
    for k in range(1, batches):
        total = total + lax.ppermute(own[k], "batch", moved_by(k, batches)).astype(F32)
    return total


def scatter_sums(packed):
    return sum_batch(sum_chips_second(sum_chips_first(sum_cores(packed))))


def together(*values):
    return lax.optimization_barrier(values)


def exchange(message):
    return lax.all_to_all(message, AXES, 0, 0, tiled=True)


def swap_edges(edges):
    top, bottom, side, corner_top, corner_bottom = edges
    count = lax.axis_size("ha")
    cores = lax.axis_size("wa")
    forward = [(i, i + 1) for i in range(count - 1)]
    backward = [(i + 1, i) for i in range(count - 1)]
    across = [(0, 1), (1, 0)]

    def both(moves):
        return [(a * cores + i, b * cores + j) for a, b in moves for i, j in across]

    up = lax.ppermute(bottom, "ha", forward)
    down = lax.ppermute(top, "ha", backward)
    corner_up = lax.ppermute(corner_bottom, ("ha", "wa"), both(forward))
    corner_down = lax.ppermute(corner_top, ("ha", "wa"), both(backward))
    beside = lax.ppermute(side, "wa", across)
    return [up, down, beside, corner_up, corner_down]


def per_device(
    block_input,
    cotangent,
    frame_sides,
    owner_list,
    master_slots,
    first_slots,
    second_slots,
    norm_gains,
    norm_biases,
    norm_first,
    norm_second,
):
    clip_count, frames, tile_rows, tile_cols, width = block_input.shape
    devices = lax.axis_size(AXES)
    slot_count, piece_len = master_slots.shape
    middle = norm_gains.shape[0] // 2 - width
    middle_pad = -(-middle // LANES) * LANES
    rows = clip_count * frames * tile_rows * tile_cols

    low_slots = master_slots.astype(BF16).reshape(slot_count * PIECE_ROWS, LANES)

    own_side = frame_sides[0]
    row_ids = lax.axis_index("ha") * tile_rows + jnp.arange(tile_rows, dtype=jnp.int32)
    col_ids = lax.axis_index("wa") * tile_cols + jnp.arange(tile_cols, dtype=jnp.int32)
    grid_rows = tile_rows * lax.axis_size("ha")
    grid_cols = tile_cols * lax.axis_size("wa")
    valid = (
        (row_ids[:, None] >= grid_rows - own_side) & (col_ids[None, :] >= grid_cols - own_side)
    ).astype(F32)
    valid_flat = valid.reshape(-1)
    place = lax.axis_index("wa").reshape(1)
    owner_ids = owner_list[:, 0]
    ranking = ranks_of_pieces(owner_ids, devices)
    here = [lax.axis_index(axis) for axis in AXES]
    slot_index = part_position(owner_ids, here) * slot_count + ranking
    half = owner_list.shape[0] // 2
    kept = min(slot_count, int(slot_count / 2 + 1.83 * math.sqrt(slot_count)))
    target = target_position(owner_ids, here)
    all_slots = target * slot_count + ranking
    late_rank = ranking[half:] - (slot_count - kept)
    fits = jnp.all(ranking[:half] < kept) & jnp.all(late_rank >= 0)
    early_slots = jnp.where(fits, target[:half] * kept + ranking[:half], 0)
    late_slots = jnp.where(fits, target[half:] * kept + late_rank, 0)

    bounds = [0, middle, middle + width, 2 * middle + width, 2 * middle + 2 * width]
    gb = []
    for i in range(4):
        for vector in (norm_gains, norm_biases):
            part = vector[bounds[i] : bounds[i + 1]]
            gb.append(jnp.pad(part, (0, middle_pad - part.shape[0])))
    gb = jnp.stack(gb)

    def to_tile(array):
        return jnp.transpose(array, (2, 3, 1, 0, 4)).reshape(tile_rows, tile_cols, CELL, width)

    x_tile = to_tile(block_input) * valid[:, :, None, None].astype(BF16)
    cot_tile = to_tile(cotangent)
    edge = jnp.where(place[0] == 0, tile_cols - 1, 0)
    x_side = lax.dynamic_index_in_dim(x_tile, edge, axis=1, keepdims=False)
    x_halo = swap_edges([x_tile[0], x_tile[-1], x_side, x_side[0], x_side[-1]])
    prepared = (x_tile, x_halo, cot_tile, valid_flat, gb, slot_index, all_slots, early_slots, late_slots, fits)
    parts, prepared = gather_parts(low_slots, prepared)
    x_tile, x_halo, cot_tile, valid_flat, gb, slot_index, all_slots, early_slots, late_slots, fits = prepared

    tap_rows = 9 * width
    stage = [pltpu.VMEM((UNROLL, 144, LANES), F32), pltpu.VMEM((UNROLL, 5, 32, LANES), F32)]
    weight_shapes = [((tap_rows, middle_pad), BF16), ((3 * middle_pad, width), BF16)]
    (all_weights,) = run(
        gather_weights_kernel,
        parts,
        [((devices * slot_count * PIECE_ROWS, LANES), BF16)],
        [pltpu.SemaphoreType.DMA((len(parts),))],
        us=3.0,
        spec=pl.BlockSpec(memory_space=pl.ANY),
    )

    def unpack(all_weights, unit):
        return run(
            unpack_weights_kernel,
            [slot_index, all_weights],
            weight_shapes,
            stage,
            1,
            4.3,
            base=unit * (owner_list.shape[0] // 2),
        )

    tile_shape = (tile_rows, tile_cols, CELL, width)
    padded_tile = (tile_rows + 2, tile_cols + 2, CELL, width)
    ds_shape = (tile_rows, tile_cols + 4, CELL, middle_pad)
    stats_mid = (devices, 1, 2 * middle_pad + LANES)
    stats_wide = (devices, 1, 2 * width + LANES)

    def edge_shapes(lanes):
        row, col = (tile_cols, CELL, lanes), (tile_rows, CELL, lanes)
        return [(row, BF16), (row, BF16), (col, BF16), ((CELL, lanes), BF16), ((CELL, lanes), BF16)]

    def unit_forward(tile, halo, ws, wt, index):
        padded, s, msg = run(
            spatial_kernel,
            [place, valid_flat, tile, *halo, ws],
            [(padded_tile, BF16), ((rows, middle_pad), F32), (stats_mid, F32)],
            us=5.5,
            scalars=2,
        )
        columns, t, s_stats, msg = run(
            temporal_kernel,
            [valid_flat, s, exchange(msg), gb, wt],
            [
                ((rows, 3 * middle_pad), BF16),
                ((rows, width), F32),
                ((8, middle_pad), F32),
                (stats_wide, F32),
            ],
            scalars=1,
            us=4.2,
            index=index,
        )
        return padded, s, s_stats, columns, t, exchange(msg)

    ws1, wt1 = unpack(all_weights, 0)
    padded1, s1, s_stats1, columns1, t1, msg = unit_forward(x_tile, x_halo, ws1, wt1, 0)
    t_stats1, y_tile, *edges = run(
        middle_kernel,
        [place, valid_flat, t1, msg, gb],
        [((8, width), F32), (tile_shape, BF16)] + edge_shapes(width),
        scalars=2,
        index=1,
    )
    edges, all_weights = together(edges, all_weights)
    halo = swap_edges(edges)
    ws2, wt2 = unpack(all_weights, 1)
    ws2, wt2, halo = together(ws2, wt2, halo)
    padded2, s2, s_stats2, columns2, t2, msg = unit_forward(y_tile, halo, ws2, wt2, 2)
    t_stats2, block_output, dpre, msg = run(
        top_kernel,
        [valid_flat, t2, msg, gb, x_tile.reshape(rows, width), cot_tile.reshape(rows, width)],
        [((8, width), F32), ((rows, width), F32), ((rows, width), F32), ((devices, 1, 2 * width), F32)],
        scalars=1,
        loose=(1,),
        index=3,
    )

    def unit_backward(e, msg, t, t_stats, s, s_stats, columns, padded, ws, wt, index, aside=None):
        dt, en, t_sums, msg = run(
            temporal_grad_kernel,
            [valid_flat, e, t, t_stats, exchange(msg), s, s_stats, gb, wt],
            [
                ((rows, width), BF16),
                ((rows, middle_pad), F32),
                ((2, width), F32),
                ((devices, 1, 2 * middle_pad), F32),
            ],
            [pltpu.VMEM((rows, 3 * width), BF16)],
            scalars=1,
            us=4.5,
            index=index,
        )
        if aside is not None:
            msg, aside = together(msg, sum_cores(aside))
        msg = exchange(msg)
        if aside is not None:
            msg, aside = together(msg, aside)
            aside = sum_chips_first(aside)
        s_sums, ds, *edges = run(
            ds_kernel,
            [place, valid_flat, en, s, s_stats, msg, gb, ws],
            [((2, middle_pad), F32), (ds_shape, BF16)] + edge_shapes(width),
            [pltpu.VMEM((tile_cols + 1, CELL, width), BF16)],
            scalars=2,
            us=4.0,
            index=index,
        )
        edges, columns, dt = together(edges, columns, dt)
        halo = swap_edges(edges)
        (wt_grad,) = run(temporal_weight_kernel, [columns, dt], [((3 * middle_pad, width), F32)], us=1.2)
        (ws_grad,) = run(spatial_weight_kernel, [padded, ds], [((tap_rows, middle_pad), F32)], us=4.0)
        (inner,) = run(spatial_grad_kernel, [ds, ws], [((rows, width), F32)], us=3.0)
        return inner, halo, (ws_grad, wt_grad), s_sums, t_sums, aside

    def pack(grads, positions, kept):
        (packed,) = run(
            pack_grads_kernel,
            [positions, *grads],
            [((devices * kept * PIECE_ROWS, LANES), BF16)],
            stage,
            scalars=1,
            us=5.0,
            loose=(0,),
        )
        return packed

    inner, halo, grads2, s_sums2, t_sums2, _ = unit_backward(
        dpre, msg, t2, t_stats2, s2, s_stats2, columns2, padded2, ws2, wt2, 2
    )
    packed2 = pack(grads2, late_slots, kept)
    inner, halo, packed2 = together(inner, halo, packed2)
    e1, msg = run(
        between_kernel,
        [place, valid_flat, inner, *halo, t1, t_stats1, gb],
        [((rows, width), F32), ((devices, 1, 2 * width), F32)],
        scalars=2,
        us=2.0,
        index=1,
    )
    inner, halo, grads1, s_sums1, t_sums1, sums2 = unit_backward(
        e1, msg, t1, t_stats1, s1, s_stats1, columns1, padded1, ws1, wt1, 0, packed2
    )
    packed1 = pack(grads1, early_slots, kept)
    packed1, sums2, block_output = together(packed1, sums2, block_output)
    sums2 = sum_batch(sum_chips_second(sums2))
    sums1 = scatter_sums(packed1)
    (input_grad,) = run(
        input_grad_kernel,
        [place, valid_flat, inner, *halo, dpre],
        [((rows, width), F32)],
        scalars=2,
        us=2.0,
        loose=(0,),
    )

    def joined(early, late):
        rest = (slot_count - kept) * PIECE_ROWS
        return jnp.pad(early, ((0, rest), (0, 0))) + jnp.pad(late, ((rest, 0), (0, 0)))

    def whole(grads1, grads2):
        return scatter_sums(
            pack(grads1, all_slots[:half], slot_count) + pack(grads2, all_slots[half:], slot_count)
        )

    if kept == slot_count:
        grad_mine = joined(sums1, sums2)
    else:
        grad_mine = lax.cond(
            fits,
            lambda early, late, *_: joined(early, late),
            lambda early, late, ones, twos: whole(ones, twos),
            sums1,
            sums2,
            grads1,
            grads2,
        )

    def from_tile(array):
        array = array.reshape(tile_rows, tile_cols, frames, clip_count, width)
        return jnp.transpose(array, (3, 2, 0, 1, 4))

    grad_mine = grad_mine.reshape(slot_count, piece_len)
    correction = 1.0 - 0.5**STEP
    step_rate = 1.8 / math.sqrt(9.0 * width)
    first_new = 0.5 * first_slots + 0.5 * grad_mine
    second_new = 0.5 * second_slots + 0.5 * grad_mine * grad_mine
    master_new = master_slots - step_rate * (
        first_new / correction / (jnp.sqrt(second_new / correction) + ADAM_EPSILON)
        + DECAY_RATE * master_slots
    )
    weight_copy = master_new.astype(BF16)
    norm_grad = jnp.concatenate([s_sums1[:, :middle], t_sums1, s_sums2[:, :middle], t_sums2], axis=1)
    norm_pair = jnp.stack([norm_gains, norm_biases])
    norm_first_new = 0.5 * norm_first + 0.5 * norm_grad
    norm_second_new = 0.5 * norm_second + 0.5 * norm_grad * norm_grad
    norm_new = norm_pair - NORM_RATE * (norm_first_new / correction) / (
        jnp.sqrt(norm_second_new / correction) + ADAM_EPSILON
    )
    return (
        from_tile(block_output),
        from_tile(input_grad),
        master_new,
        first_new,
        second_new,
        weight_copy,
        norm_first_new,
        norm_second_new,
        norm_new,
    )


def solution(mesh):
    wide = P("batch", None, "ha", "wa", None)
    owned = P(AXES, None)
    return jax.shard_map(
        per_device,
        mesh=mesh,
        in_specs=(wide, wide, P("batch"), P(), owned, owned, owned, P(), P(), P(), P()),
        out_specs=(wide, wide, owned, owned, owned, owned, P(), P(), P()),
        check_vma=False,
    )
```

```python
import functools
import math

import jax
import jax.numpy as jnp
from jax import lax
from jax.experimental import pallas as pl
from jax.experimental.pallas import tpu as pltpu
from jax.sharding import PartitionSpec as P

STEP = 5
EPSILON = 1e-05
ADAM_EPSILON = 1e-08
DECAY_RATE = 0.1
NORM_RATE = 0.3

AXES = ("batch", "ha", "wa")
F32 = jnp.float32
BF16 = jnp.bfloat16
VMEM = pl.BlockSpec(memory_space=pltpu.VMEM)
SMEM = pl.BlockSpec(memory_space=pltpu.SMEM)
CELL = 64
LANES = 128
PIECE_ROWS = 16


def sigmoid(v):
    return 1.0 / (1.0 + jnp.exp(-v))


def cell_rows(index, count=1):
    return pl.ds(pl.multiple_of(index * CELL, CELL), count * CELL)


def block_rows(index, size):
    return pl.ds(pl.multiple_of(index * size, size), size)


def fold8(block):
    return jnp.sum(block.reshape(-1, 8, block.shape[-1]), axis=0)


def widen(lane_block, width):
    return jnp.concatenate([lane_block] * (width // LANES), axis=1)


def valid_rows(valid_ref, cells):
    total = valid_ref[0]
    for cell in range(1, cells):
        total = total + valid_ref[cell]
    return total * CELL


def send_stats(values_ref, valid_ref, msg_ref):
    rows, width = values_ref.shape
    cells = rows // CELL
    count = valid_rows(valid_ref, cells)

    def add(cell, total):
        return total + valid_ref[cell] * fold8(values_ref[cell_rows(cell), :])

    total = lax.fori_loop(0, cells, add, jnp.zeros((8, width), F32))
    total = jnp.sum(total, axis=0, keepdims=True)
    mean = total / jnp.maximum(jnp.full((1, width), count, F32), 1.0)

    def add_squares(cell, squares):
        centered = values_ref[cell_rows(cell), :] - mean
        return squares + valid_ref[cell] * fold8(centered * centered)

    squares = lax.fori_loop(0, cells, add_squares, jnp.zeros((8, width), F32))
    squares = jnp.sum(squares, axis=0, keepdims=True)
    message = jnp.concatenate([total, squares, jnp.full((1, LANES), count, F32)], axis=1)
    msg_ref[...] = jnp.broadcast_to(message[None], msg_ref.shape)


def receive_stats(msg_ref):
    devices, _, length = msg_ref.shape
    width = (length - LANES) // 2

    def add(i, carry):
        total, count = carry
        return (total + msg_ref[i, :, :width], count + msg_ref[i, :, 2 * width :])

    total, count = lax.fori_loop(
        0, devices, add, (jnp.zeros((1, width), F32), jnp.zeros((1, LANES), F32)), unroll=4
    )
    count = widen(count, width)
    mean = total / count

    def add_squares(i, squares):
        own = widen(msg_ref[i, :, 2 * width :], width)
        offset = msg_ref[i, :, :width] / jnp.maximum(own, 1.0) - mean
        return squares + msg_ref[i, :, width : 2 * width] + own * offset * offset

    squares = lax.fori_loop(0, devices, add_squares, jnp.zeros((1, width), F32), unroll=4)
    return mean, lax.rsqrt(squares / count + EPSILON), count


def keep_stats(stats_ref, mean, rstd, count):
    stats_ref[0:1, :] = mean
    stats_ref[1:2, :] = rstd
    stats_ref[2:3, :] = count


def receive_sums(msg_ref):
    devices, _, length = msg_ref.shape
    total = lax.fori_loop(
        0, devices, lambda i, t: t + msg_ref[i], jnp.zeros((1, length), F32), unroll=4
    )
    return total[:, : length // 2], total[:, length // 2 :]


def send_sums(bias, gain, msg_ref):
    message = jnp.concatenate(
        [jnp.sum(bias, axis=0, keepdims=True), jnp.sum(gain, axis=0, keepdims=True)], axis=1
    )
    msg_ref[...] = jnp.broadcast_to(message[None], msg_ref.shape)


def later_frame(block):
    return jnp.concatenate([block[8:], jnp.zeros((8, block.shape[1]), block.dtype)], axis=0)


def earlier_frame(block):
    return jnp.concatenate([jnp.zeros((8, block.shape[1]), block.dtype), block[:-8]], axis=0)


UNROLL = 4


def gather_weights_kernel(*refs):
    parts, all_ref, sems = refs[:-2], refs[-2], refs[-1]
    rows = parts[0].shape[0]
    copies = [
        pltpu.make_async_copy(part, all_ref.at[i * rows : (i + 1) * rows, :], sems.at[i])
        for i, part in enumerate(parts)
    ]
    for copy in copies:
        copy.start()
    for copy in copies:
        copy.wait()


def unpack_weights_kernel(slot_ref, all_ref, ws_ref, wt_ref, stage, turn, *, base):
    low = lax.broadcasted_iota(jnp.int32, (8, LANES), 1) < 64
    zero = jnp.zeros((8, LANES), F32)
    spatial_groups = ws_ref.shape[0] // 32

    def load_piece(number):
        start = pl.multiple_of(slot_ref[number] * PIECE_ROWS, PIECE_ROWS)
        return all_ref[pl.ds(start, PIECE_ROWS), :].astype(F32)

    def spatial_groups_at(k, _):
        first = k * UNROLL
        for u in range(UNROLL):
            for q in range(9):
                stage[u, 16 * q : 16 * q + 16, :] = load_piece(base + 9 * (first + u) + q)
        for u in range(UNROLL):
            for i in range(2):
                a = [stage[u, pl.ds(72 * i + j, 8, stride=9), :] for j in range(9)]
                r = [pltpu.roll(a[4 + j], 64, axis=1) for j in range(5)]
                even = a[:4] + [jnp.where(low, a[4], zero)]
                odd = [jnp.where(low, r[j], r[j + 1]) for j in range(4)]
                odd += [jnp.where(low, r[4], zero)]
                for j in range(5):
                    turn[u, j, pl.ds(16 * i, 8, stride=2), :] = even[j]
                    turn[u, j, pl.ds(16 * i + 1, 8, stride=2), :] = odd[j]
        for u in range(UNROLL):
            rows = block_rows(first + u, 32)
            for j in range(5):
                ws_ref[rows, LANES * j : LANES * (j + 1)] = turn[u, j].astype(BF16)
        return 0

    lax.fori_loop(0, spatial_groups // UNROLL, spatial_groups_at, 0)
    temporal_base = base + 9 * spatial_groups
    padded = wt_ref.shape[0] // 3
    pairs = (9 * spatial_groups) // 3 // 6
    for tap in range(3):

        def temporal_pairs(k, _):
            for u in range(UNROLL):
                first = temporal_base + tap * 2 * pairs + 2 * (k * UNROLL + u)
                stage[u, 0:16, :] = load_piece(first)
                stage[u, 16:32, :] = load_piece(first + 1)
            for u in range(UNROLL):
                start = tap * padded + (k * UNROLL + u) * 16
                rows = pl.ds(pl.multiple_of(start, 16), 16)
                for h in range(2):
                    half = stage[u, pl.ds(h, 16, stride=2), :]
                    wt_ref[rows, LANES * h : LANES * (h + 1)] = half.astype(BF16)
            return 0

        lax.fori_loop(0, pairs // UNROLL, temporal_pairs, 0)
        wt_ref[tap * padded + 16 * pairs : (tap + 1) * padded, :] = jnp.zeros(
            (padded - 16 * pairs, wt_ref.shape[1]), BF16
        )


def pack_grads_kernel(slot_ref, spatial, temporal, out_ref, stage, turn):
    low = lax.broadcasted_iota(jnp.int32, (8, LANES), 1) < 64
    spatial_groups = spatial.shape[0] // 32
    padded = temporal.shape[0] // 3
    pairs = (9 * spatial_groups) // 3 // 6

    def clear(i, _):
        out_ref[block_rows(i, 128), :] = jnp.zeros((128, LANES), BF16)
        return 0

    lax.fori_loop(0, out_ref.shape[0] // 128, clear, 0)

    def store_piece(number, rows16):
        start = pl.multiple_of(slot_ref[number] * PIECE_ROWS, PIECE_ROWS)
        out_ref[pl.ds(start, PIECE_ROWS), :] = rows16.astype(BF16)

    def spatial_groups_at(k, _):
        first = k * UNROLL
        for u in range(UNROLL):
            rows = block_rows(first + u, 32)
            for j in range(5):
                turn[u, j] = spatial[rows, LANES * j : LANES * (j + 1)]
        for u in range(UNROLL):
            for i in range(2):
                even = [turn[u, j, pl.ds(16 * i, 8, stride=2), :] for j in range(5)]
                odd = [turn[u, j, pl.ds(16 * i + 1, 8, stride=2), :] for j in range(5)]
                r = [pltpu.roll(odd[j], 64, axis=1) for j in range(5)]
                flat = even[:4] + [jnp.where(low, even[4], r[0])]
                flat += [jnp.where(low, r[j], r[j + 1]) for j in range(4)]
                for j in range(9):
                    stage[u, pl.ds(72 * i + j, 8, stride=9), :] = flat[j]
        for u in range(UNROLL):
            for q in range(9):
                store_piece(9 * (first + u) + q, stage[u, 16 * q : 16 * q + 16, :])
        return 0

    lax.fori_loop(0, spatial_groups // UNROLL, spatial_groups_at, 0)
    base = 9 * spatial_groups
    for tap in range(3):

        def temporal_pairs(k, _):
            for u in range(UNROLL):
                start = tap * padded + (k * UNROLL + u) * 16
                rows = pl.ds(pl.multiple_of(start, 16), 16)
                for h in range(2):
                    stage[u, pl.ds(h, 16, stride=2), :] = temporal[
                        rows, LANES * h : LANES * (h + 1)
                    ]
            for u in range(UNROLL):
                first = base + tap * 2 * pairs + 2 * (k * UNROLL + u)
                store_piece(first, stage[u, 0:16, :])
                store_piece(first + 1, stage[u, 16:32, :])
            return 0

        lax.fori_loop(0, pairs // UNROLL, temporal_pairs, 0)


def fill_padded(place_ref, padded_ref, tile_ref, halo_refs):
    up, down, side, corner_up, corner_down = halo_refs
    rows, cols = tile_ref.shape[:2]
    padded_ref[1 : rows + 1, 1 : cols + 1] = tile_ref[...]
    padded_ref[0, 1 : cols + 1] = up[...]
    padded_ref[rows + 1, 1 : cols + 1] = down[...]
    for core in range(2):
        near, far = (cols + 1, 0) if core == 0 else (0, cols + 1)

        @pl.when(place_ref[0] == core)
        def _():
            padded_ref[1 : rows + 1, near] = side[...]
            padded_ref[0, near] = corner_up[...]
            padded_ref[rows + 1, near] = corner_down[...]
            padded_ref[:, far] = jnp.zeros((rows + 2,) + tile_ref.shape[2:], BF16)


def write_edges(place_ref, tile_ref, edge_refs):
    top, bottom, side, corner_top, corner_bottom = edge_refs
    rows, cols = tile_ref.shape[:2]
    top[...] = tile_ref[0]
    bottom[...] = tile_ref[rows - 1]
    edge = jnp.where(place_ref[0] == 0, cols - 1, 0)
    side[...] = tile_ref[:, edge]
    corner_top[...] = tile_ref[0, edge]
    corner_bottom[...] = tile_ref[rows - 1, edge]


def spatial_kernel(
    place_ref, valid_ref, tile_ref, up, down, side, cup, cdown, ws_ref, padded_ref, s_ref, msg_ref
):
    rows, cols, cell, width = tile_ref.shape
    fill_padded(place_ref, padded_ref, tile_ref, (up, down, side, cup, cdown))

    def one_row(r, _):
        windows = []
        for row_tap in range(3):
            for col_tap in range(3):
                window = padded_ref[r + row_tap, col_tap : col_tap + cols]
                windows.append(window.reshape(cols * cell, width))
        s_ref[block_rows(r, cols * cell), :] = jnp.dot(
            jnp.concatenate(windows, axis=1), ws_ref[...], preferred_element_type=F32
        )
        return 0

    lax.fori_loop(0, rows, one_row, 0)
    send_stats(s_ref, valid_ref, msg_ref)


def weight_back(window, ws_ref, tap, width):
    return lax.dot_general(
        window.reshape(-1, window.shape[-1]),
        ws_ref[block_rows(tap, width), :],
        (((1,), (1,)), ((), ())),
        preferred_element_type=F32,
    )


def edge_grads(place_ref, ds_ref, ws_ref, edge_refs, row_ref):
    top, bottom, side, corner_top, corner_bottom = edge_refs
    width = top.shape[-1]
    cols, cell = top.shape[:2]
    rows = side.shape[0]
    core = place_ref[0]
    for row, row_tap, out, corner in ((0, 0, top, corner_top), (rows - 1, 2, bottom, corner_bottom)):
        total = None
        for col_tap in range(3):
            window = ds_ref[row, pl.ds(3 - core - col_tap, cols + 1)]
            term = weight_back(window, ws_ref, 3 * row_tap + col_tap, width)
            total = term if total is None else total + term
        row_ref[...] = total.astype(BF16).reshape(row_ref.shape)
        out[...] = row_ref[pl.ds(core, cols)]
        corner[...] = row_ref[cols * (1 - core)]
    column = ds_ref[:, jnp.where(core == 0, cols + 1, 2)]
    above, level, below = [
        weight_back(column, ws_ref, 3 * row_tap + 2 - 2 * core, width) for row_tap in range(3)
    ]
    empty = jnp.zeros((cell, width), F32)
    total = level + jnp.concatenate([above[cell:], empty]) + jnp.concatenate([empty, below[:-cell]])
    side[...] = total.astype(BF16).reshape(side.shape)


def spatial_grad_kernel(ds_ref, ws_ref, grad_ref):
    rows, cols, cell = ds_ref.shape[0], ds_ref.shape[1] - 4, ds_ref.shape[2]
    width = grad_ref.shape[1]
    for row in range(rows):
        total = None
        for row_tap in range(3):
            if not 0 <= row + 1 - row_tap < rows:
                continue
            for col_tap in range(3):
                window = ds_ref[row + 1 - row_tap, 3 - col_tap : 3 - col_tap + cols]
                term = weight_back(window, ws_ref, 3 * row_tap + col_tap, width)
                total = term if total is None else total + term
        grad_ref[row * cols * cell : (row + 1) * cols * cell, :] = total


def add_halo(place_ref, grad_ref, out_ref, halo_refs):
    up, down, side, corner_up, corner_down = halo_refs
    rows, cols = side.shape[0], up.shape[0]
    edge = jnp.where(place_ref[0] == 0, cols - 1, 0)
    out_ref[...] = grad_ref[...]
    last = (rows - 1) * cols
    for c in range(cols):
        out_ref[cell_rows(c), :] += up[c].astype(F32)
        out_ref[cell_rows(last + c), :] += down[c].astype(F32)
    for r in range(rows):
        out_ref[cell_rows(r * cols + edge), :] += side[r].astype(F32)
    out_ref[cell_rows(edge), :] += corner_up[...].astype(F32)
    out_ref[cell_rows(last + edge), :] += corner_down[...].astype(F32)


def spatial_weight_kernel(padded_ref, ds_ref, grad_ref):
    rows, cols, cell, middle = ds_ref.shape
    cols = cols - 4
    width = padded_ref.shape[-1]
    grads = ds_ref[:, 2 : cols + 2].reshape(rows * cols * cell, middle)
    for row_tap in range(3):
        for col_tap in range(3):
            window = padded_ref[row_tap : row_tap + rows, col_tap : col_tap + cols]
            tap = 3 * row_tap + col_tap
            grad_ref[tap * width : (tap + 1) * width, :] = lax.dot_general(
                window.reshape(rows * cols * cell, width),
                grads,
                (((0,), (0,)), ((), ())),
                preferred_element_type=F32,
            )


def between_kernel(
    place_ref, valid_ref, grad_ref, up, down, side, cup, cdown, t_ref, stats_ref, gb_ref,
    e_ref, msg_ref, *, index,
):
    rows, width = e_ref.shape
    add_halo(place_ref, grad_ref, e_ref, (up, down, side, cup, cdown))
    mean, rstd = stats_ref[0:1, :], stats_ref[1:2, :]
    gain, bias = gb_ref[2 * index : 2 * index + 1, :width], gb_ref[2 * index + 1 : 2 * index + 2, :width]

    def one_cell(c, carry):
        bias_sum, gain_sum = carry
        normal = (t_ref[cell_rows(c), :] - mean) * rstd
        value = normal * gain + bias
        sigma = sigmoid(value)
        e = e_ref[cell_rows(c), :] * valid_ref[c] * (sigma * (1.0 + value * (1.0 - sigma)))
        e_ref[cell_rows(c), :] = e
        return (bias_sum + fold8(e), gain_sum + fold8(e * normal))

    start = jnp.zeros((8, width), F32)
    bias_sum, gain_sum = lax.fori_loop(0, rows // CELL, one_cell, (start, start))
    send_sums(bias_sum, gain_sum, msg_ref)


def input_grad_kernel(
    place_ref, valid_ref, grad_ref, up, down, side, cup, cdown, dpre_ref, out_ref
):
    add_halo(place_ref, grad_ref, out_ref, (up, down, side, cup, cdown))

    def one_cell(c, carry):
        rows = cell_rows(c)
        out_ref[rows, :] = (out_ref[rows, :] + dpre_ref[rows, :]) * valid_ref[c]
        return carry

    lax.fori_loop(0, out_ref.shape[0] // CELL, one_cell, 0)


def temporal_kernel(
    valid_ref, s_ref, msg_ref, gb_ref, wt_ref, columns_ref, t_ref, stats_ref, out_ref, *, index
):
    rows, middle = s_ref.shape
    mean, rstd, count = receive_stats(msg_ref)
    keep_stats(stats_ref, mean, rstd, count)
    gain, bias = gb_ref[2 * index : 2 * index + 1, :], gb_ref[2 * index + 1 : 2 * index + 2, :]

    def one_cell(c, _):
        value = (s_ref[cell_rows(c), :] - mean) * rstd * gain + bias
        inner = value * sigmoid(value) * valid_ref[c]
        columns_ref[cell_rows(c), 0:middle] = earlier_frame(inner).astype(BF16)
        columns_ref[cell_rows(c), middle : 2 * middle] = inner.astype(BF16)
        columns_ref[cell_rows(c), 2 * middle : 3 * middle] = later_frame(inner).astype(BF16)
        return 0

    lax.fori_loop(0, rows // CELL, one_cell, 0)

    def one_block(i, _):
        t_ref[block_rows(i, 320), :] = jnp.dot(
            columns_ref[block_rows(i, 320), :], wt_ref[...], preferred_element_type=F32
        )
        return 0

    lax.fori_loop(0, rows // 320, one_block, 0)
    send_stats(t_ref, valid_ref, out_ref)


def middle_kernel(
    place_ref, valid_ref, t_ref, msg_ref, gb_ref, stats_ref, tile_ref, top, bottom, side, ctop, cbottom,
    *, index,
):
    width = t_ref.shape[1]
    rows, cols = tile_ref.shape[:2]
    mean, rstd, count = receive_stats(msg_ref)
    keep_stats(stats_ref, mean, rstd, count)
    gain, bias = gb_ref[2 * index : 2 * index + 1, :width], gb_ref[2 * index + 1 : 2 * index + 2, :width]
    for r in range(rows):
        for c in range(cols):
            number = r * cols + c
            value = (t_ref[number * CELL : (number + 1) * CELL, :] - mean) * rstd * gain + bias
            tile_ref[r, c] = (value * sigmoid(value) * valid_ref[number]).astype(BF16)
    write_edges(place_ref, tile_ref, (top, bottom, side, ctop, cbottom))


def top_kernel(
    valid_ref, t_ref, msg_ref, gb_ref, x_ref, cot_ref, stats_ref, out_ref, dpre_ref, msg_out, *, index
):
    rows, width = t_ref.shape
    mean, rstd, count = receive_stats(msg_ref)
    keep_stats(stats_ref, mean, rstd, count)
    gain, bias = gb_ref[2 * index : 2 * index + 1, :width], gb_ref[2 * index + 1 : 2 * index + 2, :width]

    def one_cell(c, carry):
        bias_sum, gain_sum = carry
        normal = (t_ref[cell_rows(c), :] - mean) * rstd
        pre = normal * gain + bias + x_ref[cell_rows(c), :].astype(F32)
        sigma = sigmoid(pre)
        valid = valid_ref[c]
        out_ref[cell_rows(c), :] = pre * sigma * valid
        dpre = cot_ref[cell_rows(c), :].astype(F32) * valid * (sigma * (1.0 + pre * (1.0 - sigma)))
        dpre_ref[cell_rows(c), :] = dpre
        return (bias_sum + fold8(dpre), gain_sum + fold8(dpre * normal))

    start = jnp.zeros((8, width), F32)
    bias_sum, gain_sum = lax.fori_loop(0, rows // CELL, one_cell, (start, start))
    send_sums(bias_sum, gain_sum, msg_out)


def temporal_grad_kernel(
    valid_ref, e_ref, t_ref, tstats_ref, msg_ref, s_ref, sstats_ref, gb_ref, wt_ref,
    dt_ref, en_ref, sums_ref, msg_out, columns_ref, *, index,
):
    rows, width = e_ref.shape
    middle = s_ref.shape[1]
    bias_grad, gain_grad = receive_sums(msg_ref)
    sums_ref[0:1, :] = gain_grad
    sums_ref[1:2, :] = bias_grad
    mean, rstd, count = tstats_ref[0:1, :], tstats_ref[1:2, :], tstats_ref[2:3, :]
    gain = gb_ref[2 * index + 2 : 2 * index + 3, :width]

    def one_cell(c, _):
        normal = (t_ref[cell_rows(c), :] - mean) * rstd
        dt = (rstd * gain) * (
            e_ref[cell_rows(c), :] - valid_ref[c] * ((bias_grad + normal * gain_grad) / count)
        )
        dt_ref[cell_rows(c), :] = dt.astype(BF16)
        columns_ref[cell_rows(c), 0:width] = later_frame(dt).astype(BF16)
        columns_ref[cell_rows(c), width : 2 * width] = dt.astype(BF16)
        columns_ref[cell_rows(c), 2 * width : 3 * width] = earlier_frame(dt).astype(BF16)
        return 0

    lax.fori_loop(0, rows // CELL, one_cell, 0)

    def one_block(i, _):
        total = None
        for tap in range(3):
            term = lax.dot_general(
                columns_ref[block_rows(i, 320), tap * width : (tap + 1) * width],
                wt_ref[tap * middle : (tap + 1) * middle, :],
                (((1,), (1,)), ((), ())),
                preferred_element_type=F32,
            )
            total = term if total is None else total + term
        en_ref[block_rows(i, 320), :] = total
        return 0

    lax.fori_loop(0, rows // 320, one_block, 0)
    mean_s, rstd_s = sstats_ref[0:1, :], sstats_ref[1:2, :]
    gain_s, bias_s = gb_ref[2 * index : 2 * index + 1, :], gb_ref[2 * index + 1 : 2 * index + 2, :]

    def one_mid_cell(c, carry):
        bias_sum, gain_sum = carry
        normal = (s_ref[cell_rows(c), :] - mean_s) * rstd_s
        value = normal * gain_s + bias_s
        sigma = sigmoid(value)
        e = en_ref[cell_rows(c), :] * valid_ref[c] * (sigma * (1.0 + value * (1.0 - sigma)))
        en_ref[cell_rows(c), :] = e
        return (bias_sum + fold8(e), gain_sum + fold8(e * normal))

    start = jnp.zeros((8, middle), F32)
    bias_sum, gain_sum = lax.fori_loop(0, rows // CELL, one_mid_cell, (start, start))
    send_sums(bias_sum, gain_sum, msg_out)


def temporal_weight_kernel(columns_ref, dt_ref, grad_ref):
    middle = columns_ref.shape[1] // 3
    for tap in range(3):
        grad_ref[tap * middle : (tap + 1) * middle, :] = lax.dot_general(
            columns_ref[:, tap * middle : (tap + 1) * middle],
            dt_ref[...],
            (((0,), (0,)), ((), ())),
            preferred_element_type=F32,
        )


def ds_kernel(
    place_ref, valid_ref, en_ref, s_ref, stats_ref, msg_ref, gb_ref, ws_ref,
    sums_ref, ds_ref, top, bottom, side, ctop, cbottom, row_ref, *, index,
):
    rows, cols = ds_ref.shape[0], ds_ref.shape[1] - 4
    bias_grad, gain_grad = receive_sums(msg_ref)
    sums_ref[0:1, :] = gain_grad
    sums_ref[1:2, :] = bias_grad
    mean, rstd, count = stats_ref[0:1, :], stats_ref[1:2, :], stats_ref[2:3, :]
    scale = rstd * gb_ref[2 * index : 2 * index + 1, :]
    for r in range(rows):
        for c in (0, 1, cols + 2, cols + 3):
            ds_ref[r, c] = jnp.zeros(ds_ref.shape[2:], BF16)
        for c in range(cols):
            number = r * cols + c
            block = slice(number * CELL, (number + 1) * CELL)
            normal = (s_ref[block, :] - mean) * rstd
            ds_ref[r, c + 2] = (
                scale
                * (en_ref[block, :] - valid_ref[number] * ((bias_grad + normal * gain_grad) / count))
            ).astype(BF16)
    edge_grads(place_ref, ds_ref, ws_ref, (top, bottom, side, ctop, cbottom), row_ref)


def run(kernel, ins, outs, scratch=(), scalars=0, us=1.0, extra=8, loose=(), spec=VMEM, **settings):
    held = sum(
        math.prod(x.shape) * jnp.dtype(x.dtype).itemsize
        for x in scratch
        if x.memory_space == pltpu.VMEM
    )
    return pl.pallas_call(
        functools.partial(kernel, **settings),
        out_shape=[
            jax.ShapeDtypeStruct(shape, dtype) if i in loose else pltpu.VMEM(shape, dtype)
            for i, (shape, dtype) in enumerate(outs)
        ],
        in_specs=[SMEM] * scalars + [spec] * (len(ins) - scalars),
        out_specs=[VMEM] * len(outs),
        scratch_shapes=list(scratch),
        cost_estimate=pl.CostEstimate(
            flops=int(us * 1.1e9), bytes_accessed=1000, transcendentals=0
        ),
        compiler_params=pltpu.CompilerParams(vmem_limit_bytes=held + extra * 2**20),
    )(*ins)


def ranks_of_pieces(owner_ids, devices):
    block = 64
    onehot = (owner_ids.reshape(-1, block, 1) == jnp.arange(devices, dtype=jnp.int32)).astype(BF16)
    earlier = jnp.tril(jnp.ones((block, block), BF16), -1)
    within = jnp.einsum("ij,bjd->bid", earlier, onehot, preferred_element_type=F32)
    sums = jnp.sum(onehot.astype(F32), axis=1)
    blocks = jnp.tril(jnp.ones((sums.shape[0],) * 2, F32), -1)
    before = jnp.sum(blocks[:, :, None] * sums[None], axis=1)
    ranking = jnp.sum(onehot.astype(F32) * (within + before[:, None, :]), axis=-1)
    return ranking.reshape(-1).astype(jnp.int32)


def moved_by(step, size):
    return [(i, (i + step) % size) for i in range(size)]


def mirrored(bit, size):
    return [(i, i ^ bit) for i in range(size)]


def gather_batch(own):
    batches = lax.axis_size("batch")
    return [own] + [lax.ppermute(own, "batch", moved_by(k, batches)) for k in range(1, batches)]


def gather_chips_first(steps):
    heights, half = lax.axis_size("ha"), len(steps) // 2
    one, two = jnp.concatenate(steps[:half]), jnp.concatenate(steps[half:])
    one = jnp.concatenate([one, lax.ppermute(one, "ha", mirrored(1, heights))])
    two = jnp.concatenate([two, lax.ppermute(two, "ha", mirrored(2, heights))])
    return one, two


def gather_chips_second(one, two, beside):
    heights = lax.axis_size("ha")
    across = mirrored(1, 2)
    one_next = lax.ppermute(one, "ha", mirrored(2, heights))
    two_next = lax.ppermute(two, "ha", mirrored(1, heights))
    others = [lax.ppermute(one, "wa", across), lax.ppermute(two, "wa", across)]
    one_next, two_next, beside = together(one_next, two_next, beside)
    others = [
        others[0],
        lax.ppermute(one_next, "wa", across),
        others[1],
        lax.ppermute(two_next, "wa", across),
    ]
    return [one, one_next, two, two_next] + others, beside


def part_position(owner_ids, place):
    batches, heights, cores = (lax.axis_size(axis) for axis in AXES)
    z, h, w = place
    core = (owner_ids % cores) ^ w
    turn = (owner_ids // cores % heights) ^ h
    step = (z - owner_ids // (cores * heights)) % batches
    half = batches // 2
    swapped = jnp.where(turn == 1, 2, jnp.where(turn == 2, 1, turn))
    block = jnp.where(
        step < half, turn * half + step, heights * half + swapped * half + step - half
    )
    return core * batches * heights + block


def target_position(owner_ids, place):
    batches, heights, cores = (lax.axis_size(axis) for axis in AXES)
    z, h, w = place
    core = (owner_ids % cores) ^ w
    turn = (owner_ids // cores % heights) ^ h
    step = (owner_ids // (cores * heights) - z) % batches
    return (core * heights + turn) * batches + step


def add_low(a, b):
    return (a.astype(F32) + b.astype(F32)).astype(BF16)


def sum_cores(packed):
    heights = lax.axis_size("ha")
    rows = packed.shape[0] // (2 * heights)
    other = lax.ppermute(packed[heights * rows :], "wa", mirrored(1, 2))
    return add_low(packed[: heights * rows], other).reshape(heights, rows, LANES)


def sum_chips_first(both):
    heights, rows = both.shape[:2]
    half = rows // 2
    one, two = both[:, :half], both[:, half:]
    one_in = lax.ppermute(jnp.concatenate([one[1], one[3]]), "ha", mirrored(1, heights))
    two_in = lax.ppermute(jnp.concatenate([two[2], two[3]]), "ha", mirrored(2, heights))
    return [
        add_low(one[0], one_in[:half]),
        add_low(one[2], one_in[half:]),
        add_low(two[0], two_in[:half]),
        add_low(two[1], two_in[half:]),
    ]


def sum_chips_second(sums):
    one, one_out, two, two_out = sums
    heights, batches = lax.axis_size("ha"), lax.axis_size("batch")
    one_in = lax.ppermute(one_out, "ha", mirrored(2, heights))
    two_in = lax.ppermute(two_out, "ha", mirrored(1, heights))
    own = jnp.concatenate([add_low(one, one_in), add_low(two, two_in)])
    return own.reshape(batches, -1, LANES)


def sum_batch(own):
    batches = own.shape[0]
    total = own[0].astype(F32)
    for k in range(1, batches):
        total = total + lax.ppermute(own[k], "batch", moved_by(k, batches)).astype(F32)
    return total


def scatter_sums(packed):
    return sum_batch(sum_chips_second(sum_chips_first(sum_cores(packed))))


def together(*values):
    return lax.optimization_barrier(values)


def exchange(message):
    return lax.all_to_all(message, AXES, 0, 0, tiled=True)


def swap_edges(edges):
    top, bottom, side, corner_top, corner_bottom = edges
    count = lax.axis_size("ha")
    cores = lax.axis_size("wa")
    forward = [(i, i + 1) for i in range(count - 1)]
    backward = [(i + 1, i) for i in range(count - 1)]
    across = [(0, 1), (1, 0)]

    def both(moves):
        return [(a * cores + i, b * cores + j) for a, b in moves for i, j in across]

    up = lax.ppermute(bottom, "ha", forward)
    down = lax.ppermute(top, "ha", backward)
    corner_up = lax.ppermute(corner_bottom, ("ha", "wa"), both(forward))
    corner_down = lax.ppermute(corner_top, ("ha", "wa"), both(backward))
    beside = lax.ppermute(side, "wa", across)
    return [up, down, beside, corner_up, corner_down]


def per_device(
    block_input,
    cotangent,
    frame_sides,
    owner_list,
    master_slots,
    first_slots,
    second_slots,
    norm_gains,
    norm_biases,
    norm_first,
    norm_second,
):
    clip_count, frames, tile_rows, tile_cols, width = block_input.shape
    devices = lax.axis_size(AXES)
    slot_count, piece_len = master_slots.shape
    middle = norm_gains.shape[0] // 2 - width
    middle_pad = -(-middle // LANES) * LANES
    rows = clip_count * frames * tile_rows * tile_cols

    low_slots = master_slots.astype(BF16).reshape(slot_count * PIECE_ROWS, LANES)

    steps = gather_batch(low_slots)

    own_side = frame_sides[0]
    row_ids = lax.axis_index("ha") * tile_rows + jnp.arange(tile_rows, dtype=jnp.int32)
    col_ids = lax.axis_index("wa") * tile_cols + jnp.arange(tile_cols, dtype=jnp.int32)
    grid_rows = tile_rows * lax.axis_size("ha")
    grid_cols = tile_cols * lax.axis_size("wa")
    valid = (
        (row_ids[:, None] >= grid_rows - own_side) & (col_ids[None, :] >= grid_cols - own_side)
    ).astype(F32)
    valid_flat = valid.reshape(-1)
    place = lax.axis_index("wa").reshape(1)
    def to_tile(array):
        return jnp.transpose(array, (2, 3, 1, 0, 4)).reshape(tile_rows, tile_cols, CELL, width)

    x_tile = to_tile(block_input) * valid[:, :, None, None].astype(BF16)
    edge = jnp.where(place[0] == 0, tile_cols - 1, 0)
    x_side = lax.dynamic_index_in_dim(x_tile, edge, axis=1, keepdims=False)
    x_halo = swap_edges([x_tile[0], x_tile[-1], x_side, x_side[0], x_side[-1]])
    steps, x_tile, x_halo, cotangent, owner_list, norm_gains, norm_biases = together(
        steps, x_tile, x_halo, cotangent, owner_list, norm_gains, norm_biases
    )
    one, two = gather_chips_first(steps)

    cot_tile = to_tile(cotangent)
    owner_ids = owner_list[:, 0]
    ranking = ranks_of_pieces(owner_ids, devices)
    here = [lax.axis_index(axis) for axis in AXES]
    slot_index = part_position(owner_ids, here) * slot_count + ranking
    half = owner_list.shape[0] // 2
    kept = min(slot_count, int(slot_count / 2 + 1.83 * math.sqrt(slot_count)))
    target = target_position(owner_ids, here)
    all_slots = target * slot_count + ranking
    late_rank = ranking[half:] - (slot_count - kept)
    fits = jnp.all(ranking[:half] < kept) & jnp.all(late_rank >= 0)
    early_slots = jnp.where(fits, target[:half] * kept + ranking[:half], 0)
    late_slots = jnp.where(fits, target[half:] * kept + late_rank, 0)

    bounds = [0, middle, middle + width, 2 * middle + width, 2 * middle + 2 * width]
    gb = []
    for i in range(4):
        for vector in (norm_gains, norm_biases):
            part = vector[bounds[i] : bounds[i + 1]]
            gb.append(jnp.pad(part, (0, middle_pad - part.shape[0])))
    gb = jnp.stack(gb)

    prepared = (x_tile, x_halo, cot_tile, valid_flat, gb, slot_index, all_slots, early_slots, late_slots, fits)
    parts, prepared = gather_chips_second(one, two, prepared)
    x_tile, x_halo, cot_tile, valid_flat, gb, slot_index, all_slots, early_slots, late_slots, fits = prepared

    tap_rows = 9 * width
    stage = [pltpu.VMEM((UNROLL, 144, LANES), F32), pltpu.VMEM((UNROLL, 5, 32, LANES), F32)]
    weight_shapes = [((tap_rows, middle_pad), BF16), ((3 * middle_pad, width), BF16)]
    (all_weights,) = run(
        gather_weights_kernel,
        parts,
        [((devices * slot_count * PIECE_ROWS, LANES), BF16)],
        [pltpu.SemaphoreType.DMA((len(parts),))],
        us=3.0,
        spec=pl.BlockSpec(memory_space=pl.ANY),
    )

    def unpack(all_weights, unit):
        return run(
            unpack_weights_kernel,
            [slot_index, all_weights],
            weight_shapes,
            stage,
            1,
            4.3,
            base=unit * (owner_list.shape[0] // 2),
        )

    tile_shape = (tile_rows, tile_cols, CELL, width)
    padded_tile = (tile_rows + 2, tile_cols + 2, CELL, width)
    ds_shape = (tile_rows, tile_cols + 4, CELL, middle_pad)
    stats_mid = (devices, 1, 2 * middle_pad + LANES)
    stats_wide = (devices, 1, 2 * width + LANES)

    def edge_shapes(lanes):
        row, col = (tile_cols, CELL, lanes), (tile_rows, CELL, lanes)
        return [(row, BF16), (row, BF16), (col, BF16), ((CELL, lanes), BF16), ((CELL, lanes), BF16)]

    def unit_forward(tile, halo, ws, wt, index):
        padded, s, msg = run(
            spatial_kernel,
            [place, valid_flat, tile, *halo, ws],
            [(padded_tile, BF16), ((rows, middle_pad), F32), (stats_mid, F32)],
            us=5.5,
            scalars=2,
        )
        columns, t, s_stats, msg = run(
            temporal_kernel,
            [valid_flat, s, exchange(msg), gb, wt],
            [
                ((rows, 3 * middle_pad), BF16),
                ((rows, width), F32),
                ((8, middle_pad), F32),
                (stats_wide, F32),
            ],
            scalars=1,
            us=4.2,
            index=index,
        )
        return padded, s, s_stats, columns, t, exchange(msg)

    ws1, wt1 = unpack(all_weights, 0)
    padded1, s1, s_stats1, columns1, t1, msg = unit_forward(x_tile, x_halo, ws1, wt1, 0)
    t_stats1, y_tile, *edges = run(
        middle_kernel,
        [place, valid_flat, t1, msg, gb],
        [((8, width), F32), (tile_shape, BF16)] + edge_shapes(width),
        scalars=2,
        index=1,
    )
    edges, all_weights = together(edges, all_weights)
    halo = swap_edges(edges)
    ws2, wt2 = unpack(all_weights, 1)
    ws2, wt2, halo = together(ws2, wt2, halo)
    padded2, s2, s_stats2, columns2, t2, msg = unit_forward(y_tile, halo, ws2, wt2, 2)
    t_stats2, block_output, dpre, msg = run(
        top_kernel,
        [valid_flat, t2, msg, gb, x_tile.reshape(rows, width), cot_tile.reshape(rows, width)],
        [((8, width), F32), ((rows, width), F32), ((rows, width), F32), ((devices, 1, 2 * width), F32)],
        scalars=1,
        loose=(1,),
        index=3,
    )

    def unit_backward(e, msg, t, t_stats, s, s_stats, columns, padded, ws, wt, index, aside=None):
        dt, en, t_sums, msg = run(
            temporal_grad_kernel,
            [valid_flat, e, t, t_stats, exchange(msg), s, s_stats, gb, wt],
            [
                ((rows, width), BF16),
                ((rows, middle_pad), F32),
                ((2, width), F32),
                ((devices, 1, 2 * middle_pad), F32),
            ],
            [pltpu.VMEM((rows, 3 * width), BF16)],
            scalars=1,
            us=4.5,
            index=index,
        )
        if aside is not None:
            msg, aside = together(msg, sum_cores(aside))
        msg = exchange(msg)
        if aside is not None:
            msg, aside = together(msg, aside)
            aside = sum_chips_first(aside)
        s_sums, ds, *edges = run(
            ds_kernel,
            [place, valid_flat, en, s, s_stats, msg, gb, ws],
            [((2, middle_pad), F32), (ds_shape, BF16)] + edge_shapes(width),
            [pltpu.VMEM((tile_cols + 1, CELL, width), BF16)],
            scalars=2,
            us=4.0,
            index=index,
        )
        edges, columns, dt = together(edges, columns, dt)
        (wt_grad,) = run(temporal_weight_kernel, [columns, dt], [((3 * middle_pad, width), F32)], us=1.2)
        (ws_grad,) = run(spatial_weight_kernel, [padded, ds], [((tap_rows, middle_pad), F32)], us=4.0)
        (inner,) = run(spatial_grad_kernel, [ds, ws], [((rows, width), F32)], us=3.0)
        return inner, edges, (ws_grad, wt_grad), s_sums, t_sums, aside

    def pack(grads, positions, kept):
        (packed,) = run(
            pack_grads_kernel,
            [positions, *grads],
            [((devices * kept * PIECE_ROWS, LANES), BF16)],
            stage,
            scalars=1,
            us=5.0,
            loose=(0,),
        )
        return packed

    inner, edges, grads2, s_sums2, t_sums2, _ = unit_backward(
        dpre, msg, t2, t_stats2, s2, s_stats2, columns2, padded2, ws2, wt2, 2
    )
    halo = swap_edges(edges)
    packed2 = pack(grads2, late_slots, kept)
    inner, halo, packed2 = together(inner, halo, packed2)
    e1, msg = run(
        between_kernel,
        [place, valid_flat, inner, *halo, t1, t_stats1, gb],
        [((rows, width), F32), ((devices, 1, 2 * width), F32)],
        scalars=2,
        us=2.0,
        index=1,
    )
    inner, edges, grads1, s_sums1, t_sums1, first2 = unit_backward(
        e1, msg, t1, t_stats1, s1, s_stats1, columns1, padded1, ws1, wt1, 0, packed2
    )
    packed1, first2 = together(pack(grads1, early_slots, kept), first2)
    both1, edges = together(sum_cores(packed1), edges)
    halo = swap_edges(edges)
    first1, second2, halo, block_output = together(
        sum_chips_first(both1), sum_chips_second(first2), halo, block_output
    )
    sums2 = sum_batch(second2)
    sums1 = sum_batch(sum_chips_second(first1))
    (input_grad,) = run(
        input_grad_kernel,
        [place, valid_flat, inner, *halo, dpre],
        [((rows, width), F32)],
        scalars=2,
        us=2.0,
        loose=(0,),
    )

    def joined(early, late):
        rest = (slot_count - kept) * PIECE_ROWS
        return jnp.pad(early, ((0, rest), (0, 0))) + jnp.pad(late, ((rest, 0), (0, 0)))

    def whole(grads1, grads2):
        return scatter_sums(
            pack(grads1, all_slots[:half], slot_count) + pack(grads2, all_slots[half:], slot_count)
        )

    if kept == slot_count:
        grad_mine = joined(sums1, sums2)
    else:
        grad_mine = lax.cond(
            fits,
            lambda early, late, *_: joined(early, late),
            lambda early, late, ones, twos: whole(ones, twos),
            sums1,
            sums2,
            grads1,
            grads2,
        )

    def from_tile(array):
        array = array.reshape(tile_rows, tile_cols, frames, clip_count, width)
        return jnp.transpose(array, (3, 2, 0, 1, 4))

    grad_mine = grad_mine.reshape(slot_count, piece_len)
    correction = 1.0 - 0.5**STEP
    step_rate = 1.8 / math.sqrt(9.0 * width)
    first_new = 0.5 * first_slots + 0.5 * grad_mine
    second_new = 0.5 * second_slots + 0.5 * grad_mine * grad_mine
    master_new = master_slots - step_rate * (
        first_new / correction / (jnp.sqrt(second_new / correction) + ADAM_EPSILON)
        + DECAY_RATE * master_slots
    )
    weight_copy = master_new.astype(BF16)
    norm_grad = jnp.concatenate([s_sums1[:, :middle], t_sums1, s_sums2[:, :middle], t_sums2], axis=1)
    norm_pair = jnp.stack([norm_gains, norm_biases])
    norm_first_new = 0.5 * norm_first + 0.5 * norm_grad
    norm_second_new = 0.5 * norm_second + 0.5 * norm_grad * norm_grad
    norm_new = norm_pair - NORM_RATE * (norm_first_new / correction) / (
        jnp.sqrt(norm_second_new / correction) + ADAM_EPSILON
    )
    return (
        from_tile(block_output),
        from_tile(input_grad),
        master_new,
        first_new,
        second_new,
        weight_copy,
        norm_first_new,
        norm_second_new,
        norm_new,
    )


def solution(mesh):
    wide = P("batch", None, "ha", "wa", None)
    owned = P(AXES, None)
    return jax.shard_map(
        per_device,
        mesh=mesh,
        in_specs=(wide, wide, P("batch"), P(), owned, owned, owned, P(), P(), P(), P()),
        out_specs=(wide, wide, owned, owned, owned, owned, P(), P(), P()),
        check_vma=False,
    )
```

```python
import functools
import math

import jax
import jax.numpy as jnp
from jax import lax
from jax.experimental import pallas as pl
from jax.experimental.pallas import tpu as pltpu
from jax.sharding import PartitionSpec as P

STEP = 5
EPSILON = 1e-05
ADAM_EPSILON = 1e-08
DECAY_RATE = 0.1
NORM_RATE = 0.3

AXES = ("batch", "ha", "wa")
F32 = jnp.float32
BF16 = jnp.bfloat16
VMEM = pl.BlockSpec(memory_space=pltpu.VMEM)
SMEM = pl.BlockSpec(memory_space=pltpu.SMEM)
CELL = 64
LANES = 128
PIECE_ROWS = 16


def sigmoid(v):
    return 1.0 / (1.0 + jnp.exp(-v))


def cell_rows(index, count=1):
    return pl.ds(pl.multiple_of(index * CELL, CELL), count * CELL)


def block_rows(index, size):
    return pl.ds(pl.multiple_of(index * size, size), size)


def fold8(block):
    return jnp.sum(block.reshape(-1, 8, block.shape[-1]), axis=0)


def widen(lane_block, width):
    return jnp.concatenate([lane_block] * (width // LANES), axis=1)


def valid_rows(valid_ref, cells):
    total = valid_ref[0]
    for cell in range(1, cells):
        total = total + valid_ref[cell]
    return total * CELL


def send_stats(values_ref, valid_ref, msg_ref):
    rows, width = values_ref.shape
    cells = rows // CELL
    count = valid_rows(valid_ref, cells)

    def add(cell, total):
        return total + valid_ref[cell] * fold8(values_ref[cell_rows(cell), :])

    total = lax.fori_loop(0, cells, add, jnp.zeros((8, width), F32))
    total = jnp.sum(total, axis=0, keepdims=True)
    mean = total / jnp.maximum(jnp.full((1, width), count, F32), 1.0)

    def add_squares(cell, squares):
        centered = values_ref[cell_rows(cell), :] - mean
        return squares + valid_ref[cell] * fold8(centered * centered)

    squares = lax.fori_loop(0, cells, add_squares, jnp.zeros((8, width), F32))
    squares = jnp.sum(squares, axis=0, keepdims=True)
    message = jnp.concatenate([total, squares, jnp.full((1, LANES), count, F32)], axis=1)
    msg_ref[...] = jnp.broadcast_to(message[None], msg_ref.shape)


def receive_stats(msg_ref):
    devices, _, length = msg_ref.shape
    width = (length - LANES) // 2

    def add(i, carry):
        total, count = carry
        return (total + msg_ref[i, :, :width], count + msg_ref[i, :, 2 * width :])

    total, count = lax.fori_loop(
        0, devices, add, (jnp.zeros((1, width), F32), jnp.zeros((1, LANES), F32)), unroll=4
    )
    count = widen(count, width)
    mean = total / count

    def add_squares(i, squares):
        own = widen(msg_ref[i, :, 2 * width :], width)
        offset = msg_ref[i, :, :width] / jnp.maximum(own, 1.0) - mean
        return squares + msg_ref[i, :, width : 2 * width] + own * offset * offset

    squares = lax.fori_loop(0, devices, add_squares, jnp.zeros((1, width), F32), unroll=4)
    return mean, lax.rsqrt(squares / count + EPSILON), count


def keep_stats(stats_ref, mean, rstd, count):
    stats_ref[0:1, :] = mean
    stats_ref[1:2, :] = rstd
    stats_ref[2:3, :] = count


def receive_sums(msg_ref):
    devices, _, length = msg_ref.shape
    total = lax.fori_loop(
        0, devices, lambda i, t: t + msg_ref[i], jnp.zeros((1, length), F32), unroll=4
    )
    return total[:, : length // 2], total[:, length // 2 :]


def send_sums(bias, gain, msg_ref):
    message = jnp.concatenate(
        [jnp.sum(bias, axis=0, keepdims=True), jnp.sum(gain, axis=0, keepdims=True)], axis=1
    )
    msg_ref[...] = jnp.broadcast_to(message[None], msg_ref.shape)


def later_frame(block):
    return jnp.concatenate([block[8:], jnp.zeros((8, block.shape[1]), block.dtype)], axis=0)


def earlier_frame(block):
    return jnp.concatenate([jnp.zeros((8, block.shape[1]), block.dtype), block[:-8]], axis=0)


UNROLL = 4


def gather_weights_kernel(*refs):
    parts, all_ref, sems = refs[:-2], refs[-2], refs[-1]
    rows = parts[0].shape[0]
    copies = [
        pltpu.make_async_copy(part, all_ref.at[i * rows : (i + 1) * rows, :], sems.at[i])
        for i, part in enumerate(parts)
    ]
    for copy in copies:
        copy.start()
    for copy in copies:
        copy.wait()


def unpack_weights_kernel(slot_ref, all_ref, ws_ref, wt_ref, stage, turn, *, base):
    low = lax.broadcasted_iota(jnp.int32, (8, LANES), 1) < 64
    zero = jnp.zeros((8, LANES), F32)
    spatial_groups = ws_ref.shape[0] // 32

    def load_piece(number):
        start = pl.multiple_of(slot_ref[number] * PIECE_ROWS, PIECE_ROWS)
        return all_ref[pl.ds(start, PIECE_ROWS), :].astype(F32)

    def spatial_groups_at(k, _):
        first = k * UNROLL
        for u in range(UNROLL):
            for q in range(9):
                stage[u, 16 * q : 16 * q + 16, :] = load_piece(base + 9 * (first + u) + q)
        for u in range(UNROLL):
            for i in range(2):
                a = [stage[u, pl.ds(72 * i + j, 8, stride=9), :] for j in range(9)]
                r = [pltpu.roll(a[4 + j], 64, axis=1) for j in range(5)]
                even = a[:4] + [jnp.where(low, a[4], zero)]
                odd = [jnp.where(low, r[j], r[j + 1]) for j in range(4)]
                odd += [jnp.where(low, r[4], zero)]
                for j in range(5):
                    turn[u, j, pl.ds(16 * i, 8, stride=2), :] = even[j]
                    turn[u, j, pl.ds(16 * i + 1, 8, stride=2), :] = odd[j]
        for u in range(UNROLL):
            rows = block_rows(first + u, 32)
            for j in range(5):
                ws_ref[rows, LANES * j : LANES * (j + 1)] = turn[u, j].astype(BF16)
        return 0

    lax.fori_loop(0, spatial_groups // UNROLL, spatial_groups_at, 0)
    temporal_base = base + 9 * spatial_groups
    padded = wt_ref.shape[0] // 3
    pairs = (9 * spatial_groups) // 3 // 6
    for tap in range(3):

        def temporal_pairs(k, _):
            for u in range(UNROLL):
                first = temporal_base + tap * 2 * pairs + 2 * (k * UNROLL + u)
                stage[u, 0:16, :] = load_piece(first)
                stage[u, 16:32, :] = load_piece(first + 1)
            for u in range(UNROLL):
                start = tap * padded + (k * UNROLL + u) * 16
                rows = pl.ds(pl.multiple_of(start, 16), 16)
                for h in range(2):
                    half = stage[u, pl.ds(h, 16, stride=2), :]
                    wt_ref[rows, LANES * h : LANES * (h + 1)] = half.astype(BF16)
            return 0

        lax.fori_loop(0, pairs // UNROLL, temporal_pairs, 0)
        wt_ref[tap * padded + 16 * pairs : (tap + 1) * padded, :] = jnp.zeros(
            (padded - 16 * pairs, wt_ref.shape[1]), BF16
        )


def pack_grads_kernel(sent_at, kept_at, spatial, temporal, sent_ref, kept_ref, stage, turn):
    low = lax.broadcasted_iota(jnp.int32, (8, LANES), 1) < 64
    spatial_groups = spatial.shape[0] // 32
    padded = temporal.shape[0] // 3
    pairs = (9 * spatial_groups) // 3 // 6

    def clear(i, _):
        for out_ref in (sent_ref, kept_ref):
            out_ref[block_rows(i, 128), :] = jnp.zeros((128, LANES), BF16)
        return 0

    lax.fori_loop(0, sent_ref.shape[0] // 128, clear, 0)

    def store_piece(number, rows16):
        low_rows = rows16.astype(BF16)
        for out_ref, at in ((sent_ref, sent_at), (kept_ref, kept_at)):
            start = pl.multiple_of(at[number] * PIECE_ROWS, PIECE_ROWS)
            out_ref[pl.ds(start, PIECE_ROWS), :] = low_rows

    def spatial_groups_at(k, _):
        first = k * UNROLL
        for u in range(UNROLL):
            rows = block_rows(first + u, 32)
            for j in range(5):
                turn[u, j] = spatial[rows, LANES * j : LANES * (j + 1)]
        for u in range(UNROLL):
            for i in range(2):
                even = [turn[u, j, pl.ds(16 * i, 8, stride=2), :] for j in range(5)]
                odd = [turn[u, j, pl.ds(16 * i + 1, 8, stride=2), :] for j in range(5)]
                r = [pltpu.roll(odd[j], 64, axis=1) for j in range(5)]
                flat = even[:4] + [jnp.where(low, even[4], r[0])]
                flat += [jnp.where(low, r[j], r[j + 1]) for j in range(4)]
                for j in range(9):
                    stage[u, pl.ds(72 * i + j, 8, stride=9), :] = flat[j]
        for u in range(UNROLL):
            for q in range(9):
                store_piece(9 * (first + u) + q, stage[u, 16 * q : 16 * q + 16, :])
        return 0

    lax.fori_loop(0, spatial_groups // UNROLL, spatial_groups_at, 0)
    base = 9 * spatial_groups
    for tap in range(3):

        def temporal_pairs(k, _):
            for u in range(UNROLL):
                start = tap * padded + (k * UNROLL + u) * 16
                rows = pl.ds(pl.multiple_of(start, 16), 16)
                for h in range(2):
                    stage[u, pl.ds(h, 16, stride=2), :] = temporal[
                        rows, LANES * h : LANES * (h + 1)
                    ]
            for u in range(UNROLL):
                first = base + tap * 2 * pairs + 2 * (k * UNROLL + u)
                store_piece(first, stage[u, 0:16, :])
                store_piece(first + 1, stage[u, 16:32, :])
            return 0

        lax.fori_loop(0, pairs // UNROLL, temporal_pairs, 0)


def fill_padded(place_ref, padded_ref, tile_ref, halo_refs):
    up, down, side = halo_refs
    rows, cols = tile_ref.shape[:2]
    padded_ref[1 : rows + 1, 1 : cols + 1] = tile_ref[...]
    padded_ref[0, 1 : cols + 1] = up[:cols]
    padded_ref[rows + 1, 1 : cols + 1] = down[:cols]
    for core in range(2):
        near, far = (cols + 1, 0) if core == 0 else (0, cols + 1)

        @pl.when(place_ref[0] == core)
        def _():
            padded_ref[1 : rows + 1, near] = side[...]
            padded_ref[0, near] = up[cols]
            padded_ref[rows + 1, near] = down[cols]
            padded_ref[:, far] = jnp.zeros((rows + 2,) + tile_ref.shape[2:], BF16)


def write_edges(place_ref, tile_ref, edge_refs):
    top, bottom, side = edge_refs
    rows, cols = tile_ref.shape[:2]
    top[...] = tile_ref[0]
    bottom[...] = tile_ref[rows - 1]
    side[...] = tile_ref[:, jnp.where(place_ref[0] == 0, cols - 1, 0)]


def spatial_kernel(
    place_ref, valid_ref, tile_ref, up, down, side, ws_ref, padded_ref, s_ref, msg_ref
):
    rows, cols, cell, width = tile_ref.shape
    fill_padded(place_ref, padded_ref, tile_ref, (up, down, side))

    def one_row(r, _):
        windows = []
        for row_tap in range(3):
            for col_tap in range(3):
                window = padded_ref[r + row_tap, col_tap : col_tap + cols]
                windows.append(window.reshape(cols * cell, width))
        s_ref[block_rows(r, cols * cell), :] = jnp.dot(
            jnp.concatenate(windows, axis=1), ws_ref[...], preferred_element_type=F32
        )
        return 0

    lax.fori_loop(0, rows, one_row, 0)
    send_stats(s_ref, valid_ref, msg_ref)


def weight_back(window, ws_ref, tap, width):
    return lax.dot_general(
        window.reshape(-1, window.shape[-1]),
        ws_ref[block_rows(tap, width), :],
        (((1,), (1,)), ((), ())),
        preferred_element_type=F32,
    )


def edge_grads(place_ref, ds_ref, ws_ref, edge_refs, row_ref):
    top, bottom, side = edge_refs
    width = top.shape[-1]
    cols, cell = top.shape[:2]
    rows = side.shape[0] - 2
    core = place_ref[0]
    for row, row_tap, out, corner in ((0, 0, top, 0), (rows - 1, 2, bottom, rows + 1)):
        total = None
        for col_tap in range(3):
            window = ds_ref[row, pl.ds(3 - core - col_tap, cols + 1)]
            term = weight_back(window, ws_ref, 3 * row_tap + col_tap, width)
            total = term if total is None else total + term
        row_ref[...] = total.astype(BF16).reshape(row_ref.shape)
        out[...] = row_ref[pl.ds(core, cols)]
        side[corner] = row_ref[cols * (1 - core)]
    column = ds_ref[:, jnp.where(core == 0, cols + 1, 2)]
    above, level, below = [
        weight_back(column, ws_ref, 3 * row_tap + 2 - 2 * core, width) for row_tap in range(3)
    ]
    empty = jnp.zeros((cell, width), F32)
    total = level + jnp.concatenate([above[cell:], empty]) + jnp.concatenate([empty, below[:-cell]])
    side[1 : rows + 1] = total.astype(BF16).reshape(rows, cell, width)


def spatial_grad_kernel(ds_ref, ws_ref, grad_ref):
    rows, cols, cell = ds_ref.shape[0], ds_ref.shape[1] - 4, ds_ref.shape[2]
    width = grad_ref.shape[1]
    for row in range(rows):
        total = None
        for row_tap in range(3):
            if not 0 <= row + 1 - row_tap < rows:
                continue
            for col_tap in range(3):
                window = ds_ref[row + 1 - row_tap, 3 - col_tap : 3 - col_tap + cols]
                term = weight_back(window, ws_ref, 3 * row_tap + col_tap, width)
                total = term if total is None else total + term
        grad_ref[row * cols * cell : (row + 1) * cols * cell, :] = total


def add_halo(place_ref, grad_ref, out_ref, halo_refs):
    up, down, side = halo_refs
    rows, cols = side.shape[0] - 2, up.shape[0]
    edge = jnp.where(place_ref[0] == 0, cols - 1, 0)
    out_ref[...] = grad_ref[...]
    last = (rows - 1) * cols
    for c in range(cols):
        out_ref[cell_rows(c), :] += up[c].astype(F32)
        out_ref[cell_rows(last + c), :] += down[c].astype(F32)
    for r in range(rows):
        out_ref[cell_rows(r * cols + edge), :] += side[r + 1].astype(F32)


def spatial_weight_kernel(padded_ref, ds_ref, grad_ref):
    rows, cols, cell, middle = ds_ref.shape
    cols = cols - 4
    width = padded_ref.shape[-1]
    grads = ds_ref[:, 2 : cols + 2].reshape(rows * cols * cell, middle)
    for row_tap in range(3):
        for col_tap in range(3):
            window = padded_ref[row_tap : row_tap + rows, col_tap : col_tap + cols]
            tap = 3 * row_tap + col_tap
            grad_ref[tap * width : (tap + 1) * width, :] = lax.dot_general(
                window.reshape(rows * cols * cell, width),
                grads,
                (((0,), (0,)), ((), ())),
                preferred_element_type=F32,
            )


def between_kernel(
    place_ref, valid_ref, grad_ref, up, down, side, t_ref, stats_ref, gb_ref,
    e_ref, msg_ref, *, index,
):
    rows, width = e_ref.shape
    add_halo(place_ref, grad_ref, e_ref, (up, down, side))
    mean, rstd = stats_ref[0:1, :], stats_ref[1:2, :]
    gain, bias = gb_ref[2 * index : 2 * index + 1, :width], gb_ref[2 * index + 1 : 2 * index + 2, :width]

    def one_cell(c, carry):
        bias_sum, gain_sum = carry
        normal = (t_ref[cell_rows(c), :] - mean) * rstd
        value = normal * gain + bias
        sigma = sigmoid(value)
        e = e_ref[cell_rows(c), :] * valid_ref[c] * (sigma * (1.0 + value * (1.0 - sigma)))
        e_ref[cell_rows(c), :] = e
        return (bias_sum + fold8(e), gain_sum + fold8(e * normal))

    start = jnp.zeros((8, width), F32)
    bias_sum, gain_sum = lax.fori_loop(0, rows // CELL, one_cell, (start, start))
    send_sums(bias_sum, gain_sum, msg_ref)


def input_grad_kernel(
    place_ref, valid_ref, grad_ref, up, down, side, dpre_ref, out_ref
):
    add_halo(place_ref, grad_ref, out_ref, (up, down, side))

    def one_cell(c, carry):
        rows = cell_rows(c)
        out_ref[rows, :] = (out_ref[rows, :] + dpre_ref[rows, :]) * valid_ref[c]
        return carry

    lax.fori_loop(0, out_ref.shape[0] // CELL, one_cell, 0)


def temporal_kernel(
    valid_ref, s_ref, msg_ref, gb_ref, wt_ref, columns_ref, t_ref, stats_ref, out_ref, *, index
):
    rows, middle = s_ref.shape
    mean, rstd, count = receive_stats(msg_ref)
    keep_stats(stats_ref, mean, rstd, count)
    gain, bias = gb_ref[2 * index : 2 * index + 1, :], gb_ref[2 * index + 1 : 2 * index + 2, :]

    def one_cell(c, _):
        value = (s_ref[cell_rows(c), :] - mean) * rstd * gain + bias
        inner = value * sigmoid(value) * valid_ref[c]
        columns_ref[cell_rows(c), 0:middle] = earlier_frame(inner).astype(BF16)
        columns_ref[cell_rows(c), middle : 2 * middle] = inner.astype(BF16)
        columns_ref[cell_rows(c), 2 * middle : 3 * middle] = later_frame(inner).astype(BF16)
        return 0

    lax.fori_loop(0, rows // CELL, one_cell, 0)

    def one_block(i, _):
        t_ref[block_rows(i, 320), :] = jnp.dot(
            columns_ref[block_rows(i, 320), :], wt_ref[...], preferred_element_type=F32
        )
        return 0

    lax.fori_loop(0, rows // 320, one_block, 0)
    send_stats(t_ref, valid_ref, out_ref)


def middle_kernel(
    place_ref, valid_ref, t_ref, msg_ref, gb_ref, stats_ref, tile_ref, top, bottom, side, *, index,
):
    width = t_ref.shape[1]
    rows, cols = tile_ref.shape[:2]
    mean, rstd, count = receive_stats(msg_ref)
    keep_stats(stats_ref, mean, rstd, count)
    gain, bias = gb_ref[2 * index : 2 * index + 1, :width], gb_ref[2 * index + 1 : 2 * index + 2, :width]
    for r in range(rows):
        for c in range(cols):
            number = r * cols + c
            value = (t_ref[number * CELL : (number + 1) * CELL, :] - mean) * rstd * gain + bias
            tile_ref[r, c] = (value * sigmoid(value) * valid_ref[number]).astype(BF16)
    write_edges(place_ref, tile_ref, (top, bottom, side))


def top_kernel(
    valid_ref, t_ref, msg_ref, gb_ref, x_ref, cot_ref, stats_ref, out_ref, dpre_ref, msg_out, *, index
):
    rows, width = t_ref.shape
    mean, rstd, count = receive_stats(msg_ref)
    keep_stats(stats_ref, mean, rstd, count)
    gain, bias = gb_ref[2 * index : 2 * index + 1, :width], gb_ref[2 * index + 1 : 2 * index + 2, :width]

    def one_cell(c, carry):
        bias_sum, gain_sum = carry
        normal = (t_ref[cell_rows(c), :] - mean) * rstd
        pre = normal * gain + bias + x_ref[cell_rows(c), :].astype(F32)
        sigma = sigmoid(pre)
        valid = valid_ref[c]
        out_ref[cell_rows(c), :] = pre * sigma * valid
        dpre = cot_ref[cell_rows(c), :].astype(F32) * valid * (sigma * (1.0 + pre * (1.0 - sigma)))
        dpre_ref[cell_rows(c), :] = dpre
        return (bias_sum + fold8(dpre), gain_sum + fold8(dpre * normal))

    start = jnp.zeros((8, width), F32)
    bias_sum, gain_sum = lax.fori_loop(0, rows // CELL, one_cell, (start, start))
    send_sums(bias_sum, gain_sum, msg_out)


def temporal_grad_kernel(
    valid_ref, e_ref, t_ref, tstats_ref, msg_ref, s_ref, sstats_ref, gb_ref, wt_ref,
    dt_ref, en_ref, sums_ref, msg_out, columns_ref, *, index,
):
    rows, width = e_ref.shape
    middle = s_ref.shape[1]
    bias_grad, gain_grad = receive_sums(msg_ref)
    sums_ref[0:1, :] = gain_grad
    sums_ref[1:2, :] = bias_grad
    mean, rstd, count = tstats_ref[0:1, :], tstats_ref[1:2, :], tstats_ref[2:3, :]
    gain = gb_ref[2 * index + 2 : 2 * index + 3, :width]

    def one_cell(c, _):
        normal = (t_ref[cell_rows(c), :] - mean) * rstd
        dt = (rstd * gain) * (
            e_ref[cell_rows(c), :] - valid_ref[c] * ((bias_grad + normal * gain_grad) / count)
        )
        dt_ref[cell_rows(c), :] = dt.astype(BF16)
        columns_ref[cell_rows(c), 0:width] = later_frame(dt).astype(BF16)
        columns_ref[cell_rows(c), width : 2 * width] = dt.astype(BF16)
        columns_ref[cell_rows(c), 2 * width : 3 * width] = earlier_frame(dt).astype(BF16)
        return 0

    lax.fori_loop(0, rows // CELL, one_cell, 0)

    def one_block(i, _):
        total = None
        for tap in range(3):
            term = lax.dot_general(
                columns_ref[block_rows(i, 320), tap * width : (tap + 1) * width],
                wt_ref[tap * middle : (tap + 1) * middle, :],
                (((1,), (1,)), ((), ())),
                preferred_element_type=F32,
            )
            total = term if total is None else total + term
        en_ref[block_rows(i, 320), :] = total
        return 0

    lax.fori_loop(0, rows // 320, one_block, 0)
    mean_s, rstd_s = sstats_ref[0:1, :], sstats_ref[1:2, :]
    gain_s, bias_s = gb_ref[2 * index : 2 * index + 1, :], gb_ref[2 * index + 1 : 2 * index + 2, :]

    def one_mid_cell(c, carry):
        bias_sum, gain_sum = carry
        normal = (s_ref[cell_rows(c), :] - mean_s) * rstd_s
        value = normal * gain_s + bias_s
        sigma = sigmoid(value)
        e = en_ref[cell_rows(c), :] * valid_ref[c] * (sigma * (1.0 + value * (1.0 - sigma)))
        en_ref[cell_rows(c), :] = e
        return (bias_sum + fold8(e), gain_sum + fold8(e * normal))

    start = jnp.zeros((8, middle), F32)
    bias_sum, gain_sum = lax.fori_loop(0, rows // CELL, one_mid_cell, (start, start))
    send_sums(bias_sum, gain_sum, msg_out)


def temporal_weight_kernel(columns_ref, dt_ref, grad_ref):
    middle = columns_ref.shape[1] // 3
    for tap in range(3):
        grad_ref[tap * middle : (tap + 1) * middle, :] = lax.dot_general(
            columns_ref[:, tap * middle : (tap + 1) * middle],
            dt_ref[...],
            (((0,), (0,)), ((), ())),
            preferred_element_type=F32,
        )


def ds_kernel(
    place_ref, valid_ref, en_ref, s_ref, stats_ref, msg_ref, gb_ref, ws_ref,
    sums_ref, ds_ref, top, bottom, side, row_ref, *, index,
):
    rows, cols = ds_ref.shape[0], ds_ref.shape[1] - 4
    bias_grad, gain_grad = receive_sums(msg_ref)
    sums_ref[0:1, :] = gain_grad
    sums_ref[1:2, :] = bias_grad
    mean, rstd, count = stats_ref[0:1, :], stats_ref[1:2, :], stats_ref[2:3, :]
    scale = rstd * gb_ref[2 * index : 2 * index + 1, :]
    for r in range(rows):
        for c in (0, 1, cols + 2, cols + 3):
            ds_ref[r, c] = jnp.zeros(ds_ref.shape[2:], BF16)
        for c in range(cols):
            number = r * cols + c
            block = slice(number * CELL, (number + 1) * CELL)
            normal = (s_ref[block, :] - mean) * rstd
            ds_ref[r, c + 2] = (
                scale
                * (en_ref[block, :] - valid_ref[number] * ((bias_grad + normal * gain_grad) / count))
            ).astype(BF16)
    edge_grads(place_ref, ds_ref, ws_ref, (top, bottom, side), row_ref)


def run(kernel, ins, outs, scratch=(), scalars=0, us=1.0, extra=8, loose=(), spec=VMEM, **settings):
    held = sum(
        math.prod(x.shape) * jnp.dtype(x.dtype).itemsize
        for x in scratch
        if x.memory_space == pltpu.VMEM
    )
    return pl.pallas_call(
        functools.partial(kernel, **settings),
        out_shape=[
            jax.ShapeDtypeStruct(shape, dtype) if i in loose else pltpu.VMEM(shape, dtype)
            for i, (shape, dtype) in enumerate(outs)
        ],
        in_specs=[SMEM] * scalars + [spec] * (len(ins) - scalars),
        out_specs=[VMEM] * len(outs),
        scratch_shapes=list(scratch),
        cost_estimate=pl.CostEstimate(
            flops=int(us * 1.1e9), bytes_accessed=1000, transcendentals=0
        ),
        compiler_params=pltpu.CompilerParams(vmem_limit_bytes=held + extra * 2**20),
    )(*ins)


def ranks_of_pieces(owner_ids, devices):
    block = 64
    onehot = (owner_ids.reshape(-1, block, 1) == jnp.arange(devices, dtype=jnp.int32)).astype(BF16)
    earlier = jnp.tril(jnp.ones((block, block), BF16), -1)
    within = jnp.einsum("ij,bjd->bid", earlier, onehot, preferred_element_type=F32)
    sums = jnp.sum(onehot.astype(F32), axis=1)
    blocks = jnp.tril(jnp.ones((sums.shape[0],) * 2, F32), -1)
    before = jnp.sum(blocks[:, :, None] * sums[None], axis=1)
    ranking = jnp.sum(onehot.astype(F32) * (within + before[:, None, :]), axis=-1)
    return ranking.reshape(-1).astype(jnp.int32)


def moved_by(step, size):
    return [(i, (i + step) % size) for i in range(size)]


def mirrored(bit, size):
    return [(i, i ^ bit) for i in range(size)]


def gather_batch(own):
    batches = lax.axis_size("batch")
    return [own] + [lax.ppermute(own, "batch", moved_by(k, batches)) for k in range(1, batches)]


def gather_chips_first(steps):
    heights, half = lax.axis_size("ha"), len(steps) // 2
    one, two = jnp.concatenate(steps[:half]), jnp.concatenate(steps[half:])
    one = jnp.concatenate([one, lax.ppermute(one, "ha", mirrored(1, heights))])
    two = jnp.concatenate([two, lax.ppermute(two, "ha", mirrored(2, heights))])
    return one, two


def gather_chips_second(one, two, beside):
    heights = lax.axis_size("ha")
    across = mirrored(1, 2)
    one_next = lax.ppermute(one, "ha", mirrored(2, heights))
    two_next = lax.ppermute(two, "ha", mirrored(1, heights))
    others = [lax.ppermute(one, "wa", across), lax.ppermute(two, "wa", across)]
    one_next, two_next, beside = together(one_next, two_next, beside)
    others = [
        others[0],
        lax.ppermute(one_next, "wa", across),
        others[1],
        lax.ppermute(two_next, "wa", across),
    ]
    return [one, one_next, two, two_next] + others, beside


def part_position(owner_ids, place):
    batches, heights, cores = (lax.axis_size(axis) for axis in AXES)
    z, h, w = place
    core = (owner_ids % cores) ^ w
    turn = (owner_ids // cores % heights) ^ h
    step = (z - owner_ids // (cores * heights)) % batches
    half = batches // 2
    swapped = jnp.where(turn == 1, 2, jnp.where(turn == 2, 1, turn))
    block = jnp.where(
        step < half, turn * half + step, heights * half + swapped * half + step - half
    )
    return core * batches * heights + block


def target_position(owner_ids, place):
    batches, heights, cores = (lax.axis_size(axis) for axis in AXES)
    z, h, w = place
    core = (owner_ids % cores) ^ w
    turn = (owner_ids // cores % heights) ^ h
    step = (owner_ids // (cores * heights) - z) % batches
    return (core * heights + turn) * batches + step


def add_low(a, b):
    return (a.astype(F32) + b.astype(F32)).astype(BF16)


def sum_cores(packed):
    sent, kept = packed
    return [kept, lax.ppermute(sent, "wa", mirrored(1, 2))]


def sum_chips_first(terms, rows):
    heights, half = lax.axis_size("ha"), rows // 2

    def added(block, part):
        start = block * rows + part * half
        return add_low(*[t[start : start + half] for t in terms])

    one_in = lax.ppermute(jnp.stack([added(1, 0), added(3, 0)]), "ha", mirrored(1, heights))
    two_in = lax.ppermute(jnp.stack([added(2, 1), added(3, 1)]), "ha", mirrored(2, heights))
    return [
        add_low(added(0, 0), one_in[0]),
        add_low(added(2, 0), one_in[1]),
        add_low(added(0, 1), two_in[0]),
        add_low(added(1, 1), two_in[1]),
    ]


def sum_chips_second(sums):
    one, one_out, two, two_out = sums
    heights, batches = lax.axis_size("ha"), lax.axis_size("batch")
    one_in = lax.ppermute(one_out, "ha", mirrored(2, heights))
    two_in = lax.ppermute(two_out, "ha", mirrored(1, heights))
    own = jnp.concatenate([add_low(one, one_in), add_low(two, two_in)])
    return own.reshape(batches, -1, LANES)


def sum_batch(own):
    batches = own.shape[0]
    total = own[0].astype(F32)
    for k in range(1, batches):
        total = total + lax.ppermute(own[k], "batch", moved_by(k, batches)).astype(F32)
    return total


def scatter_sums(packed, rows):
    return sum_batch(sum_chips_second(sum_chips_first(sum_cores(packed), rows)))


def together(*values):
    return lax.optimization_barrier(values)


def exchange(message):
    return lax.all_to_all(message, AXES, 0, 0, tiled=True)


def swap_side(side):
    return lax.ppermute(side, "wa", mirrored(1, 2))


def swap_rows(top, bottom):
    count = lax.axis_size("ha")
    forward = [(i, i + 1) for i in range(count - 1)]
    backward = [(i + 1, i) for i in range(count - 1)]
    return [lax.ppermute(bottom, "ha", forward), lax.ppermute(top, "ha", backward)]


def swap_values(edges, side):
    top, bottom, _ = edges
    rows = swap_rows(
        jnp.concatenate([top, side[:1]]), jnp.concatenate([bottom, side[-1:]])
    )
    return rows + [side]


def with_ends(at_edge, edges, side):
    top, bottom, _ = edges
    return [
        jnp.where(at_edge[:, None, None], add_low(row, side[end][None]), row)
        for row, end in ((top, 0), (bottom, -1))
    ]


def per_device(
    block_input,
    cotangent,
    frame_sides,
    owner_list,
    master_slots,
    first_slots,
    second_slots,
    norm_gains,
    norm_biases,
    norm_first,
    norm_second,
):
    clip_count, frames, tile_rows, tile_cols, width = block_input.shape
    devices = lax.axis_size(AXES)
    slot_count, piece_len = master_slots.shape
    middle = norm_gains.shape[0] // 2 - width
    middle_pad = -(-middle // LANES) * LANES
    rows = clip_count * frames * tile_rows * tile_cols

    low_slots = master_slots.astype(BF16).reshape(slot_count * PIECE_ROWS, LANES)

    steps = gather_batch(low_slots)

    own_side = frame_sides[0]
    row_ids = lax.axis_index("ha") * tile_rows + jnp.arange(tile_rows, dtype=jnp.int32)
    col_ids = lax.axis_index("wa") * tile_cols + jnp.arange(tile_cols, dtype=jnp.int32)
    grid_rows = tile_rows * lax.axis_size("ha")
    grid_cols = tile_cols * lax.axis_size("wa")
    valid = (
        (row_ids[:, None] >= grid_rows - own_side) & (col_ids[None, :] >= grid_cols - own_side)
    ).astype(F32)
    valid_flat = valid.reshape(-1)
    place = lax.axis_index("wa").reshape(1)
    def to_tile(array):
        return jnp.transpose(array, (2, 3, 1, 0, 4)).reshape(tile_rows, tile_cols, CELL, width)

    x_tile = to_tile(block_input) * valid[:, :, None, None].astype(BF16)
    edge = jnp.where(place[0] == 0, tile_cols - 1, 0)
    x_side = lax.dynamic_index_in_dim(x_tile, edge, axis=1, keepdims=False)
    x_halo = swap_values((x_tile[0], x_tile[-1], x_side), swap_side(x_side))
    steps, x_tile, x_halo, cotangent, owner_list, norm_gains, norm_biases = together(
        steps, x_tile, x_halo, cotangent, owner_list, norm_gains, norm_biases
    )
    one, two = gather_chips_first(steps)

    cot_tile = to_tile(cotangent)
    owner_ids = owner_list[:, 0]
    ranking = ranks_of_pieces(owner_ids, devices)
    here = [lax.axis_index(axis) for axis in AXES]
    slot_index = part_position(owner_ids, here) * slot_count + ranking
    half = owner_list.shape[0] // 2
    kept = min(slot_count, int(slot_count / 2 + 1.83 * math.sqrt(slot_count)))
    target = target_position(owner_ids, here)
    all_slots = target * slot_count + ranking
    late_rank = ranking[half:] - (slot_count - kept)
    fits = jnp.all(ranking[:half] < kept) & jnp.all(late_rank >= 0)

    def by_core(positions, kept):
        here = devices // 2 * kept
        sent_at = jnp.where(positions >= here, positions - here, here)
        return sent_at, jnp.where(positions < here, positions, here)

    def spare_rows(kept):
        return -(-(devices // 2 * kept + 1) * PIECE_ROWS // 128) * 128

    early_slots = by_core(jnp.where(fits, target[:half] * kept + ranking[:half], 0), kept)
    late_slots = by_core(jnp.where(fits, target[half:] * kept + late_rank, 0), kept)

    bounds = [0, middle, middle + width, 2 * middle + width, 2 * middle + 2 * width]
    gb = []
    for i in range(4):
        for vector in (norm_gains, norm_biases):
            part = vector[bounds[i] : bounds[i + 1]]
            gb.append(jnp.pad(part, (0, middle_pad - part.shape[0])))
    gb = jnp.stack(gb)

    at_edge = jnp.arange(tile_cols) == edge
    prepared = (at_edge, x_tile, x_halo, cot_tile, valid_flat, gb, slot_index, all_slots, early_slots, late_slots, fits)
    parts, prepared = gather_chips_second(one, two, prepared)
    at_edge, x_tile, x_halo, cot_tile, valid_flat, gb, slot_index, all_slots, early_slots, late_slots, fits = prepared

    tap_rows = 9 * width
    stage = [pltpu.VMEM((UNROLL, 144, LANES), F32), pltpu.VMEM((UNROLL, 5, 32, LANES), F32)]
    weight_shapes = [((tap_rows, middle_pad), BF16), ((3 * middle_pad, width), BF16)]
    (all_weights,) = run(
        gather_weights_kernel,
        parts,
        [((devices * slot_count * PIECE_ROWS, LANES), BF16)],
        [pltpu.SemaphoreType.DMA((len(parts),))],
        us=3.0,
        spec=pl.BlockSpec(memory_space=pl.ANY),
    )

    def unpack(all_weights, unit):
        return run(
            unpack_weights_kernel,
            [slot_index, all_weights],
            weight_shapes,
            stage,
            1,
            4.3,
            base=unit * (owner_list.shape[0] // 2),
        )

    tile_shape = (tile_rows, tile_cols, CELL, width)
    padded_tile = (tile_rows + 2, tile_cols + 2, CELL, width)
    ds_shape = (tile_rows, tile_cols + 4, CELL, middle_pad)
    stats_mid = (devices, 1, 2 * middle_pad + LANES)
    stats_wide = (devices, 1, 2 * width + LANES)

    def edge_shapes(lanes, beside=0):
        row, col = (tile_cols, CELL, lanes), (tile_rows + beside, CELL, lanes)
        return [(row, BF16), (row, BF16), (col, BF16)]

    def unit_forward(tile, halo, ws, wt, index):
        padded, s, msg = run(
            spatial_kernel,
            [place, valid_flat, tile, *halo, ws],
            [(padded_tile, BF16), ((rows, middle_pad), F32), (stats_mid, F32)],
            us=5.5,
            scalars=2,
        )
        columns, t, s_stats, msg = run(
            temporal_kernel,
            [valid_flat, s, exchange(msg), gb, wt],
            [
                ((rows, 3 * middle_pad), BF16),
                ((rows, width), F32),
                ((8, middle_pad), F32),
                (stats_wide, F32),
            ],
            scalars=1,
            us=4.2,
            index=index,
        )
        return padded, s, s_stats, columns, t, exchange(msg)

    ws1, wt1 = unpack(all_weights, 0)
    padded1, s1, s_stats1, columns1, t1, msg = unit_forward(x_tile, x_halo, ws1, wt1, 0)
    t_stats1, y_tile, *edges = run(
        middle_kernel,
        [place, valid_flat, t1, msg, gb],
        [((8, width), F32), (tile_shape, BF16)] + edge_shapes(width),
        scalars=2,
        index=1,
    )
    y_in, all_weights = together(swap_side(edges[2]), all_weights)
    halo = swap_values(edges, y_in)
    ws2, wt2 = unpack(all_weights, 1)
    ws2, wt2, halo = together(ws2, wt2, halo)
    padded2, s2, s_stats2, columns2, t2, msg = unit_forward(y_tile, halo, ws2, wt2, 2)
    t_stats2, block_output, dpre, msg = run(
        top_kernel,
        [valid_flat, t2, msg, gb, x_tile.reshape(rows, width), cot_tile.reshape(rows, width)],
        [((8, width), F32), ((rows, width), F32), ((rows, width), F32), ((devices, 1, 2 * width), F32)],
        scalars=1,
        loose=(1,),
        index=3,
    )

    chip_rows = lax.axis_size("batch") * kept * PIECE_ROWS

    def pack(grads, places, kept):
        shape = ((spare_rows(kept), LANES), BF16)
        return run(
            pack_grads_kernel, [*places, *grads], [shape, shape], stage, scalars=2, us=0.1
        )

    def unit_backward(e, msg, t, t_stats, s, s_stats, columns, padded, ws, wt, index, aside=None):
        dt, en, t_sums, msg = run(
            temporal_grad_kernel,
            [valid_flat, e, t, t_stats, exchange(msg), s, s_stats, gb, wt],
            [
                ((rows, width), BF16),
                ((rows, middle_pad), F32),
                ((2, width), F32),
                ((devices, 1, 2 * middle_pad), F32),
            ],
            [pltpu.VMEM((rows, 3 * width), BF16)],
            scalars=1,
            us=4.5,
            index=index,
        )
        if aside is not None:
            msg, aside = together(msg, sum_cores(aside))
        msg = exchange(msg)
        if aside is not None:
            msg, aside = together(msg, aside)
            aside = sum_chips_first(aside, chip_rows)
        s_sums, ds, *edges = run(
            ds_kernel,
            [place, valid_flat, en, s, s_stats, msg, gb, ws],
            [((2, middle_pad), F32), (ds_shape, BF16)] + edge_shapes(width, 2),
            [pltpu.VMEM((tile_cols + 1, CELL, width), BF16)],
            scalars=2,
            us=4.0,
            index=index,
        )
        edges, columns, dt = together(edges, columns, dt)
        (wt_grad,) = run(temporal_weight_kernel, [columns, dt], [((3 * middle_pad, width), F32)], us=0.1)
        (ws_grad,) = run(spatial_weight_kernel, [padded, ds], [((tap_rows, middle_pad), F32)], us=0.1)
        return ds, edges, (ws_grad, wt_grad), s_sums, t_sums, aside

    def inner_grad(ds, ws):
        return run(spatial_grad_kernel, [ds, ws], [((rows, width), F32)], us=0.1)[0]

    ds, edges, grads2, s_sums2, t_sums2, _ = unit_backward(
        dpre, msg, t2, t_stats2, s2, s_stats2, columns2, padded2, ws2, wt2, 2
    )
    side = swap_side(edges[2])
    halo = swap_rows(*with_ends(at_edge, edges, side)) + [side]
    packed2 = pack(grads2, late_slots, kept)
    inner, halo, packed2 = together(inner_grad(ds, ws2), halo, packed2)
    e1, msg = run(
        between_kernel,
        [place, valid_flat, inner, *halo, t1, t_stats1, gb],
        [((rows, width), F32), ((devices, 1, 2 * width), F32)],
        scalars=2,
        us=2.0,
        index=1,
    )
    ds, edges, grads1, s_sums1, t_sums1, first2 = unit_backward(
        e1, msg, t1, t_stats1, s1, s_stats1, columns1, padded1, ws1, wt1, 0, packed2
    )
    packed1, edges, ds = together(pack(grads1, early_slots, kept), edges, ds)
    terms1, first2, side, ds = together(sum_cores(packed1), first2, swap_side(edges[2]), ds)
    first1, second2, ends, block_output, inner = together(
        sum_chips_first(terms1, chip_rows),
        sum_chips_second(first2),
        with_ends(at_edge, edges, side),
        block_output,
        inner_grad(ds, ws1),
    )
    norm_sums = (s_sums1, t_sums1, s_sums2, t_sums2)
    second1, sums2, ends, norm_sums = together(
        sum_chips_second(first1), sum_batch(second2), ends, norm_sums
    )
    s_sums1, t_sums1, s_sums2, t_sums2 = norm_sums
    sums1 = sum_batch(second1)
    halo = swap_rows(*ends) + [side]
    (input_grad,) = run(
        input_grad_kernel,
        [place, valid_flat, inner, *halo, dpre],
        [((rows, width), F32)],
        scalars=2,
        us=2.0,
        loose=(0,),
    )

    def joined(early, late):
        rest = (slot_count - kept) * PIECE_ROWS
        return jnp.pad(early, ((0, rest), (0, 0))) + jnp.pad(late, ((rest, 0), (0, 0)))

    def whole(grads1, grads2):
        one = pack(grads1, by_core(all_slots[:half], slot_count), slot_count)
        two = pack(grads2, by_core(all_slots[half:], slot_count), slot_count)
        rows = lax.axis_size("batch") * slot_count * PIECE_ROWS
        return scatter_sums([a + b for a, b in zip(one, two)], rows)

    if kept == slot_count:
        grad_mine = joined(sums1, sums2)
    else:
        grad_mine = lax.cond(
            fits,
            lambda early, late, *_: joined(early, late),
            lambda early, late, ones, twos: whole(ones, twos),
            sums1,
            sums2,
            grads1,
            grads2,
        )

    def from_tile(array):
        array = array.reshape(tile_rows, tile_cols, frames, clip_count, width)
        return jnp.transpose(array, (3, 2, 0, 1, 4))

    grad_mine = grad_mine.reshape(slot_count, piece_len)
    correction = 1.0 - 0.5**STEP
    step_rate = 1.8 / math.sqrt(9.0 * width)
    first_new = 0.5 * first_slots + 0.5 * grad_mine
    second_new = 0.5 * second_slots + 0.5 * grad_mine * grad_mine
    master_new = master_slots - step_rate * (
        first_new / correction / (jnp.sqrt(second_new / correction) + ADAM_EPSILON)
        + DECAY_RATE * master_slots
    )
    weight_copy = master_new.astype(BF16)
    norm_grad = jnp.concatenate([s_sums1[:, :middle], t_sums1, s_sums2[:, :middle], t_sums2], axis=1)
    norm_pair = jnp.stack([norm_gains, norm_biases])
    norm_first_new = 0.5 * norm_first + 0.5 * norm_grad
    norm_second_new = 0.5 * norm_second + 0.5 * norm_grad * norm_grad
    norm_new = norm_pair - NORM_RATE * (norm_first_new / correction) / (
        jnp.sqrt(norm_second_new / correction) + ADAM_EPSILON
    )
    return (
        from_tile(block_output),
        from_tile(input_grad),
        master_new,
        first_new,
        second_new,
        weight_copy,
        norm_first_new,
        norm_second_new,
        norm_new,
    )


def solution(mesh):
    wide = P("batch", None, "ha", "wa", None)
    owned = P(AXES, None)
    return jax.shard_map(
        per_device,
        mesh=mesh,
        in_specs=(wide, wide, P("batch"), P(), owned, owned, owned, P(), P(), P(), P()),
        out_specs=(wide, wide, owned, owned, owned, owned, P(), P(), P()),
        check_vma=False,
    )
```

```python
import functools
import math

import jax
import jax.numpy as jnp
from jax import lax
from jax.experimental import pallas as pl
from jax.experimental.pallas import tpu as pltpu
from jax.sharding import PartitionSpec as P

STEP = 5
EPSILON = 1e-05
ADAM_EPSILON = 1e-08
DECAY_RATE = 0.1
NORM_RATE = 0.3

AXES = ("batch", "ha", "wa")
F32 = jnp.float32
BF16 = jnp.bfloat16
VMEM = pl.BlockSpec(memory_space=pltpu.VMEM)
SMEM = pl.BlockSpec(memory_space=pltpu.SMEM)
CELL = 64
LANES = 128
PIECE_ROWS = 16


def sigmoid(v):
    return 1.0 / (1.0 + jnp.exp(-v))


def cell_rows(index, count=1):
    return pl.ds(pl.multiple_of(index * CELL, CELL), count * CELL)


def block_rows(index, size):
    return pl.ds(pl.multiple_of(index * size, size), size)


def fold8(block):
    return jnp.sum(block.reshape(-1, 8, block.shape[-1]), axis=0)


def widen(lane_block, width):
    return jnp.concatenate([lane_block] * (width // LANES), axis=1)


def valid_rows(valid_ref, cells):
    total = valid_ref[0]
    for cell in range(1, cells):
        total = total + valid_ref[cell]
    return total * CELL


def send_stats(values_ref, valid_ref, msg_ref):
    rows, width = values_ref.shape
    cells = rows // CELL
    count = valid_rows(valid_ref, cells)

    def add(cell, total):
        return total + valid_ref[cell] * fold8(values_ref[cell_rows(cell), :])

    total = lax.fori_loop(0, cells, add, jnp.zeros((8, width), F32))
    total = jnp.sum(total, axis=0, keepdims=True)
    mean = total / jnp.maximum(jnp.full((1, width), count, F32), 1.0)

    def add_squares(cell, squares):
        centered = values_ref[cell_rows(cell), :] - mean
        return squares + valid_ref[cell] * fold8(centered * centered)

    squares = lax.fori_loop(0, cells, add_squares, jnp.zeros((8, width), F32))
    squares = jnp.sum(squares, axis=0, keepdims=True)
    message = jnp.concatenate([total, squares, jnp.full((1, LANES), count, F32)], axis=1)
    msg_ref[...] = jnp.broadcast_to(message[None], msg_ref.shape)


def receive_stats(msg_ref):
    devices, _, length = msg_ref.shape
    width = (length - LANES) // 2

    def add(i, carry):
        total, count = carry
        return (total + msg_ref[i, :, :width], count + msg_ref[i, :, 2 * width :])

    total, count = lax.fori_loop(
        0, devices, add, (jnp.zeros((1, width), F32), jnp.zeros((1, LANES), F32)), unroll=4
    )
    count = widen(count, width)
    mean = total / count

    def add_squares(i, squares):
        own = widen(msg_ref[i, :, 2 * width :], width)
        offset = msg_ref[i, :, :width] / jnp.maximum(own, 1.0) - mean
        return squares + msg_ref[i, :, width : 2 * width] + own * offset * offset

    squares = lax.fori_loop(0, devices, add_squares, jnp.zeros((1, width), F32), unroll=4)
    return mean, lax.rsqrt(squares / count + EPSILON), count


def keep_stats(stats_ref, mean, rstd, count):
    stats_ref[0:1, :] = mean
    stats_ref[1:2, :] = rstd
    stats_ref[2:3, :] = count


def receive_sums(msg_ref):
    devices, _, length = msg_ref.shape
    total = lax.fori_loop(
        0, devices, lambda i, t: t + msg_ref[i], jnp.zeros((1, length), F32), unroll=4
    )
    return total[:, : length // 2], total[:, length // 2 :]


def send_sums(bias, gain, msg_ref):
    message = jnp.concatenate(
        [jnp.sum(bias, axis=0, keepdims=True), jnp.sum(gain, axis=0, keepdims=True)], axis=1
    )
    msg_ref[...] = jnp.broadcast_to(message[None], msg_ref.shape)


def later_frame(block):
    return jnp.concatenate([block[8:], jnp.zeros((8, block.shape[1]), block.dtype)], axis=0)


def earlier_frame(block):
    return jnp.concatenate([jnp.zeros((8, block.shape[1]), block.dtype), block[:-8]], axis=0)


UNROLL = 6


def gather_weights_kernel(*refs):
    parts, all_ref, sems = refs[:-2], refs[-2], refs[-1]
    rows = parts[0].shape[0]
    copies = [
        pltpu.make_async_copy(part, all_ref.at[i * rows : (i + 1) * rows, :], sems.at[i])
        for i, part in enumerate(parts)
    ]
    for copy in copies:
        copy.start()
    for copy in copies:
        copy.wait()


def unpack_weights_kernel(slot_ref, all_ref, ws_ref, wt_ref, stage, turn, *, base):
    low = lax.broadcasted_iota(jnp.int32, (8, LANES), 1) < 64
    zero = jnp.zeros((8, LANES), F32)
    spatial_groups = ws_ref.shape[0] // 32

    def load_piece(number):
        start = pl.multiple_of(slot_ref[number] * PIECE_ROWS, PIECE_ROWS)
        return all_ref[pl.ds(start, PIECE_ROWS), :].astype(F32)

    def spatial_groups_at(k, _):
        first = k * UNROLL
        for u in range(UNROLL):
            for q in range(9):
                stage[u, 16 * q : 16 * q + 16, :] = load_piece(base + 9 * (first + u) + q)
        for u in range(UNROLL):
            for i in range(2):
                a = [stage[u, pl.ds(72 * i + j, 8, stride=9), :] for j in range(9)]
                r = [pltpu.roll(a[4 + j], 64, axis=1) for j in range(5)]
                even = a[:4] + [jnp.where(low, a[4], zero)]
                odd = [jnp.where(low, r[j], r[j + 1]) for j in range(4)]
                odd += [jnp.where(low, r[4], zero)]
                for j in range(5):
                    turn[u, j, pl.ds(16 * i, 8, stride=2), :] = even[j]
                    turn[u, j, pl.ds(16 * i + 1, 8, stride=2), :] = odd[j]
        for u in range(UNROLL):
            rows = block_rows(first + u, 32)
            for j in range(5):
                ws_ref[rows, LANES * j : LANES * (j + 1)] = turn[u, j].astype(BF16)
        return 0

    lax.fori_loop(0, spatial_groups // UNROLL, spatial_groups_at, 0)
    temporal_base = base + 9 * spatial_groups
    padded = wt_ref.shape[0] // 3
    pairs = (9 * spatial_groups) // 3 // 6
    for tap in range(3):

        def temporal_pairs(k, _):
            for u in range(UNROLL):
                first = temporal_base + tap * 2 * pairs + 2 * (k * UNROLL + u)
                stage[u, 0:16, :] = load_piece(first)
                stage[u, 16:32, :] = load_piece(first + 1)
            for u in range(UNROLL):
                start = tap * padded + (k * UNROLL + u) * 16
                rows = pl.ds(pl.multiple_of(start, 16), 16)
                for h in range(2):
                    half = stage[u, pl.ds(h, 16, stride=2), :]
                    wt_ref[rows, LANES * h : LANES * (h + 1)] = half.astype(BF16)
            return 0

        lax.fori_loop(0, pairs // UNROLL, temporal_pairs, 0)
        wt_ref[tap * padded + 16 * pairs : (tap + 1) * padded, :] = jnp.zeros(
            (padded - 16 * pairs, wt_ref.shape[1]), BF16
        )


def pack_grads_kernel(sent_at, kept_at, spatial, temporal, sent_ref, kept_ref, stage, turn):
    low = lax.broadcasted_iota(jnp.int32, (8, LANES), 1) < 64
    spatial_groups = spatial.shape[0] // 32
    padded = temporal.shape[0] // 3
    pairs = (9 * spatial_groups) // 3 // 6

    def clear(i, _):
        for out_ref in (sent_ref, kept_ref):
            out_ref[block_rows(i, 128), :] = jnp.zeros((128, LANES), BF16)
        return 0

    lax.fori_loop(0, sent_ref.shape[0] // 128, clear, 0)

    def store_piece(number, rows16):
        low_rows = rows16.astype(BF16)
        for out_ref, at in ((sent_ref, sent_at), (kept_ref, kept_at)):
            start = pl.multiple_of(at[number] * PIECE_ROWS, PIECE_ROWS)
            out_ref[pl.ds(start, PIECE_ROWS), :] = low_rows

    def spatial_groups_at(k, _):
        first = k * UNROLL
        for u in range(UNROLL):
            rows = block_rows(first + u, 32)
            for j in range(5):
                turn[u, j] = spatial[rows, LANES * j : LANES * (j + 1)]
        for u in range(UNROLL):
            for i in range(2):
                even = [turn[u, j, pl.ds(16 * i, 8, stride=2), :] for j in range(5)]
                odd = [turn[u, j, pl.ds(16 * i + 1, 8, stride=2), :] for j in range(5)]
                r = [pltpu.roll(odd[j], 64, axis=1) for j in range(5)]
                flat = even[:4] + [jnp.where(low, even[4], r[0])]
                flat += [jnp.where(low, r[j], r[j + 1]) for j in range(4)]
                for j in range(9):
                    stage[u, pl.ds(72 * i + j, 8, stride=9), :] = flat[j]
        for u in range(UNROLL):
            for q in range(9):
                store_piece(9 * (first + u) + q, stage[u, 16 * q : 16 * q + 16, :])
        return 0

    lax.fori_loop(0, spatial_groups // UNROLL, spatial_groups_at, 0)
    base = 9 * spatial_groups
    for tap in range(3):

        def temporal_pairs(k, _):
            for u in range(UNROLL):
                start = tap * padded + (k * UNROLL + u) * 16
                rows = pl.ds(pl.multiple_of(start, 16), 16)
                for h in range(2):
                    stage[u, pl.ds(h, 16, stride=2), :] = temporal[
                        rows, LANES * h : LANES * (h + 1)
                    ]
            for u in range(UNROLL):
                first = base + tap * 2 * pairs + 2 * (k * UNROLL + u)
                store_piece(first, stage[u, 0:16, :])
                store_piece(first + 1, stage[u, 16:32, :])
            return 0

        lax.fori_loop(0, pairs // UNROLL, temporal_pairs, 0)


def fill_padded(place_ref, padded_ref, tile_ref, halo_refs):
    up, down, side = halo_refs
    rows, cols = tile_ref.shape[:2]
    padded_ref[1 : rows + 1, 1 : cols + 1] = tile_ref[...]
    padded_ref[0, 1 : cols + 1] = up[:cols]
    padded_ref[rows + 1, 1 : cols + 1] = down[:cols]
    for core in range(2):
        near, far = (cols + 1, 0) if core == 0 else (0, cols + 1)

        @pl.when(place_ref[0] == core)
        def _():
            padded_ref[1 : rows + 1, near] = side[...]
            padded_ref[0, near] = up[cols]
            padded_ref[rows + 1, near] = down[cols]
            padded_ref[:, far] = jnp.zeros((rows + 2,) + tile_ref.shape[2:], BF16)


def write_edges(place_ref, tile_ref, edge_refs):
    top, bottom, side = edge_refs
    rows, cols = tile_ref.shape[:2]
    top[...] = tile_ref[0]
    bottom[...] = tile_ref[rows - 1]
    side[...] = tile_ref[:, jnp.where(place_ref[0] == 0, cols - 1, 0)]


def spatial_kernel(
    place_ref, valid_ref, tile_ref, up, down, side, ws_ref, padded_ref, s_ref, msg_ref
):
    rows, cols, cell, width = tile_ref.shape
    fill_padded(place_ref, padded_ref, tile_ref, (up, down, side))

    def one_row(r, _):
        windows = []
        for row_tap in range(3):
            for col_tap in range(3):
                window = padded_ref[r + row_tap, col_tap : col_tap + cols]
                windows.append(window.reshape(cols * cell, width))
        s_ref[block_rows(r, cols * cell), :] = jnp.dot(
            jnp.concatenate(windows, axis=1), ws_ref[...], preferred_element_type=F32
        )
        return 0

    lax.fori_loop(0, rows, one_row, 0)
    send_stats(s_ref, valid_ref, msg_ref)


def weight_back(window, ws_ref, tap, width):
    return lax.dot_general(
        window.reshape(-1, window.shape[-1]),
        ws_ref[block_rows(tap, width), :],
        (((1,), (1,)), ((), ())),
        preferred_element_type=F32,
    )


def edge_grads(place_ref, ds_ref, ws_ref, edge_refs, row_ref):
    top, bottom, side = edge_refs
    width = top.shape[-1]
    cols, cell = top.shape[:2]
    rows = side.shape[0] - 2
    core = place_ref[0]
    for row, row_tap, out, corner in ((0, 0, top, 0), (rows - 1, 2, bottom, rows + 1)):
        total = None
        for col_tap in range(3):
            window = ds_ref[row, pl.ds(3 - core - col_tap, cols + 1)]
            term = weight_back(window, ws_ref, 3 * row_tap + col_tap, width)
            total = term if total is None else total + term
        row_ref[...] = total.astype(BF16).reshape(row_ref.shape)
        out[...] = row_ref[pl.ds(core, cols)]
        side[corner] = row_ref[cols * (1 - core)]
    column = ds_ref[:, jnp.where(core == 0, cols + 1, 2)]
    above, level, below = [
        weight_back(column, ws_ref, 3 * row_tap + 2 - 2 * core, width) for row_tap in range(3)
    ]
    empty = jnp.zeros((cell, width), F32)
    total = level + jnp.concatenate([above[cell:], empty]) + jnp.concatenate([empty, below[:-cell]])
    side[1 : rows + 1] = total.astype(BF16).reshape(rows, cell, width)


def spatial_grad_kernel(ds_ref, ws_ref, grad_ref):
    rows, cols, cell = ds_ref.shape[0], ds_ref.shape[1] - 4, ds_ref.shape[2]
    width = grad_ref.shape[1]
    for row in range(rows):
        total = None
        for row_tap in range(3):
            if not 0 <= row + 1 - row_tap < rows:
                continue
            for col_tap in range(3):
                window = ds_ref[row + 1 - row_tap, 3 - col_tap : 3 - col_tap + cols]
                term = weight_back(window, ws_ref, 3 * row_tap + col_tap, width)
                total = term if total is None else total + term
        grad_ref[row * cols * cell : (row + 1) * cols * cell, :] = total


def add_halo(place_ref, grad_ref, out_ref, halo_refs):
    up, down, side = halo_refs
    rows, cols = side.shape[0] - 2, up.shape[0]
    edge = jnp.where(place_ref[0] == 0, cols - 1, 0)
    out_ref[...] = grad_ref[...]
    last = (rows - 1) * cols
    for c in range(cols):
        out_ref[cell_rows(c), :] += up[c].astype(F32)
        out_ref[cell_rows(last + c), :] += down[c].astype(F32)
    for r in range(rows):
        out_ref[cell_rows(r * cols + edge), :] += side[r + 1].astype(F32)


def spatial_weight_kernel(padded_ref, ds_ref, grad_ref):
    rows, cols, cell, middle = ds_ref.shape
    cols = cols - 4
    width = padded_ref.shape[-1]
    grads = ds_ref[:, 2 : cols + 2].reshape(rows * cols * cell, middle)
    for row_tap in range(3):
        for col_tap in range(3):
            window = padded_ref[row_tap : row_tap + rows, col_tap : col_tap + cols]
            tap = 3 * row_tap + col_tap
            grad_ref[tap * width : (tap + 1) * width, :] = lax.dot_general(
                window.reshape(rows * cols * cell, width),
                grads,
                (((0,), (0,)), ((), ())),
                preferred_element_type=F32,
            )


def between_kernel(
    place_ref, valid_ref, grad_ref, up, down, side, t_ref, stats_ref, gb_ref,
    e_ref, msg_ref, *, index,
):
    rows, width = e_ref.shape
    add_halo(place_ref, grad_ref, e_ref, (up, down, side))
    mean, rstd = stats_ref[0:1, :], stats_ref[1:2, :]
    gain, bias = gb_ref[2 * index : 2 * index + 1, :width], gb_ref[2 * index + 1 : 2 * index + 2, :width]

    def one_cell(c, carry):
        bias_sum, gain_sum = carry
        normal = (t_ref[cell_rows(c), :] - mean) * rstd
        value = normal * gain + bias
        sigma = sigmoid(value)
        e = e_ref[cell_rows(c), :] * valid_ref[c] * (sigma * (1.0 + value * (1.0 - sigma)))
        e_ref[cell_rows(c), :] = e
        return (bias_sum + fold8(e), gain_sum + fold8(e * normal))

    start = jnp.zeros((8, width), F32)
    bias_sum, gain_sum = lax.fori_loop(0, rows // CELL, one_cell, (start, start))
    send_sums(bias_sum, gain_sum, msg_ref)


def input_grad_kernel(
    place_ref, valid_ref, grad_ref, up, down, side, dpre_ref, out_ref
):
    add_halo(place_ref, grad_ref, out_ref, (up, down, side))

    def one_cell(c, carry):
        rows = cell_rows(c)
        out_ref[rows, :] = (out_ref[rows, :] + dpre_ref[rows, :]) * valid_ref[c]
        return carry

    lax.fori_loop(0, out_ref.shape[0] // CELL, one_cell, 0)


def temporal_kernel(
    valid_ref, s_ref, msg_ref, gb_ref, wt_ref, columns_ref, t_ref, stats_ref, out_ref, *, index
):
    rows, middle = s_ref.shape
    mean, rstd, count = receive_stats(msg_ref)
    keep_stats(stats_ref, mean, rstd, count)
    gain, bias = gb_ref[2 * index : 2 * index + 1, :], gb_ref[2 * index + 1 : 2 * index + 2, :]

    def one_cell(c, _):
        value = (s_ref[cell_rows(c), :] - mean) * rstd * gain + bias
        inner = value * sigmoid(value) * valid_ref[c]
        columns_ref[cell_rows(c), 0:middle] = earlier_frame(inner).astype(BF16)
        columns_ref[cell_rows(c), middle : 2 * middle] = inner.astype(BF16)
        columns_ref[cell_rows(c), 2 * middle : 3 * middle] = later_frame(inner).astype(BF16)
        return 0

    lax.fori_loop(0, rows // CELL, one_cell, 0)

    def one_block(i, _):
        t_ref[block_rows(i, 320), :] = jnp.dot(
            columns_ref[block_rows(i, 320), :], wt_ref[...], preferred_element_type=F32
        )
        return 0

    lax.fori_loop(0, rows // 320, one_block, 0)
    send_stats(t_ref, valid_ref, out_ref)


def middle_kernel(
    place_ref, valid_ref, t_ref, msg_ref, gb_ref, stats_ref, tile_ref, top, bottom, side, *, index,
):
    width = t_ref.shape[1]
    rows, cols = tile_ref.shape[:2]
    mean, rstd, count = receive_stats(msg_ref)
    keep_stats(stats_ref, mean, rstd, count)
    gain, bias = gb_ref[2 * index : 2 * index + 1, :width], gb_ref[2 * index + 1 : 2 * index + 2, :width]
    for r in range(rows):
        for c in range(cols):
            number = r * cols + c
            value = (t_ref[number * CELL : (number + 1) * CELL, :] - mean) * rstd * gain + bias
            tile_ref[r, c] = (value * sigmoid(value) * valid_ref[number]).astype(BF16)
    write_edges(place_ref, tile_ref, (top, bottom, side))


def top_kernel(
    valid_ref, t_ref, msg_ref, gb_ref, x_ref, cot_ref, stats_ref, out_ref, dpre_ref, msg_out, *, index
):
    rows, width = t_ref.shape
    mean, rstd, count = receive_stats(msg_ref)
    keep_stats(stats_ref, mean, rstd, count)
    gain, bias = gb_ref[2 * index : 2 * index + 1, :width], gb_ref[2 * index + 1 : 2 * index + 2, :width]

    def one_cell(c, carry):
        bias_sum, gain_sum = carry
        normal = (t_ref[cell_rows(c), :] - mean) * rstd
        pre = normal * gain + bias + x_ref[cell_rows(c), :].astype(F32)
        sigma = sigmoid(pre)
        valid = valid_ref[c]
        out_ref[cell_rows(c), :] = pre * sigma * valid
        dpre = cot_ref[cell_rows(c), :].astype(F32) * valid * (sigma * (1.0 + pre * (1.0 - sigma)))
        dpre_ref[cell_rows(c), :] = dpre
        return (bias_sum + fold8(dpre), gain_sum + fold8(dpre * normal))

    start = jnp.zeros((8, width), F32)
    bias_sum, gain_sum = lax.fori_loop(0, rows // CELL, one_cell, (start, start))
    send_sums(bias_sum, gain_sum, msg_out)


def temporal_grad_kernel(
    valid_ref, e_ref, t_ref, tstats_ref, msg_ref, s_ref, sstats_ref, gb_ref, wt_ref,
    dt_ref, en_ref, sums_ref, msg_out, columns_ref, *, index,
):
    rows, width = e_ref.shape
    middle = s_ref.shape[1]
    bias_grad, gain_grad = receive_sums(msg_ref)
    sums_ref[0:1, :] = gain_grad
    sums_ref[1:2, :] = bias_grad
    mean, rstd, count = tstats_ref[0:1, :], tstats_ref[1:2, :], tstats_ref[2:3, :]
    gain = gb_ref[2 * index + 2 : 2 * index + 3, :width]

    def one_cell(c, _):
        normal = (t_ref[cell_rows(c), :] - mean) * rstd
        dt = (rstd * gain) * (
            e_ref[cell_rows(c), :] - valid_ref[c] * ((bias_grad + normal * gain_grad) / count)
        )
        dt_ref[cell_rows(c), :] = dt.astype(BF16)
        columns_ref[cell_rows(c), 0:width] = later_frame(dt).astype(BF16)
        columns_ref[cell_rows(c), width : 2 * width] = dt.astype(BF16)
        columns_ref[cell_rows(c), 2 * width : 3 * width] = earlier_frame(dt).astype(BF16)
        return 0

    lax.fori_loop(0, rows // CELL, one_cell, 0)

    def one_block(i, _):
        total = None
        for tap in range(3):
            term = lax.dot_general(
                columns_ref[block_rows(i, 320), tap * width : (tap + 1) * width],
                wt_ref[tap * middle : (tap + 1) * middle, :],
                (((1,), (1,)), ((), ())),
                preferred_element_type=F32,
            )
            total = term if total is None else total + term
        en_ref[block_rows(i, 320), :] = total
        return 0

    lax.fori_loop(0, rows // 320, one_block, 0)
    mean_s, rstd_s = sstats_ref[0:1, :], sstats_ref[1:2, :]
    gain_s, bias_s = gb_ref[2 * index : 2 * index + 1, :], gb_ref[2 * index + 1 : 2 * index + 2, :]

    def one_mid_cell(c, carry):
        bias_sum, gain_sum = carry
        normal = (s_ref[cell_rows(c), :] - mean_s) * rstd_s
        value = normal * gain_s + bias_s
        sigma = sigmoid(value)
        e = en_ref[cell_rows(c), :] * valid_ref[c] * (sigma * (1.0 + value * (1.0 - sigma)))
        en_ref[cell_rows(c), :] = e
        return (bias_sum + fold8(e), gain_sum + fold8(e * normal))

    start = jnp.zeros((8, middle), F32)
    bias_sum, gain_sum = lax.fori_loop(0, rows // CELL, one_mid_cell, (start, start))
    send_sums(bias_sum, gain_sum, msg_out)


def temporal_weight_kernel(columns_ref, dt_ref, grad_ref):
    middle = columns_ref.shape[1] // 3
    for tap in range(3):
        grad_ref[tap * middle : (tap + 1) * middle, :] = lax.dot_general(
            columns_ref[:, tap * middle : (tap + 1) * middle],
            dt_ref[...],
            (((0,), (0,)), ((), ())),
            preferred_element_type=F32,
        )


def ds_kernel(
    place_ref, valid_ref, en_ref, s_ref, stats_ref, msg_ref, gb_ref, ws_ref,
    sums_ref, ds_ref, top, bottom, side, row_ref, *, index,
):
    rows, cols = ds_ref.shape[0], ds_ref.shape[1] - 4
    bias_grad, gain_grad = receive_sums(msg_ref)
    sums_ref[0:1, :] = gain_grad
    sums_ref[1:2, :] = bias_grad
    mean, rstd, count = stats_ref[0:1, :], stats_ref[1:2, :], stats_ref[2:3, :]
    scale = rstd * gb_ref[2 * index : 2 * index + 1, :]
    for r in range(rows):
        for c in (0, 1, cols + 2, cols + 3):
            ds_ref[r, c] = jnp.zeros(ds_ref.shape[2:], BF16)
        for c in range(cols):
            number = r * cols + c
            block = slice(number * CELL, (number + 1) * CELL)
            normal = (s_ref[block, :] - mean) * rstd
            ds_ref[r, c + 2] = (
                scale
                * (en_ref[block, :] - valid_ref[number] * ((bias_grad + normal * gain_grad) / count))
            ).astype(BF16)
    edge_grads(place_ref, ds_ref, ws_ref, (top, bottom, side), row_ref)


def run(kernel, ins, outs, scratch=(), scalars=0, us=1.0, extra=8, loose=(), spec=VMEM, **settings):
    held = sum(
        math.prod(x.shape) * jnp.dtype(x.dtype).itemsize
        for x in scratch
        if x.memory_space == pltpu.VMEM
    )
    return pl.pallas_call(
        functools.partial(kernel, **settings),
        out_shape=[
            jax.ShapeDtypeStruct(shape, dtype) if i in loose else pltpu.VMEM(shape, dtype)
            for i, (shape, dtype) in enumerate(outs)
        ],
        in_specs=[SMEM] * scalars + [spec] * (len(ins) - scalars),
        out_specs=[VMEM] * len(outs),
        scratch_shapes=list(scratch),
        cost_estimate=pl.CostEstimate(
            flops=int(us * 1.1e9), bytes_accessed=1000, transcendentals=0
        ),
        compiler_params=pltpu.CompilerParams(vmem_limit_bytes=held + extra * 2**20),
    )(*ins)


def ranks_of_pieces(owner_ids, devices):
    block = 64
    onehot = (owner_ids.reshape(-1, block, 1) == jnp.arange(devices, dtype=jnp.int32)).astype(BF16)
    earlier = jnp.tril(jnp.ones((block, block), BF16), -1)
    within = jnp.einsum("ij,bjd->bid", earlier, onehot, preferred_element_type=F32)
    sums = jnp.sum(onehot.astype(F32), axis=1)
    blocks = jnp.tril(jnp.ones((sums.shape[0],) * 2, F32), -1)
    before = jnp.sum(blocks[:, :, None] * sums[None], axis=1)
    ranking = jnp.sum(onehot.astype(F32) * (within + before[:, None, :]), axis=-1)
    return ranking.reshape(-1).astype(jnp.int32)


def moved_by(step, size):
    return [(i, (i + step) % size) for i in range(size)]


def mirrored(bit, size):
    return [(i, i ^ bit) for i in range(size)]


def gather_batch(own):
    batches = lax.axis_size("batch")
    return [own] + [lax.ppermute(own, "batch", moved_by(k, batches)) for k in range(1, batches)]


def gather_chips_first(steps):
    heights, half = lax.axis_size("ha"), len(steps) // 2
    one, two = jnp.concatenate(steps[:half]), jnp.concatenate(steps[half:])
    one = jnp.concatenate([one, lax.ppermute(one, "ha", mirrored(1, heights))])
    two = jnp.concatenate([two, lax.ppermute(two, "ha", mirrored(2, heights))])
    return one, two


def gather_chips_second(one, two, beside):
    heights = lax.axis_size("ha")
    across = mirrored(1, 2)
    one_next = lax.ppermute(one, "ha", mirrored(2, heights))
    two_next = lax.ppermute(two, "ha", mirrored(1, heights))
    others = [lax.ppermute(one, "wa", across), lax.ppermute(two, "wa", across)]
    one_next, two_next, beside = together(one_next, two_next, beside)
    others = [
        others[0],
        lax.ppermute(one_next, "wa", across),
        others[1],
        lax.ppermute(two_next, "wa", across),
    ]
    return [one, one_next, two, two_next] + others, beside


def part_position(owner_ids, place):
    batches, heights, cores = (lax.axis_size(axis) for axis in AXES)
    z, h, w = place
    core = (owner_ids % cores) ^ w
    turn = (owner_ids // cores % heights) ^ h
    step = (z - owner_ids // (cores * heights)) % batches
    half = batches // 2
    swapped = jnp.where(turn == 1, 2, jnp.where(turn == 2, 1, turn))
    block = jnp.where(
        step < half, turn * half + step, heights * half + swapped * half + step - half
    )
    return core * batches * heights + block


def target_position(owner_ids, place):
    batches, heights, cores = (lax.axis_size(axis) for axis in AXES)
    z, h, w = place
    core = (owner_ids % cores) ^ w
    turn = (owner_ids // cores % heights) ^ h
    step = (owner_ids // (cores * heights) - z) % batches
    return (core * heights + turn) * batches + step


def add_low(a, b):
    return (a.astype(F32) + b.astype(F32)).astype(BF16)


def sum_cores(packed):
    sent, kept = packed
    return [kept, lax.ppermute(sent, "wa", mirrored(1, 2))]


def added(terms, block, part, rows):
    half = rows // 2
    start = block * rows + part * half
    return add_low(*[t[start : start + half] for t in terms])


def move_chips_first(terms, rows):
    heights = lax.axis_size("ha")
    one = jnp.stack([added(terms, 1, 0, rows), added(terms, 3, 0, rows)])
    two = jnp.stack([added(terms, 2, 1, rows), added(terms, 3, 1, rows)])
    return (
        lax.ppermute(one, "ha", mirrored(1, heights)),
        lax.ppermute(two, "ha", mirrored(2, heights)),
    )


def add_chips_first(terms, moved, rows):
    one, two = moved
    return [
        add_low(added(terms, 0, 0, rows), one[0]),
        add_low(added(terms, 2, 0, rows), one[1]),
        add_low(added(terms, 0, 1, rows), two[0]),
        add_low(added(terms, 1, 1, rows), two[1]),
    ]


def move_chips_second(sums):
    heights = lax.axis_size("ha")
    return (
        lax.ppermute(sums[1], "ha", mirrored(2, heights)),
        lax.ppermute(sums[3], "ha", mirrored(1, heights)),
    )


def add_chips_second(sums, moved):
    own = jnp.concatenate([add_low(sums[0], moved[0]), add_low(sums[2], moved[1])])
    return own.reshape(lax.axis_size("batch"), -1, LANES)


def move_batch(own):
    batches = own.shape[0]
    return [lax.ppermute(own[k], "batch", moved_by(k, batches)) for k in range(1, batches)]


def add_batch(own, moved):
    total = own[0].astype(F32)
    for block in moved:
        total = total + block.astype(F32)
    return total


def scatter_sums(packed, rows):
    terms = sum_cores(packed)
    sums = add_chips_first(terms, move_chips_first(terms, rows), rows)
    own = add_chips_second(sums, move_chips_second(sums))
    return add_batch(own, move_batch(own))


def together(*values):
    return lax.optimization_barrier(values)


def exchange(message):
    return lax.all_to_all(message, AXES, 0, 0, tiled=True)


def swap_side(side):
    return lax.ppermute(side, "wa", mirrored(1, 2))


def swap_rows(top, bottom):
    count = lax.axis_size("ha")
    forward = [(i, i + 1) for i in range(count - 1)]
    backward = [(i + 1, i) for i in range(count - 1)]
    return [lax.ppermute(bottom, "ha", forward), lax.ppermute(top, "ha", backward)]


def swap_values(edges, side):
    top, bottom, _ = edges
    rows = swap_rows(
        jnp.concatenate([top, side[:1]]), jnp.concatenate([bottom, side[-1:]])
    )
    return rows + [side]


def with_ends(at_edge, edges, side):
    top, bottom, _ = edges
    return [
        jnp.where(at_edge[:, None, None], add_low(row, side[end][None]), row)
        for row, end in ((top, 0), (bottom, -1))
    ]


def per_device(
    block_input,
    cotangent,
    frame_sides,
    owner_list,
    master_slots,
    first_slots,
    second_slots,
    norm_gains,
    norm_biases,
    norm_first,
    norm_second,
):
    clip_count, frames, tile_rows, tile_cols, width = block_input.shape
    devices = lax.axis_size(AXES)
    slot_count, piece_len = master_slots.shape
    middle = norm_gains.shape[0] // 2 - width
    middle_pad = -(-middle // LANES) * LANES
    rows = clip_count * frames * tile_rows * tile_cols

    low_slots = master_slots.astype(BF16).reshape(slot_count * PIECE_ROWS, LANES)

    steps = gather_batch(low_slots)

    own_side = frame_sides[0]
    row_ids = lax.axis_index("ha") * tile_rows + jnp.arange(tile_rows, dtype=jnp.int32)
    col_ids = lax.axis_index("wa") * tile_cols + jnp.arange(tile_cols, dtype=jnp.int32)
    grid_rows = tile_rows * lax.axis_size("ha")
    grid_cols = tile_cols * lax.axis_size("wa")
    valid = (
        (row_ids[:, None] >= grid_rows - own_side) & (col_ids[None, :] >= grid_cols - own_side)
    ).astype(F32)
    valid_flat = valid.reshape(-1)
    place = lax.axis_index("wa").reshape(1)
    def to_tile(array):
        return jnp.transpose(array, (2, 3, 1, 0, 4)).reshape(tile_rows, tile_cols, CELL, width)

    x_tile = to_tile(block_input) * valid[:, :, None, None].astype(BF16)
    edge = jnp.where(place[0] == 0, tile_cols - 1, 0)
    x_side = lax.dynamic_index_in_dim(x_tile, edge, axis=1, keepdims=False)
    x_halo = swap_values((x_tile[0], x_tile[-1], x_side), swap_side(x_side))
    steps, x_tile, x_halo, cotangent, owner_list, norm_gains, norm_biases = together(
        steps, x_tile, x_halo, cotangent, owner_list, norm_gains, norm_biases
    )
    one, two = gather_chips_first(steps)

    cot_tile = to_tile(cotangent)
    owner_ids = owner_list[:, 0]
    ranking = ranks_of_pieces(owner_ids, devices)
    here = [lax.axis_index(axis) for axis in AXES]
    slot_index = part_position(owner_ids, here) * slot_count + ranking
    half = owner_list.shape[0] // 2
    kept = min(slot_count, int(slot_count / 2 + 1.83 * math.sqrt(slot_count)))
    target = target_position(owner_ids, here)
    all_slots = target * slot_count + ranking
    late_rank = ranking[half:] - (slot_count - kept)
    fits = jnp.all(ranking[:half] < kept) & jnp.all(late_rank >= 0)

    def by_core(positions, kept):
        here = devices // 2 * kept
        sent_at = jnp.where(positions >= here, positions - here, here)
        return sent_at, jnp.where(positions < here, positions, here)

    def spare_rows(kept):
        return -(-(devices // 2 * kept + 1) * PIECE_ROWS // 128) * 128

    early_slots = by_core(jnp.where(fits, target[:half] * kept + ranking[:half], 0), kept)
    late_slots = by_core(jnp.where(fits, target[half:] * kept + late_rank, 0), kept)

    bounds = [0, middle, middle + width, 2 * middle + width, 2 * middle + 2 * width]
    gb = []
    for i in range(4):
        for vector in (norm_gains, norm_biases):
            part = vector[bounds[i] : bounds[i + 1]]
            gb.append(jnp.pad(part, (0, middle_pad - part.shape[0])))
    gb = jnp.stack(gb)

    at_edge = jnp.arange(tile_cols) == edge
    prepared = (at_edge, x_tile, x_halo, cot_tile, valid_flat, gb, slot_index, all_slots, early_slots, late_slots, fits)
    parts, prepared = gather_chips_second(one, two, prepared)
    at_edge, x_tile, x_halo, cot_tile, valid_flat, gb, slot_index, all_slots, early_slots, late_slots, fits = prepared

    tap_rows = 9 * width
    stage = [pltpu.VMEM((UNROLL, 144, LANES), F32), pltpu.VMEM((UNROLL, 5, 32, LANES), F32)]
    weight_shapes = [((tap_rows, middle_pad), BF16), ((3 * middle_pad, width), BF16)]
    (all_weights,) = run(
        gather_weights_kernel,
        parts,
        [((devices * slot_count * PIECE_ROWS, LANES), BF16)],
        [pltpu.SemaphoreType.DMA((len(parts),))],
        us=3.0,
        spec=pl.BlockSpec(memory_space=pl.ANY),
    )

    def unpack(all_weights, unit):
        return run(
            unpack_weights_kernel,
            [slot_index, all_weights],
            weight_shapes,
            stage,
            1,
            4.3,
            base=unit * (owner_list.shape[0] // 2),
        )

    tile_shape = (tile_rows, tile_cols, CELL, width)
    padded_tile = (tile_rows + 2, tile_cols + 2, CELL, width)
    ds_shape = (tile_rows, tile_cols + 4, CELL, middle_pad)
    stats_mid = (devices, 1, 2 * middle_pad + LANES)
    stats_wide = (devices, 1, 2 * width + LANES)

    def edge_shapes(lanes, beside=0):
        row, col = (tile_cols, CELL, lanes), (tile_rows + beside, CELL, lanes)
        return [(row, BF16), (row, BF16), (col, BF16)]

    def unit_forward(tile, halo, ws, wt, index):
        padded, s, msg = run(
            spatial_kernel,
            [place, valid_flat, tile, *halo, ws],
            [(padded_tile, BF16), ((rows, middle_pad), F32), (stats_mid, F32)],
            us=5.5,
            scalars=2,
        )
        columns, t, s_stats, msg = run(
            temporal_kernel,
            [valid_flat, s, exchange(msg), gb, wt],
            [
                ((rows, 3 * middle_pad), BF16),
                ((rows, width), F32),
                ((8, middle_pad), F32),
                (stats_wide, F32),
            ],
            scalars=1,
            us=4.2,
            index=index,
        )
        return padded, s, s_stats, columns, t, exchange(msg)

    ws1, wt1 = unpack(all_weights, 0)
    padded1, s1, s_stats1, columns1, t1, msg = unit_forward(x_tile, x_halo, ws1, wt1, 0)
    t_stats1, y_tile, *edges = run(
        middle_kernel,
        [place, valid_flat, t1, msg, gb],
        [((8, width), F32), (tile_shape, BF16)] + edge_shapes(width),
        scalars=2,
        index=1,
    )
    y_in, all_weights = together(swap_side(edges[2]), all_weights)
    halo = swap_values(edges, y_in)
    ws2, wt2 = unpack(all_weights, 1)
    ws2, wt2, halo = together(ws2, wt2, halo)
    padded2, s2, s_stats2, columns2, t2, msg = unit_forward(y_tile, halo, ws2, wt2, 2)
    t_stats2, block_output, dpre, msg = run(
        top_kernel,
        [valid_flat, t2, msg, gb, x_tile.reshape(rows, width), cot_tile.reshape(rows, width)],
        [((8, width), F32), ((rows, width), F32), ((rows, width), F32), ((devices, 1, 2 * width), F32)],
        scalars=1,
        loose=(1,),
        index=3,
    )

    chip_rows = lax.axis_size("batch") * kept * PIECE_ROWS

    def pack(grads, places, kept):
        shape = ((spare_rows(kept), LANES), BF16)
        return run(
            pack_grads_kernel, [*places, *grads], [shape, shape], stage, scalars=2, us=0.1
        )

    def unit_backward(e, msg, t, t_stats, s, s_stats, columns, padded, ws, wt, index, aside=None):
        dt, en, t_sums, msg = run(
            temporal_grad_kernel,
            [valid_flat, e, t, t_stats, exchange(msg), s, s_stats, gb, wt],
            [
                ((rows, width), BF16),
                ((rows, middle_pad), F32),
                ((2, width), F32),
                ((devices, 1, 2 * middle_pad), F32),
            ],
            [pltpu.VMEM((rows, 3 * width), BF16)],
            scalars=1,
            us=4.5,
            index=index,
        )
        if aside is not None:
            msg, aside = together(msg, sum_cores(aside))
        msg = exchange(msg)
        if aside is not None:
            msg, aside = together(msg, aside)
            moved = move_chips_first(aside, chip_rows)
        s_sums, ds, *edges = run(
            ds_kernel,
            [place, valid_flat, en, s, s_stats, msg, gb, ws],
            [((2, middle_pad), F32), (ds_shape, BF16)] + edge_shapes(width, 2),
            [pltpu.VMEM((tile_cols + 1, CELL, width), BF16)],
            scalars=2,
            us=4.0,
            index=index,
        )
        edges, columns, dt = together(edges, columns, dt)
        (wt_grad,) = run(temporal_weight_kernel, [columns, dt], [((3 * middle_pad, width), F32)], us=0.1)
        (ws_grad,) = run(spatial_weight_kernel, [padded, ds], [((tap_rows, middle_pad), F32)], us=0.1)
        return ds, edges, (ws_grad, wt_grad), s_sums, t_sums, aside and (aside, moved)

    def inner_grad(ds, ws):
        return run(spatial_grad_kernel, [ds, ws], [((rows, width), F32)], us=3.0)[0]

    ds, edges, grads2, s_sums2, t_sums2, _ = unit_backward(
        dpre, msg, t2, t_stats2, s2, s_stats2, columns2, padded2, ws2, wt2, 2
    )
    side = swap_side(edges[2])
    halo = swap_rows(*with_ends(at_edge, edges, side)) + [side]
    packed2 = pack(grads2, late_slots, kept)
    inner, halo, packed2 = together(inner_grad(ds, ws2), halo, packed2)
    e1, msg = run(
        between_kernel,
        [place, valid_flat, inner, *halo, t1, t_stats1, gb],
        [((rows, width), F32), ((devices, 1, 2 * width), F32)],
        scalars=2,
        us=2.0,
        index=1,
    )
    ds, edges, grads1, s_sums1, t_sums1, moving2 = unit_backward(
        e1, msg, t1, t_stats1, s1, s_stats1, columns1, padded1, ws1, wt1, 0, packed2
    )
    packed1, moving2, edges, ds = together(pack(grads1, early_slots, kept), moving2, edges, ds)
    first2 = add_chips_first(*moving2, chip_rows)
    side, ds = together(swap_side(edges[2]), ds)
    terms1, moved2, side, inner, first2 = together(
        sum_cores(packed1), move_chips_second(first2), side, inner_grad(ds, ws1), first2
    )
    own2 = add_chips_second(first2, moved2)
    moved1, moved2, ends, block_output, terms1, own2 = together(
        move_chips_first(terms1, chip_rows),
        move_batch(own2),
        with_ends(at_edge, edges, side),
        block_output,
        terms1,
        own2,
    )
    first1 = add_chips_first(terms1, moved1, chip_rows)
    sums = (own2, moved2, s_sums1, t_sums1, s_sums2, t_sums2)
    moved1, ends, sums, first1 = together(move_chips_second(first1), ends, sums, first1)
    own2, moved2, s_sums1, t_sums1, s_sums2, t_sums2 = sums
    own1 = add_chips_second(first1, moved1)
    moved1, rows_in, own1 = together(move_batch(own1), swap_rows(*ends), own1)
    (input_grad,) = run(
        input_grad_kernel,
        [place, valid_flat, inner, *rows_in, side, dpre],
        [((rows, width), F32)],
        scalars=2,
        us=2.0,
        loose=(0,),
    )
    sums1, sums2 = add_batch(own1, moved1), add_batch(own2, moved2)

    def joined(early, late):
        rest = (slot_count - kept) * PIECE_ROWS
        return jnp.pad(early, ((0, rest), (0, 0))) + jnp.pad(late, ((rest, 0), (0, 0)))

    def whole(grads1, grads2):
        one = pack(grads1, by_core(all_slots[:half], slot_count), slot_count)
        two = pack(grads2, by_core(all_slots[half:], slot_count), slot_count)
        rows = lax.axis_size("batch") * slot_count * PIECE_ROWS
        return scatter_sums([a + b for a, b in zip(one, two)], rows)

    if kept == slot_count:
        grad_mine = joined(sums1, sums2)
    else:
        grad_mine = lax.cond(
            fits,
            lambda early, late, *_: joined(early, late),
            lambda early, late, ones, twos: whole(ones, twos),
            sums1,
            sums2,
            grads1,
            grads2,
        )

    def from_tile(array):
        array = array.reshape(tile_rows, tile_cols, frames, clip_count, width)
        return jnp.transpose(array, (3, 2, 0, 1, 4))

    grad_mine = grad_mine.reshape(slot_count, piece_len)
    correction = 1.0 - 0.5**STEP
    step_rate = 1.8 / math.sqrt(9.0 * width)
    first_new = 0.5 * first_slots + 0.5 * grad_mine
    second_new = 0.5 * second_slots + 0.5 * grad_mine * grad_mine
    master_new = master_slots - step_rate * (
        first_new / correction / (jnp.sqrt(second_new / correction) + ADAM_EPSILON)
        + DECAY_RATE * master_slots
    )
    weight_copy = master_new.astype(BF16)
    norm_grad = jnp.concatenate([s_sums1[:, :middle], t_sums1, s_sums2[:, :middle], t_sums2], axis=1)
    norm_pair = jnp.stack([norm_gains, norm_biases])
    norm_first_new = 0.5 * norm_first + 0.5 * norm_grad
    norm_second_new = 0.5 * norm_second + 0.5 * norm_grad * norm_grad
    norm_new = norm_pair - NORM_RATE * (norm_first_new / correction) / (
        jnp.sqrt(norm_second_new / correction) + ADAM_EPSILON
    )
    return (
        from_tile(block_output),
        from_tile(input_grad),
        master_new,
        first_new,
        second_new,
        weight_copy,
        norm_first_new,
        norm_second_new,
        norm_new,
    )


def solution(mesh):
    wide = P("batch", None, "ha", "wa", None)
    owned = P(AXES, None)
    return jax.shard_map(
        per_device,
        mesh=mesh,
        in_specs=(wide, wide, P("batch"), P(), owned, owned, owned, P(), P(), P(), P()),
        out_specs=(wide, wide, owned, owned, owned, owned, P(), P(), P()),
        check_vma=False,
    )
```

```python
import functools
import math

import jax
import jax.numpy as jnp
from jax import lax
from jax.experimental import pallas as pl
from jax.experimental.pallas import tpu as pltpu
from jax.sharding import PartitionSpec as P

STEP = 5
EPSILON = 1e-05
ADAM_EPSILON = 1e-08
DECAY_RATE = 0.1
NORM_RATE = 0.3

AXES = ("batch", "ha", "wa")
F32 = jnp.float32
BF16 = jnp.bfloat16
VMEM = pl.BlockSpec(memory_space=pltpu.VMEM)
SMEM = pl.BlockSpec(memory_space=pltpu.SMEM)
CELL = 64
LANES = 128
PIECE_ROWS = 16


def sigmoid(v):
    return 1.0 / (1.0 + jnp.exp(-v))


def cell_rows(index, count=1):
    return pl.ds(pl.multiple_of(index * CELL, CELL), count * CELL)


def block_rows(index, size):
    return pl.ds(pl.multiple_of(index * size, size), size)


def fold8(block):
    return jnp.sum(block.reshape(-1, 8, block.shape[-1]), axis=0)


def widen(lane_block, width):
    return jnp.concatenate([lane_block] * (width // LANES), axis=1)


def valid_rows(valid_ref, cells):
    total = valid_ref[0]
    for cell in range(1, cells):
        total = total + valid_ref[cell]
    return total * CELL


def send_stats(values_ref, valid_ref, msg_ref):
    rows, width = values_ref.shape
    cells = rows // CELL
    count = valid_rows(valid_ref, cells)

    def add(cell, total):
        return total + valid_ref[cell] * fold8(values_ref[cell_rows(cell), :])

    total = lax.fori_loop(0, cells, add, jnp.zeros((8, width), F32))
    total = jnp.sum(total, axis=0, keepdims=True)
    mean = total / jnp.maximum(jnp.full((1, width), count, F32), 1.0)

    def add_squares(cell, squares):
        centered = values_ref[cell_rows(cell), :] - mean
        return squares + valid_ref[cell] * fold8(centered * centered)

    squares = lax.fori_loop(0, cells, add_squares, jnp.zeros((8, width), F32))
    squares = jnp.sum(squares, axis=0, keepdims=True)
    message = jnp.concatenate([total, squares, jnp.full((1, LANES), count, F32)], axis=1)
    msg_ref[...] = jnp.broadcast_to(message[None], msg_ref.shape)


def receive_stats(msg_ref):
    devices, _, length = msg_ref.shape
    width = (length - LANES) // 2

    def add(i, carry):
        total, count = carry
        return (total + msg_ref[i, :, :width], count + msg_ref[i, :, 2 * width :])

    total, count = lax.fori_loop(
        0, devices, add, (jnp.zeros((1, width), F32), jnp.zeros((1, LANES), F32)), unroll=4
    )
    count = widen(count, width)
    mean = total / count

    def add_squares(i, squares):
        own = widen(msg_ref[i, :, 2 * width :], width)
        offset = msg_ref[i, :, :width] / jnp.maximum(own, 1.0) - mean
        return squares + msg_ref[i, :, width : 2 * width] + own * offset * offset

    squares = lax.fori_loop(0, devices, add_squares, jnp.zeros((1, width), F32), unroll=4)
    return mean, lax.rsqrt(squares / count + EPSILON), count


def keep_stats(stats_ref, mean, rstd, count):
    stats_ref[0:1, :] = mean
    stats_ref[1:2, :] = rstd
    stats_ref[2:3, :] = count


def receive_sums(msg_ref):
    devices, _, length = msg_ref.shape
    total = lax.fori_loop(
        0, devices, lambda i, t: t + msg_ref[i], jnp.zeros((1, length), F32), unroll=4
    )
    return total[:, : length // 2], total[:, length // 2 :]


def send_sums(bias, gain, msg_ref):
    message = jnp.concatenate(
        [jnp.sum(bias, axis=0, keepdims=True), jnp.sum(gain, axis=0, keepdims=True)], axis=1
    )
    msg_ref[...] = jnp.broadcast_to(message[None], msg_ref.shape)


def later_frame(block):
    return jnp.concatenate([block[8:], jnp.zeros((8, block.shape[1]), block.dtype)], axis=0)


def earlier_frame(block):
    return jnp.concatenate([jnp.zeros((8, block.shape[1]), block.dtype), block[:-8]], axis=0)


UNROLL = 6


def gather_weights_kernel(*refs):
    parts, all_ref, sems = refs[:-2], refs[-2], refs[-1]
    rows = parts[0].shape[0]
    copies = [
        pltpu.make_async_copy(part, all_ref.at[i * rows : (i + 1) * rows, :], sems.at[i])
        for i, part in enumerate(parts)
    ]
    for copy in copies:
        copy.start()
    for copy in copies:
        copy.wait()


def unpack_weights_kernel(slot_ref, all_ref, ws_ref, wt_ref, stage, turn, *, base):
    low = lax.broadcasted_iota(jnp.int32, (8, LANES), 1) < 64
    zero = jnp.zeros((8, LANES), F32)
    spatial_groups = ws_ref.shape[0] // 32

    def load_piece(number):
        start = pl.multiple_of(slot_ref[number], PIECE_ROWS)
        return all_ref[pl.ds(start, PIECE_ROWS), :].astype(F32)

    def spatial_groups_at(k, _):
        first = k * UNROLL
        for u in range(UNROLL):
            for q in range(9):
                stage[u, 16 * q : 16 * q + 16, :] = load_piece(base + 9 * (first + u) + q)
        for u in range(UNROLL):
            for i in range(2):
                a = [stage[u, pl.ds(72 * i + j, 8, stride=9), :] for j in range(9)]
                r = [pltpu.roll(a[4 + j], 64, axis=1) for j in range(5)]
                even = a[:4] + [jnp.where(low, a[4], zero)]
                odd = [jnp.where(low, r[j], r[j + 1]) for j in range(4)]
                odd += [jnp.where(low, r[4], zero)]
                for j in range(5):
                    turn[u, j, pl.ds(16 * i, 8, stride=2), :] = even[j]
                    turn[u, j, pl.ds(16 * i + 1, 8, stride=2), :] = odd[j]
        for u in range(UNROLL):
            rows = block_rows(first + u, 32)
            for j in range(5):
                ws_ref[rows, LANES * j : LANES * (j + 1)] = turn[u, j].astype(BF16)
        return 0

    lax.fori_loop(0, spatial_groups // UNROLL, spatial_groups_at, 0)
    temporal_base = base + 9 * spatial_groups
    padded = wt_ref.shape[0] // 3
    pairs = (9 * spatial_groups) // 3 // 6
    for tap in range(3):

        def temporal_pairs(k, _):
            for u in range(UNROLL):
                first = temporal_base + tap * 2 * pairs + 2 * (k * UNROLL + u)
                stage[u, 0:16, :] = load_piece(first)
                stage[u, 16:32, :] = load_piece(first + 1)
            for u in range(UNROLL):
                start = tap * padded + (k * UNROLL + u) * 16
                rows = pl.ds(pl.multiple_of(start, 16), 16)
                for h in range(2):
                    half = stage[u, pl.ds(h, 16, stride=2), :]
                    wt_ref[rows, LANES * h : LANES * (h + 1)] = half.astype(BF16)
            return 0

        lax.fori_loop(0, pairs // UNROLL, temporal_pairs, 0)
        wt_ref[tap * padded + 16 * pairs : (tap + 1) * padded, :] = jnp.zeros(
            (padded - 16 * pairs, wt_ref.shape[1]), BF16
        )


def pack_grads_kernel(*refs, places, begun):
    at_refs, (spatial, temporal) = refs[:places], refs[places : places + 2]
    out_refs = refs[places + 2 + begun : -2]
    stage, turn = refs[-2:]
    low = lax.broadcasted_iota(jnp.int32, (8, LANES), 1) < 64
    spatial_groups = spatial.shape[0] // 32
    padded = temporal.shape[0] // 3
    pairs = (9 * spatial_groups) // 3 // 6

    for out_ref in out_refs[begun:]:

        def clear(i, _):
            out_ref[block_rows(i, 128), :] = jnp.zeros((128, LANES), BF16)
            return 0

        lax.fori_loop(0, out_ref.shape[0] // 128, clear, 0)

    def store_piece(number, rows16):
        low_rows = rows16.astype(BF16)
        for out_ref, at_ref in zip(out_refs, at_refs):
            start = pl.multiple_of(at_ref[number], PIECE_ROWS)
            out_ref[pl.ds(start, PIECE_ROWS), :] = low_rows

    def spatial_groups_at(k, _):
        first = k * UNROLL
        for u in range(UNROLL):
            rows = block_rows(first + u, 32)
            for j in range(5):
                turn[u, j] = spatial[rows, LANES * j : LANES * (j + 1)]
        for u in range(UNROLL):
            for i in range(2):
                even = [turn[u, j, pl.ds(16 * i, 8, stride=2), :] for j in range(5)]
                odd = [turn[u, j, pl.ds(16 * i + 1, 8, stride=2), :] for j in range(5)]
                r = [pltpu.roll(odd[j], 64, axis=1) for j in range(5)]
                flat = even[:4] + [jnp.where(low, even[4], r[0])]
                flat += [jnp.where(low, r[j], r[j + 1]) for j in range(4)]
                for j in range(9):
                    stage[u, pl.ds(72 * i + j, 8, stride=9), :] = flat[j]
        for u in range(UNROLL):
            for q in range(9):
                store_piece(9 * (first + u) + q, stage[u, 16 * q : 16 * q + 16, :])
        return 0

    lax.fori_loop(0, spatial_groups // UNROLL, spatial_groups_at, 0)
    base = 9 * spatial_groups
    for tap in range(3):

        def temporal_pairs(k, _):
            for u in range(UNROLL):
                start = tap * padded + (k * UNROLL + u) * 16
                rows = pl.ds(pl.multiple_of(start, 16), 16)
                for h in range(2):
                    stage[u, pl.ds(h, 16, stride=2), :] = temporal[
                        rows, LANES * h : LANES * (h + 1)
                    ]
            for u in range(UNROLL):
                first = base + tap * 2 * pairs + 2 * (k * UNROLL + u)
                store_piece(first, stage[u, 0:16, :])
                store_piece(first + 1, stage[u, 16:32, :])
            return 0

        lax.fori_loop(0, pairs // UNROLL, temporal_pairs, 0)


def fill_padded(place_ref, padded_ref, tile_ref, halo_refs):
    up, down, side = halo_refs
    rows, cols = tile_ref.shape[:2]
    padded_ref[1 : rows + 1, 1 : cols + 1] = tile_ref[...]
    padded_ref[0, 1 : cols + 1] = up[:cols]
    padded_ref[rows + 1, 1 : cols + 1] = down[:cols]
    for core in range(2):
        near, far = (cols + 1, 0) if core == 0 else (0, cols + 1)

        @pl.when(place_ref[0] == core)
        def _():
            padded_ref[1 : rows + 1, near] = side[...]
            padded_ref[0, near] = up[cols]
            padded_ref[rows + 1, near] = down[cols]
            padded_ref[:, far] = jnp.zeros((rows + 2,) + tile_ref.shape[2:], BF16)


def write_edges(place_ref, tile_ref, edge_refs):
    top, bottom, side = edge_refs
    rows, cols = tile_ref.shape[:2]
    top[...] = tile_ref[0]
    bottom[...] = tile_ref[rows - 1]
    side[...] = tile_ref[:, jnp.where(place_ref[0] == 0, cols - 1, 0)]


def spatial_kernel(
    place_ref, valid_ref, tile_ref, up, down, side, ws_ref, padded_ref, s_ref, msg_ref
):
    rows, cols, cell, width = tile_ref.shape
    fill_padded(place_ref, padded_ref, tile_ref, (up, down, side))

    def one_row(r, _):
        windows = []
        for row_tap in range(3):
            for col_tap in range(3):
                window = padded_ref[r + row_tap, col_tap : col_tap + cols]
                windows.append(window.reshape(cols * cell, width))
        s_ref[block_rows(r, cols * cell), :] = jnp.dot(
            jnp.concatenate(windows, axis=1), ws_ref[...], preferred_element_type=F32
        )
        return 0

    lax.fori_loop(0, rows, one_row, 0)
    send_stats(s_ref, valid_ref, msg_ref)


def weight_back(window, ws_ref, tap, width):
    return lax.dot_general(
        window.reshape(-1, window.shape[-1]),
        ws_ref[block_rows(tap, width), :],
        (((1,), (1,)), ((), ())),
        preferred_element_type=F32,
    )


def edge_grads(place_ref, ds_ref, ws_ref, edge_refs, row_ref):
    top, bottom, side = edge_refs
    width = top.shape[-1]
    cols, cell = top.shape[:2]
    rows = side.shape[0] - 2
    core = place_ref[0]
    for row, row_tap, out, corner in ((0, 0, top, 0), (rows - 1, 2, bottom, rows + 1)):
        total = None
        for col_tap in range(3):
            window = ds_ref[row, pl.ds(3 - core - col_tap, cols + 1)]
            term = weight_back(window, ws_ref, 3 * row_tap + col_tap, width)
            total = term if total is None else total + term
        row_ref[...] = total.astype(BF16).reshape(row_ref.shape)
        out[...] = row_ref[pl.ds(core, cols)]
        side[corner] = row_ref[cols * (1 - core)]
    column = ds_ref[:, jnp.where(core == 0, cols + 1, 2)]
    above, level, below = [
        weight_back(column, ws_ref, 3 * row_tap + 2 - 2 * core, width) for row_tap in range(3)
    ]
    empty = jnp.zeros((cell, width), F32)
    total = level + jnp.concatenate([above[cell:], empty]) + jnp.concatenate([empty, below[:-cell]])
    side[1 : rows + 1] = total.astype(BF16).reshape(rows, cell, width)


def spatial_grad_kernel(ds_ref, ws_ref, grad_ref):
    rows, cols, cell = ds_ref.shape[0], ds_ref.shape[1] - 4, ds_ref.shape[2]
    width = grad_ref.shape[1]
    for row in range(rows):
        total = None
        for row_tap in range(3):
            if not 0 <= row + 1 - row_tap < rows:
                continue
            for col_tap in range(3):
                window = ds_ref[row + 1 - row_tap, 3 - col_tap : 3 - col_tap + cols]
                term = weight_back(window, ws_ref, 3 * row_tap + col_tap, width)
                total = term if total is None else total + term
        grad_ref[row * cols * cell : (row + 1) * cols * cell, :] = total


def add_halo(place_ref, grad_ref, out_ref, halo_refs):
    up, down, side = halo_refs
    rows, cols = side.shape[0] - 2, up.shape[0]
    edge = jnp.where(place_ref[0] == 0, cols - 1, 0)
    out_ref[...] = grad_ref[...]
    last = (rows - 1) * cols
    for c in range(cols):
        out_ref[cell_rows(c), :] += up[c].astype(F32)
        out_ref[cell_rows(last + c), :] += down[c].astype(F32)
    for r in range(rows):
        out_ref[cell_rows(r * cols + edge), :] += side[r + 1].astype(F32)


def spatial_weight_kernel(padded_ref, ds_ref, grad_ref):
    rows, cols, cell, middle = ds_ref.shape
    cols = cols - 4
    width = padded_ref.shape[-1]
    grads = ds_ref[:, 2 : cols + 2].reshape(rows * cols * cell, middle)
    for row_tap in range(3):
        for col_tap in range(3):
            window = padded_ref[row_tap : row_tap + rows, col_tap : col_tap + cols]
            tap = 3 * row_tap + col_tap
            grad_ref[tap * width : (tap + 1) * width, :] = lax.dot_general(
                window.reshape(rows * cols * cell, width),
                grads,
                (((0,), (0,)), ((), ())),
                preferred_element_type=F32,
            )


def between_kernel(
    place_ref, valid_ref, grad_ref, up, down, side, t_ref, stats_ref, gb_ref,
    e_ref, msg_ref, *, index,
):
    rows, width = e_ref.shape
    add_halo(place_ref, grad_ref, e_ref, (up, down, side))
    mean, rstd = stats_ref[0:1, :], stats_ref[1:2, :]
    gain, bias = gb_ref[2 * index : 2 * index + 1, :width], gb_ref[2 * index + 1 : 2 * index + 2, :width]

    def one_cell(c, carry):
        bias_sum, gain_sum = carry
        normal = (t_ref[cell_rows(c), :] - mean) * rstd
        value = normal * gain + bias
        sigma = sigmoid(value)
        e = e_ref[cell_rows(c), :] * valid_ref[c] * (sigma * (1.0 + value * (1.0 - sigma)))
        e_ref[cell_rows(c), :] = e
        return (bias_sum + fold8(e), gain_sum + fold8(e * normal))

    start = jnp.zeros((8, width), F32)
    bias_sum, gain_sum = lax.fori_loop(0, rows // CELL, one_cell, (start, start))
    send_sums(bias_sum, gain_sum, msg_ref)


def input_grad_kernel(
    place_ref, valid_ref, grad_ref, up, down, side, dpre_ref, out_ref
):
    add_halo(place_ref, grad_ref, out_ref, (up, down, side))

    def one_cell(c, carry):
        rows = cell_rows(c)
        out_ref[rows, :] = (out_ref[rows, :] + dpre_ref[rows, :]) * valid_ref[c]
        return carry

    lax.fori_loop(0, out_ref.shape[0] // CELL, one_cell, 0)


def temporal_kernel(
    valid_ref, s_ref, msg_ref, gb_ref, wt_ref, columns_ref, t_ref, stats_ref, out_ref, *, index
):
    rows, middle = s_ref.shape
    mean, rstd, count = receive_stats(msg_ref)
    keep_stats(stats_ref, mean, rstd, count)
    gain, bias = gb_ref[2 * index : 2 * index + 1, :], gb_ref[2 * index + 1 : 2 * index + 2, :]

    def one_cell(c, _):
        value = (s_ref[cell_rows(c), :] - mean) * rstd * gain + bias
        inner = value * sigmoid(value) * valid_ref[c]
        columns_ref[cell_rows(c), 0:middle] = earlier_frame(inner).astype(BF16)
        columns_ref[cell_rows(c), middle : 2 * middle] = inner.astype(BF16)
        columns_ref[cell_rows(c), 2 * middle : 3 * middle] = later_frame(inner).astype(BF16)
        return 0

    lax.fori_loop(0, rows // CELL, one_cell, 0)

    def one_block(i, _):
        t_ref[block_rows(i, 320), :] = jnp.dot(
            columns_ref[block_rows(i, 320), :], wt_ref[...], preferred_element_type=F32
        )
        return 0

    lax.fori_loop(0, rows // 320, one_block, 0)
    send_stats(t_ref, valid_ref, out_ref)


def middle_kernel(
    place_ref, valid_ref, t_ref, msg_ref, gb_ref, stats_ref, tile_ref, top, bottom, side, *, index,
):
    width = t_ref.shape[1]
    rows, cols = tile_ref.shape[:2]
    mean, rstd, count = receive_stats(msg_ref)
    keep_stats(stats_ref, mean, rstd, count)
    gain, bias = gb_ref[2 * index : 2 * index + 1, :width], gb_ref[2 * index + 1 : 2 * index + 2, :width]
    for r in range(rows):
        for c in range(cols):
            number = r * cols + c
            value = (t_ref[number * CELL : (number + 1) * CELL, :] - mean) * rstd * gain + bias
            tile_ref[r, c] = (value * sigmoid(value) * valid_ref[number]).astype(BF16)
    write_edges(place_ref, tile_ref, (top, bottom, side))


def top_kernel(
    valid_ref, t_ref, msg_ref, gb_ref, x_ref, cot_ref, stats_ref, out_ref, dpre_ref, msg_out, *, index
):
    rows, width = t_ref.shape
    mean, rstd, count = receive_stats(msg_ref)
    keep_stats(stats_ref, mean, rstd, count)
    gain, bias = gb_ref[2 * index : 2 * index + 1, :width], gb_ref[2 * index + 1 : 2 * index + 2, :width]

    def one_cell(c, carry):
        bias_sum, gain_sum = carry
        normal = (t_ref[cell_rows(c), :] - mean) * rstd
        pre = normal * gain + bias + x_ref[cell_rows(c), :].astype(F32)
        sigma = sigmoid(pre)
        valid = valid_ref[c]
        out_ref[cell_rows(c), :] = pre * sigma * valid
        dpre = cot_ref[cell_rows(c), :].astype(F32) * valid * (sigma * (1.0 + pre * (1.0 - sigma)))
        dpre_ref[cell_rows(c), :] = dpre
        return (bias_sum + fold8(dpre), gain_sum + fold8(dpre * normal))

    start = jnp.zeros((8, width), F32)
    bias_sum, gain_sum = lax.fori_loop(0, rows // CELL, one_cell, (start, start))
    send_sums(bias_sum, gain_sum, msg_out)


def temporal_grad_kernel(
    valid_ref, e_ref, t_ref, tstats_ref, msg_ref, s_ref, sstats_ref, gb_ref, wt_ref,
    dt_ref, en_ref, sums_ref, msg_out, columns_ref, *, index,
):
    rows, width = e_ref.shape
    middle = s_ref.shape[1]
    bias_grad, gain_grad = receive_sums(msg_ref)
    sums_ref[0:1, :] = gain_grad
    sums_ref[1:2, :] = bias_grad
    mean, rstd, count = tstats_ref[0:1, :], tstats_ref[1:2, :], tstats_ref[2:3, :]
    gain = gb_ref[2 * index + 2 : 2 * index + 3, :width]

    def one_cell(c, _):
        normal = (t_ref[cell_rows(c), :] - mean) * rstd
        dt = (rstd * gain) * (
            e_ref[cell_rows(c), :] - valid_ref[c] * ((bias_grad + normal * gain_grad) / count)
        )
        dt_ref[cell_rows(c), :] = dt.astype(BF16)
        columns_ref[cell_rows(c), 0:width] = later_frame(dt).astype(BF16)
        columns_ref[cell_rows(c), width : 2 * width] = dt.astype(BF16)
        columns_ref[cell_rows(c), 2 * width : 3 * width] = earlier_frame(dt).astype(BF16)
        return 0

    lax.fori_loop(0, rows // CELL, one_cell, 0)

    def one_block(i, _):
        total = None
        for tap in range(3):
            term = lax.dot_general(
                columns_ref[block_rows(i, 320), tap * width : (tap + 1) * width],
                wt_ref[tap * middle : (tap + 1) * middle, :],
                (((1,), (1,)), ((), ())),
                preferred_element_type=F32,
            )
            total = term if total is None else total + term
        en_ref[block_rows(i, 320), :] = total
        return 0

    lax.fori_loop(0, rows // 320, one_block, 0)
    mean_s, rstd_s = sstats_ref[0:1, :], sstats_ref[1:2, :]
    gain_s, bias_s = gb_ref[2 * index : 2 * index + 1, :], gb_ref[2 * index + 1 : 2 * index + 2, :]

    def one_mid_cell(c, carry):
        bias_sum, gain_sum = carry
        normal = (s_ref[cell_rows(c), :] - mean_s) * rstd_s
        value = normal * gain_s + bias_s
        sigma = sigmoid(value)
        e = en_ref[cell_rows(c), :] * valid_ref[c] * (sigma * (1.0 + value * (1.0 - sigma)))
        en_ref[cell_rows(c), :] = e
        return (bias_sum + fold8(e), gain_sum + fold8(e * normal))

    start = jnp.zeros((8, middle), F32)
    bias_sum, gain_sum = lax.fori_loop(0, rows // CELL, one_mid_cell, (start, start))
    send_sums(bias_sum, gain_sum, msg_out)


def temporal_weight_kernel(columns_ref, dt_ref, grad_ref):
    middle = columns_ref.shape[1] // 3
    for tap in range(3):
        grad_ref[tap * middle : (tap + 1) * middle, :] = lax.dot_general(
            columns_ref[:, tap * middle : (tap + 1) * middle],
            dt_ref[...],
            (((0,), (0,)), ((), ())),
            preferred_element_type=F32,
        )


def ds_kernel(
    place_ref, valid_ref, en_ref, s_ref, stats_ref, msg_ref, gb_ref, ws_ref,
    sums_ref, ds_ref, top, bottom, side, row_ref, *, index,
):
    rows, cols = ds_ref.shape[0], ds_ref.shape[1] - 4
    bias_grad, gain_grad = receive_sums(msg_ref)
    sums_ref[0:1, :] = gain_grad
    sums_ref[1:2, :] = bias_grad
    mean, rstd, count = stats_ref[0:1, :], stats_ref[1:2, :], stats_ref[2:3, :]
    scale = rstd * gb_ref[2 * index : 2 * index + 1, :]
    for r in range(rows):
        for c in (0, 1, cols + 2, cols + 3):
            ds_ref[r, c] = jnp.zeros(ds_ref.shape[2:], BF16)
        for c in range(cols):
            number = r * cols + c
            block = slice(number * CELL, (number + 1) * CELL)
            normal = (s_ref[block, :] - mean) * rstd
            ds_ref[r, c + 2] = (
                scale
                * (en_ref[block, :] - valid_ref[number] * ((bias_grad + normal * gain_grad) / count))
            ).astype(BF16)
    edge_grads(place_ref, ds_ref, ws_ref, (top, bottom, side), row_ref)


def run(
    kernel, ins, outs, scratch=(), scalars=0, us=1.0, extra=8, loose=(), spec=VMEM, aliases=(), **settings
):
    held = sum(
        math.prod(x.shape) * jnp.dtype(x.dtype).itemsize
        for x in scratch
        if x.memory_space == pltpu.VMEM
    )
    return pl.pallas_call(
        functools.partial(kernel, **settings),
        out_shape=[
            jax.ShapeDtypeStruct(shape, dtype) if i in loose else pltpu.VMEM(shape, dtype)
            for i, (shape, dtype) in enumerate(outs)
        ],
        in_specs=[SMEM] * scalars + [spec] * (len(ins) - scalars),
        out_specs=[VMEM] * len(outs),
        scratch_shapes=list(scratch),
        input_output_aliases=dict(aliases),
        cost_estimate=pl.CostEstimate(
            flops=int(us * 1.1e9), bytes_accessed=1000, transcendentals=0
        ),
        compiler_params=pltpu.CompilerParams(vmem_limit_bytes=held + extra * 2**20),
    )(*ins)


def ranks_of_pieces(owner_ids, devices):
    block = 64
    onehot = (owner_ids.reshape(-1, block, 1) == jnp.arange(devices, dtype=jnp.int32)).astype(BF16)
    earlier = jnp.tril(jnp.ones((block, block), BF16), -1)
    within = jnp.einsum("ij,bjd->bid", earlier, onehot, preferred_element_type=F32)
    sums = jnp.sum(onehot.astype(F32), axis=1)
    blocks = jnp.tril(jnp.ones((sums.shape[0],) * 2, F32), -1)
    before = jnp.sum(blocks[:, :, None] * sums[None], axis=1)
    ranking = jnp.sum(onehot.astype(F32) * (within + before[:, None, :]), axis=-1)
    return ranking.reshape(-1).astype(jnp.int32)


def moved_by(step, size):
    return [(i, (i + step) % size) for i in range(size)]


def mirrored(bit, size):
    return [(i, i ^ bit) for i in range(size)]


def gather_batch(own):
    batches = lax.axis_size("batch")
    return [own] + [lax.ppermute(own, "batch", moved_by(k, batches)) for k in range(1, batches)]


def gather_chips_first(steps):
    heights, half = lax.axis_size("ha"), len(steps) // 2
    one, two = jnp.concatenate(steps[:half]), jnp.concatenate(steps[half:])
    one = jnp.concatenate([one, lax.ppermute(one, "ha", mirrored(1, heights))])
    two = jnp.concatenate([two, lax.ppermute(two, "ha", mirrored(2, heights))])
    return one, two


def gather_chips_second(one, two, beside):
    heights = lax.axis_size("ha")
    across = mirrored(1, 2)
    one_next = lax.ppermute(one, "ha", mirrored(2, heights))
    two_next = lax.ppermute(two, "ha", mirrored(1, heights))
    others = [lax.ppermute(one, "wa", across), lax.ppermute(two, "wa", across)]
    one_next, two_next, beside = together(one_next, two_next, beside)
    others = [
        others[0],
        lax.ppermute(one_next, "wa", across),
        others[1],
        lax.ppermute(two_next, "wa", across),
    ]
    return [one, one_next, two, two_next] + others, beside


def part_position(owner_ids, place):
    batches, heights, cores = (lax.axis_size(axis) for axis in AXES)
    z, h, w = place
    core = (owner_ids % cores) ^ w
    turn = (owner_ids // cores % heights) ^ h
    step = (z - owner_ids // (cores * heights)) % batches
    half = batches // 2
    swapped = jnp.where(turn == 1, 2, jnp.where(turn == 2, 1, turn))
    block = jnp.where(
        step < half, turn * half + step, heights * half + swapped * half + step - half
    )
    return core * batches * heights + block


def target_position(owner_ids, place):
    batches, heights, cores = (lax.axis_size(axis) for axis in AXES)
    z, h, w = place
    core = (owner_ids % cores) ^ w
    turn = (owner_ids // cores % heights) ^ h
    step = (owner_ids // (cores * heights) - z) % batches
    return (core * heights + turn) * batches + step


def add_low(a, b):
    return (a.astype(F32) + b.astype(F32)).astype(BF16)


def sum_cores(packed):
    sent, kept = packed
    return [kept, lax.ppermute(sent, "wa", mirrored(1, 2))]


def added(terms, block, part, rows):
    half = rows // 2
    start = block * rows + part * half
    return add_low(*[t[start : start + half] for t in terms])


def move_chips_first(terms, rows):
    heights = lax.axis_size("ha")
    one = jnp.stack([added(terms, 1, 0, rows), added(terms, 3, 0, rows)])
    two = jnp.stack([added(terms, 2, 1, rows), added(terms, 3, 1, rows)])
    return (
        lax.ppermute(one, "ha", mirrored(1, heights)),
        lax.ppermute(two, "ha", mirrored(2, heights)),
    )


def add_chips_first(terms, moved, rows):
    one, two = moved
    return [
        add_low(added(terms, 0, 0, rows), one[0]),
        add_low(added(terms, 2, 0, rows), one[1]),
        add_low(added(terms, 0, 1, rows), two[0]),
        add_low(added(terms, 1, 1, rows), two[1]),
    ]


def move_chips_second(sums):
    heights = lax.axis_size("ha")
    return (
        lax.ppermute(sums[1], "ha", mirrored(2, heights)),
        lax.ppermute(sums[3], "ha", mirrored(1, heights)),
    )


def add_chips_second(sums, moved):
    own = jnp.concatenate([add_low(sums[0], moved[0]), add_low(sums[2], moved[1])])
    return own.reshape(lax.axis_size("batch"), -1, LANES)


def move_batch(own):
    batches = own.shape[0]
    return [lax.ppermute(own[k], "batch", moved_by(k, batches)) for k in range(1, batches)]


def add_batch(own, moved):
    total = own[0].astype(F32)
    for block in moved:
        total = total + block.astype(F32)
    return total


def scatter_sums(packed, rows):
    terms = sum_cores(packed)
    sums = add_chips_first(terms, move_chips_first(terms, rows), rows)
    own = add_chips_second(sums, move_chips_second(sums))
    return add_batch(own, move_batch(own))


def together(*values):
    return lax.optimization_barrier(values)


def exchange(message):
    return lax.all_to_all(message, AXES, 0, 0, tiled=True)


def swap_side(side):
    return lax.ppermute(side, "wa", mirrored(1, 2))


def swap_rows(top, bottom):
    count = lax.axis_size("ha")
    forward = [(i, i + 1) for i in range(count - 1)]
    backward = [(i + 1, i) for i in range(count - 1)]
    return [lax.ppermute(bottom, "ha", forward), lax.ppermute(top, "ha", backward)]


def swap_values(edges, side):
    top, bottom, _ = edges
    rows = swap_rows(
        jnp.concatenate([top, side[:1]]), jnp.concatenate([bottom, side[-1:]])
    )
    return rows + [side]


def with_ends(at_edge, edges, side):
    top, bottom, _ = edges
    return [
        jnp.where(at_edge[:, None, None], add_low(row, side[end][None]), row)
        for row, end in ((top, 0), (bottom, -1))
    ]


def per_device(
    block_input,
    cotangent,
    frame_sides,
    owner_list,
    master_slots,
    first_slots,
    second_slots,
    norm_gains,
    norm_biases,
    norm_first,
    norm_second,
):
    clip_count, frames, tile_rows, tile_cols, width = block_input.shape
    devices = lax.axis_size(AXES)
    slot_count, piece_len = master_slots.shape
    middle = norm_gains.shape[0] // 2 - width
    middle_pad = -(-middle // LANES) * LANES
    rows = clip_count * frames * tile_rows * tile_cols

    low_slots = master_slots.astype(BF16).reshape(slot_count * PIECE_ROWS, LANES)

    steps = gather_batch(low_slots)

    own_side = frame_sides[0]
    row_ids = lax.axis_index("ha") * tile_rows + jnp.arange(tile_rows, dtype=jnp.int32)
    col_ids = lax.axis_index("wa") * tile_cols + jnp.arange(tile_cols, dtype=jnp.int32)
    grid_rows = tile_rows * lax.axis_size("ha")
    grid_cols = tile_cols * lax.axis_size("wa")
    valid = (
        (row_ids[:, None] >= grid_rows - own_side) & (col_ids[None, :] >= grid_cols - own_side)
    ).astype(F32)
    valid_flat = valid.reshape(-1)
    place = lax.axis_index("wa").reshape(1)
    def to_tile(array):
        return jnp.transpose(array, (2, 3, 1, 0, 4)).reshape(tile_rows, tile_cols, CELL, width)

    x_tile = to_tile(block_input) * valid[:, :, None, None].astype(BF16)
    edge = jnp.where(place[0] == 0, tile_cols - 1, 0)
    x_side = lax.dynamic_index_in_dim(x_tile, edge, axis=1, keepdims=False)
    x_halo = swap_values((x_tile[0], x_tile[-1], x_side), swap_side(x_side))
    steps, x_tile, x_halo, cotangent, owner_list, norm_gains, norm_biases = together(
        steps, x_tile, x_halo, cotangent, owner_list, norm_gains, norm_biases
    )
    one, two = gather_chips_first(steps)

    cot_tile = to_tile(cotangent)
    owner_ids = owner_list[:, 0]
    ranking = ranks_of_pieces(owner_ids, devices)
    here = [lax.axis_index(axis) for axis in AXES]
    slot_index = (part_position(owner_ids, here) * slot_count + ranking) * PIECE_ROWS
    half = owner_list.shape[0] // 2
    kept = min(slot_count, int(slot_count / 2 + 1.7 * math.sqrt(slot_count)))
    rest = max(slot_count - kept, 1)
    target = target_position(owner_ids, here)
    fits = jnp.all(ranking[:half] < kept)

    def spare_rows(slots):
        return -(-(devices // 2 * slots + 1) * PIECE_ROWS // 128) * 128

    def by_core(number, rank, slots, here):
        spare = devices // 2 * slots * PIECE_ROWS
        place = (number * slots + rank) * PIECE_ROWS
        return (
            jnp.where(here & (place >= spare), place - spare, spare),
            jnp.where(here & (place < spare), place, spare),
        )

    late_two = fits & (ranking[half:] < kept)
    places1 = by_core(target[:half], ranking[:half], kept, fits)
    places2 = by_core(target[half:], ranking[half:], kept, late_two) + by_core(
        target[half:], ranking[half:] - (slot_count - rest), rest, fits & ~late_two
    )

    bounds = [0, middle, middle + width, 2 * middle + width, 2 * middle + 2 * width]
    gb = []
    for i in range(4):
        for vector in (norm_gains, norm_biases):
            part = vector[bounds[i] : bounds[i + 1]]
            gb.append(jnp.pad(part, (0, middle_pad - part.shape[0])))
    gb = jnp.stack(gb)

    at_edge = jnp.arange(tile_cols) == edge
    prepared = (at_edge, x_tile, x_halo, cot_tile, valid_flat, gb, slot_index, places1, places2, fits)
    parts, prepared = gather_chips_second(one, two, prepared)
    at_edge, x_tile, x_halo, cot_tile, valid_flat, gb, slot_index, places1, places2, fits = prepared

    tap_rows = 9 * width
    stage = [pltpu.VMEM((UNROLL, 144, LANES), F32), pltpu.VMEM((UNROLL, 5, 32, LANES), F32)]
    weight_shapes = [((tap_rows, middle_pad), BF16), ((3 * middle_pad, width), BF16)]
    (all_weights,) = run(
        gather_weights_kernel,
        parts,
        [((devices * slot_count * PIECE_ROWS, LANES), BF16)],
        [pltpu.SemaphoreType.DMA((len(parts),))],
        us=3.0,
        spec=pl.BlockSpec(memory_space=pl.ANY),
    )

    def unpack(all_weights, unit):
        return run(
            unpack_weights_kernel,
            [slot_index, all_weights],
            weight_shapes,
            stage,
            1,
            4.3,
            base=unit * (owner_list.shape[0] // 2),
        )

    tile_shape = (tile_rows, tile_cols, CELL, width)
    padded_tile = (tile_rows + 2, tile_cols + 2, CELL, width)
    ds_shape = (tile_rows, tile_cols + 4, CELL, middle_pad)
    stats_mid = (devices, 1, 2 * middle_pad + LANES)
    stats_wide = (devices, 1, 2 * width + LANES)

    def edge_shapes(lanes, beside=0):
        row, col = (tile_cols, CELL, lanes), (tile_rows + beside, CELL, lanes)
        return [(row, BF16), (row, BF16), (col, BF16)]

    def unit_forward(tile, halo, ws, wt, index):
        padded, s, msg = run(
            spatial_kernel,
            [place, valid_flat, tile, *halo, ws],
            [(padded_tile, BF16), ((rows, middle_pad), F32), (stats_mid, F32)],
            us=5.5,
            scalars=2,
        )
        columns, t, s_stats, msg = run(
            temporal_kernel,
            [valid_flat, s, exchange(msg), gb, wt],
            [
                ((rows, 3 * middle_pad), BF16),
                ((rows, width), F32),
                ((8, middle_pad), F32),
                (stats_wide, F32),
            ],
            scalars=1,
            us=4.2,
            index=index,
        )
        return padded, s, s_stats, columns, t, exchange(msg)

    ws1, wt1 = unpack(all_weights, 0)
    padded1, s1, s_stats1, columns1, t1, msg = unit_forward(x_tile, x_halo, ws1, wt1, 0)
    t_stats1, y_tile, *edges = run(
        middle_kernel,
        [place, valid_flat, t1, msg, gb],
        [((8, width), F32), (tile_shape, BF16)] + edge_shapes(width),
        scalars=2,
        index=1,
    )
    y_in, all_weights = together(swap_side(edges[2]), all_weights)
    halo = swap_values(edges, y_in)
    ws2, wt2 = unpack(all_weights, 1)
    ws2, wt2, halo = together(ws2, wt2, halo)
    padded2, s2, s_stats2, columns2, t2, msg = unit_forward(y_tile, halo, ws2, wt2, 2)
    t_stats2, block_output, dpre, msg = run(
        top_kernel,
        [valid_flat, t2, msg, gb, x_tile.reshape(rows, width), cot_tile.reshape(rows, width)],
        [((8, width), F32), ((rows, width), F32), ((rows, width), F32), ((devices, 1, 2 * width), F32)],
        scalars=1,
        loose=(1,),
        index=3,
    )

    batch_rows = lax.axis_size("batch") * PIECE_ROWS

    def pack(grads, places, slots, begun=()):
        shapes = [((spare_rows(n), LANES), BF16) for n in slots for _ in range(2)]
        first = len(places) + 2
        return run(
            pack_grads_kernel,
            [*places, *grads, *begun],
            shapes,
            stage,
            scalars=len(places),
            us=0.1,
            aliases={first + i: i for i in range(len(begun))},
            places=len(places),
            begun=len(begun),
        )

    def unit_backward(e, msg, t, t_stats, s, s_stats, columns, padded, ws, wt, index, aside=None):
        dt, en, t_sums, msg = run(
            temporal_grad_kernel,
            [valid_flat, e, t, t_stats, exchange(msg), s, s_stats, gb, wt],
            [
                ((rows, width), BF16),
                ((rows, middle_pad), F32),
                ((2, width), F32),
                ((devices, 1, 2 * middle_pad), F32),
            ],
            [pltpu.VMEM((rows, 3 * width), BF16)],
            scalars=1,
            us=4.5,
            index=index,
        )
        if aside is not None:
            msg, aside = together(msg, sum_cores(aside))
        msg = exchange(msg)
        if aside is not None:
            msg, aside = together(msg, aside)
            moved = move_chips_first(aside, batch_rows * rest)
        s_sums, ds, *edges = run(
            ds_kernel,
            [place, valid_flat, en, s, s_stats, msg, gb, ws],
            [((2, middle_pad), F32), (ds_shape, BF16)] + edge_shapes(width, 2),
            [pltpu.VMEM((tile_cols + 1, CELL, width), BF16)],
            scalars=2,
            us=4.0,
            index=index,
        )
        edges, columns, dt = together(edges, columns, dt)
        (wt_grad,) = run(temporal_weight_kernel, [columns, dt], [((3 * middle_pad, width), F32)], us=0.1)
        (ws_grad,) = run(spatial_weight_kernel, [padded, ds], [((tap_rows, middle_pad), F32)], us=0.1)
        return ds, edges, (ws_grad, wt_grad), s_sums, t_sums, aside and (aside, moved)

    def inner_grad(ds, ws):
        return run(spatial_grad_kernel, [ds, ws], [((rows, width), F32)], us=0.1)[0]

    ds, edges, grads2, s_sums2, t_sums2, _ = unit_backward(
        dpre, msg, t2, t_stats2, s2, s_stats2, columns2, padded2, ws2, wt2, 2
    )
    side = swap_side(edges[2])
    halo = swap_rows(*with_ends(at_edge, edges, side)) + [side]
    inner, halo, grads2 = together(inner_grad(ds, ws2), halo, grads2)
    *begun, sent2, kept2 = pack(grads2, places2, (kept, rest))
    packed2 = sent2, kept2
    inner, packed2 = together(inner, packed2)
    e1, msg = run(
        between_kernel,
        [place, valid_flat, inner, *halo, t1, t_stats1, gb],
        [((rows, width), F32), ((devices, 1, 2 * width), F32)],
        scalars=2,
        us=2.0,
        index=1,
    )
    ds, edges, grads1, s_sums1, t_sums1, moving2 = unit_backward(
        e1, msg, t1, t_stats1, s1, s_stats1, columns1, padded1, ws1, wt1, 0, packed2
    )
    packed1, moving2, edges, ds = together(
        pack(grads1, places1, (kept,), begun), moving2, edges, ds
    )
    first2 = add_chips_first(*moving2, batch_rows * rest)
    side, ds = together(swap_side(edges[2]), ds)
    terms1, moved2, side, inner, first2 = together(
        sum_cores(packed1), move_chips_second(first2), side, inner_grad(ds, ws1), first2
    )
    own2 = add_chips_second(first2, moved2)
    moved1, moved2, ends, block_output, terms1, own2 = together(
        move_chips_first(terms1, batch_rows * kept),
        move_batch(own2),
        with_ends(at_edge, edges, side),
        block_output,
        terms1,
        own2,
    )
    first1 = add_chips_first(terms1, moved1, batch_rows * kept)
    sums = (own2, moved2, s_sums1, t_sums1, s_sums2, t_sums2)
    moved1, ends, sums, first1 = together(move_chips_second(first1), ends, sums, first1)
    own2, moved2, s_sums1, t_sums1, s_sums2, t_sums2 = sums
    own1 = add_chips_second(first1, moved1)
    moved1, rows_in, own1 = together(move_batch(own1), swap_rows(*ends), own1)
    (input_grad,) = run(
        input_grad_kernel,
        [place, valid_flat, inner, *rows_in, side, dpre],
        [((rows, width), F32)],
        scalars=2,
        us=2.0,
        loose=(0,),
    )
    sums1, sums2 = add_batch(own1, moved1), add_batch(own2, moved2)

    def joined(first, last):
        after, before = [(slot_count - n) * PIECE_ROWS for n in (kept, rest)]
        return jnp.pad(first, ((0, after), (0, 0))) + jnp.pad(last, ((before, 0), (0, 0)))

    def whole(grads1, grads2):
        packed = [
            pack(grads, by_core(target[part], ranking[part], slot_count, True), (slot_count,))
            for grads, part in ((grads1, slice(0, half)), (grads2, slice(half, None)))
        ]
        return scatter_sums([a + b for a, b in zip(*packed)], batch_rows * slot_count)

    if kept == slot_count:
        grad_mine = joined(sums1, sums2)
    else:
        grad_mine = lax.cond(
            fits,
            lambda early, late, *_: joined(early, late),
            lambda early, late, ones, twos: whole(ones, twos),
            sums1,
            sums2,
            grads1,
            grads2,
        )

    def from_tile(array):
        array = array.reshape(tile_rows, tile_cols, frames, clip_count, width)
        return jnp.transpose(array, (3, 2, 0, 1, 4))

    grad_mine = grad_mine.reshape(slot_count, piece_len)
    correction = 1.0 - 0.5**STEP
    step_rate = 1.8 / math.sqrt(9.0 * width)
    first_new = 0.5 * first_slots + 0.5 * grad_mine
    second_new = 0.5 * second_slots + 0.5 * grad_mine * grad_mine
    master_new = master_slots - step_rate * (
        first_new / correction / (jnp.sqrt(second_new / correction) + ADAM_EPSILON)
        + DECAY_RATE * master_slots
    )
    weight_copy = master_new.astype(BF16)
    norm_grad = jnp.concatenate([s_sums1[:, :middle], t_sums1, s_sums2[:, :middle], t_sums2], axis=1)
    norm_pair = jnp.stack([norm_gains, norm_biases])
    norm_first_new = 0.5 * norm_first + 0.5 * norm_grad
    norm_second_new = 0.5 * norm_second + 0.5 * norm_grad * norm_grad
    norm_new = norm_pair - NORM_RATE * (norm_first_new / correction) / (
        jnp.sqrt(norm_second_new / correction) + ADAM_EPSILON
    )
    return (
        from_tile(block_output),
        from_tile(input_grad),
        master_new,
        first_new,
        second_new,
        weight_copy,
        norm_first_new,
        norm_second_new,
        norm_new,
    )


def solution(mesh):
    wide = P("batch", None, "ha", "wa", None)
    owned = P(AXES, None)
    return jax.shard_map(
        per_device,
        mesh=mesh,
        in_specs=(wide, wide, P("batch"), P(), owned, owned, owned, P(), P(), P(), P()),
        out_specs=(wide, wide, owned, owned, owned, owned, P(), P(), P()),
        check_vma=False,
    )
```

```python
import functools
import math

import jax
import jax.numpy as jnp
from jax import lax
from jax.experimental import pallas as pl
from jax.experimental.pallas import tpu as pltpu
from jax.sharding import PartitionSpec as P

STEP = 5
EPSILON = 1e-05
ADAM_EPSILON = 1e-08
DECAY_RATE = 0.1
NORM_RATE = 0.3

AXES = ("batch", "ha", "wa")
F32 = jnp.float32
BF16 = jnp.bfloat16
VMEM = pl.BlockSpec(memory_space=pltpu.VMEM)
SMEM = pl.BlockSpec(memory_space=pltpu.SMEM)
CELL = 64
LANES = 128
PIECE_ROWS = 16


def sigmoid(v):
    return 1.0 / (1.0 + jnp.exp(-v))


def cell_rows(index, count=1):
    return pl.ds(pl.multiple_of(index * CELL, CELL), count * CELL)


def block_rows(index, size):
    return pl.ds(pl.multiple_of(index * size, size), size)


def fold8(block):
    return jnp.sum(block.reshape(-1, 8, block.shape[-1]), axis=0)


def widen(lane_block, width):
    return jnp.concatenate([lane_block] * (width // LANES), axis=1)


def valid_rows(valid_ref, cells):
    total = valid_ref[0]
    for cell in range(1, cells):
        total = total + valid_ref[cell]
    return total * CELL


def send_stats(values_ref, valid_ref, msg_ref):
    rows, width = values_ref.shape
    cells = rows // CELL
    count = valid_rows(valid_ref, cells)

    def add(cell, total):
        return total + valid_ref[cell] * fold8(values_ref[cell_rows(cell), :])

    total = lax.fori_loop(0, cells, add, jnp.zeros((8, width), F32))
    total = jnp.sum(total, axis=0, keepdims=True)
    mean = total / jnp.maximum(jnp.full((1, width), count, F32), 1.0)

    def add_squares(cell, squares):
        centered = values_ref[cell_rows(cell), :] - mean
        return squares + valid_ref[cell] * fold8(centered * centered)

    squares = lax.fori_loop(0, cells, add_squares, jnp.zeros((8, width), F32))
    squares = jnp.sum(squares, axis=0, keepdims=True)
    message = jnp.concatenate([total, squares, jnp.full((1, LANES), count, F32)], axis=1)
    msg_ref[...] = jnp.broadcast_to(message[None], msg_ref.shape)


def receive_stats(msg_ref):
    devices, _, length = msg_ref.shape
    width = (length - LANES) // 2

    def add(i, carry):
        total, count = carry
        return (total + msg_ref[i, :, :width], count + msg_ref[i, :, 2 * width :])

    total, count = lax.fori_loop(
        0, devices, add, (jnp.zeros((1, width), F32), jnp.zeros((1, LANES), F32)), unroll=4
    )
    count = widen(count, width)
    mean = total / count

    def add_squares(i, squares):
        own = widen(msg_ref[i, :, 2 * width :], width)
        offset = msg_ref[i, :, :width] / jnp.maximum(own, 1.0) - mean
        return squares + msg_ref[i, :, width : 2 * width] + own * offset * offset

    squares = lax.fori_loop(0, devices, add_squares, jnp.zeros((1, width), F32), unroll=4)
    return mean, lax.rsqrt(squares / count + EPSILON), count


def keep_stats(stats_ref, mean, rstd, count):
    stats_ref[0:1, :] = mean
    stats_ref[1:2, :] = rstd
    stats_ref[2:3, :] = count


def receive_sums(msg_ref):
    devices, _, length = msg_ref.shape
    total = lax.fori_loop(
        0, devices, lambda i, t: t + msg_ref[i], jnp.zeros((1, length), F32), unroll=4
    )
    return total[:, : length // 2], total[:, length // 2 :]


def send_sums(bias, gain, msg_ref):
    message = jnp.concatenate(
        [jnp.sum(bias, axis=0, keepdims=True), jnp.sum(gain, axis=0, keepdims=True)], axis=1
    )
    msg_ref[...] = jnp.broadcast_to(message[None], msg_ref.shape)


def later_frame(block):
    return jnp.concatenate([block[8:], jnp.zeros((8, block.shape[1]), block.dtype)], axis=0)


def earlier_frame(block):
    return jnp.concatenate([jnp.zeros((8, block.shape[1]), block.dtype), block[:-8]], axis=0)


UNROLL = 12


def gather_weights_kernel(*refs):
    parts, all_ref, sems = refs[:-2], refs[-2], refs[-1]
    rows = parts[0].shape[0]
    copies = [
        pltpu.make_async_copy(part, all_ref.at[i * rows : (i + 1) * rows, :], sems.at[i])
        for i, part in enumerate(parts)
    ]
    for copy in copies:
        copy.start()
    for copy in copies:
        copy.wait()


def unpack_weights_kernel(slot_ref, all_ref, ws_ref, wt_ref, stage, turn, *, base):
    low = lax.broadcasted_iota(jnp.int32, (8, LANES), 1) < 64
    zero = jnp.zeros((8, LANES), F32)
    spatial_groups = ws_ref.shape[0] // 32

    def load_piece(number):
        start = pl.multiple_of(slot_ref[number], PIECE_ROWS)
        return all_ref[pl.ds(start, PIECE_ROWS), :].astype(F32)

    def spatial_groups_at(k, _):
        first = k * UNROLL
        for u in range(UNROLL):
            for q in range(9):
                stage[u, 16 * q : 16 * q + 16, :] = load_piece(base + 9 * (first + u) + q)
        for u in range(UNROLL):
            for i in range(2):
                a = [stage[u, pl.ds(72 * i + j, 8, stride=9), :] for j in range(9)]
                r = [pltpu.roll(a[4 + j], 64, axis=1) for j in range(5)]
                even = a[:4] + [jnp.where(low, a[4], zero)]
                odd = [jnp.where(low, r[j], r[j + 1]) for j in range(4)]
                odd += [jnp.where(low, r[4], zero)]
                for j in range(5):
                    turn[u, j, pl.ds(16 * i, 8, stride=2), :] = even[j]
                    turn[u, j, pl.ds(16 * i + 1, 8, stride=2), :] = odd[j]
        for u in range(UNROLL):
            rows = block_rows(first + u, 32)
            for j in range(5):
                ws_ref[rows, LANES * j : LANES * (j + 1)] = turn[u, j].astype(BF16)
        return 0

    lax.fori_loop(0, spatial_groups // UNROLL, spatial_groups_at, 0)
    temporal_base = base + 9 * spatial_groups
    padded = wt_ref.shape[0] // 3
    pairs = (9 * spatial_groups) // 3 // 6
    for tap in range(3):

        def temporal_pairs(k, _):
            for u in range(UNROLL):
                first = temporal_base + tap * 2 * pairs + 2 * (k * UNROLL + u)
                stage[u, 0:16, :] = load_piece(first)
                stage[u, 16:32, :] = load_piece(first + 1)
            for u in range(UNROLL):
                start = tap * padded + (k * UNROLL + u) * 16
                rows = pl.ds(pl.multiple_of(start, 16), 16)
                for h in range(2):
                    half = stage[u, pl.ds(h, 16, stride=2), :]
                    wt_ref[rows, LANES * h : LANES * (h + 1)] = half.astype(BF16)
            return 0

        lax.fori_loop(0, pairs // UNROLL, temporal_pairs, 0)
        wt_ref[tap * padded + 16 * pairs : (tap + 1) * padded, :] = jnp.zeros(
            (padded - 16 * pairs, wt_ref.shape[1]), BF16
        )


def pack_grads_kernel(*refs, places, begun):
    at_refs, (spatial, temporal) = refs[:places], refs[places : places + 2]
    out_refs = refs[places + 2 + begun : -2]
    stage, turn = refs[-2:]
    low = lax.broadcasted_iota(jnp.int32, (8, LANES), 1) < 64
    spatial_groups = spatial.shape[0] // 32
    padded = temporal.shape[0] // 3
    pairs = (9 * spatial_groups) // 3 // 6

    for out_ref in out_refs[begun:]:
        out_ref[...] = jnp.zeros(out_ref.shape, BF16)

    def store_piece(number, rows16):
        low_rows = rows16.astype(BF16)
        for out_ref, at_ref in zip(out_refs, at_refs):
            start = pl.multiple_of(at_ref[number], PIECE_ROWS)
            out_ref[pl.ds(start, PIECE_ROWS), :] = low_rows

    def spatial_groups_at(k, _):
        first = k * UNROLL
        for u in range(UNROLL):
            rows = block_rows(first + u, 32)
            for j in range(5):
                turn[u, j] = spatial[rows, LANES * j : LANES * (j + 1)]
        for u in range(UNROLL):
            for i in range(2):
                even = [turn[u, j, pl.ds(16 * i, 8, stride=2), :] for j in range(5)]
                odd = [turn[u, j, pl.ds(16 * i + 1, 8, stride=2), :] for j in range(5)]
                r = [pltpu.roll(odd[j], 64, axis=1) for j in range(5)]
                flat = even[:4] + [jnp.where(low, even[4], r[0])]
                flat += [jnp.where(low, r[j], r[j + 1]) for j in range(4)]
                for j in range(9):
                    stage[u, pl.ds(72 * i + j, 8, stride=9), :] = flat[j]
        for u in range(UNROLL):
            for q in range(9):
                store_piece(9 * (first + u) + q, stage[u, 16 * q : 16 * q + 16, :])
        return 0

    lax.fori_loop(0, spatial_groups // UNROLL, spatial_groups_at, 0)
    base = 9 * spatial_groups
    for tap in range(3):

        def temporal_pairs(k, _):
            for u in range(UNROLL):
                start = tap * padded + (k * UNROLL + u) * 16
                rows = pl.ds(pl.multiple_of(start, 16), 16)
                for h in range(2):
                    stage[u, pl.ds(h, 16, stride=2), :] = temporal[
                        rows, LANES * h : LANES * (h + 1)
                    ]
            for u in range(UNROLL):
                first = base + tap * 2 * pairs + 2 * (k * UNROLL + u)
                store_piece(first, stage[u, 0:16, :])
                store_piece(first + 1, stage[u, 16:32, :])
            return 0

        lax.fori_loop(0, pairs // UNROLL, temporal_pairs, 0)


def fill_padded(place_ref, padded_ref, tile_ref, halo_refs):
    up, down, side = halo_refs
    rows, cols = tile_ref.shape[:2]
    padded_ref[1 : rows + 1, 1 : cols + 1] = tile_ref[...]
    padded_ref[0, 1 : cols + 1] = up[:cols]
    padded_ref[rows + 1, 1 : cols + 1] = down[:cols]
    for core in range(2):
        near, far = (cols + 1, 0) if core == 0 else (0, cols + 1)

        @pl.when(place_ref[0] == core)
        def _():
            padded_ref[1 : rows + 1, near] = side[...]
            padded_ref[0, near] = up[cols]
            padded_ref[rows + 1, near] = down[cols]
            padded_ref[:, far] = jnp.zeros((rows + 2,) + tile_ref.shape[2:], BF16)


def write_edges(place_ref, tile_ref, edge_refs):
    top, bottom, side = edge_refs
    rows, cols = tile_ref.shape[:2]
    top[...] = tile_ref[0]
    bottom[...] = tile_ref[rows - 1]
    side[...] = tile_ref[:, jnp.where(place_ref[0] == 0, cols - 1, 0)]


def spatial_kernel(
    place_ref, valid_ref, tile_ref, up, down, side, ws_ref, padded_ref, s_ref, msg_ref
):
    rows, cols, cell, width = tile_ref.shape
    fill_padded(place_ref, padded_ref, tile_ref, (up, down, side))

    def one_row(r, _):
        windows = []
        for row_tap in range(3):
            for col_tap in range(3):
                window = padded_ref[r + row_tap, col_tap : col_tap + cols]
                windows.append(window.reshape(cols * cell, width))
        s_ref[block_rows(r, cols * cell), :] = jnp.dot(
            jnp.concatenate(windows, axis=1), ws_ref[...], preferred_element_type=F32
        )
        return 0

    lax.fori_loop(0, rows, one_row, 0)
    send_stats(s_ref, valid_ref, msg_ref)


def weight_back(window, ws_ref, tap, width):
    return lax.dot_general(
        window.reshape(-1, window.shape[-1]),
        ws_ref[block_rows(tap, width), :],
        (((1,), (1,)), ((), ())),
        preferred_element_type=F32,
    )


def edge_grads(place_ref, ds_ref, ws_ref, edge_refs, row_ref):
    top, bottom, side = edge_refs
    width = top.shape[-1]
    cols, cell = top.shape[:2]
    rows = side.shape[0] - 2
    core = place_ref[0]
    for row, row_tap, out, corner in ((0, 0, top, 0), (rows - 1, 2, bottom, rows + 1)):
        total = None
        for col_tap in range(3):
            window = ds_ref[row, pl.ds(3 - core - col_tap, cols + 1)]
            term = weight_back(window, ws_ref, 3 * row_tap + col_tap, width)
            total = term if total is None else total + term
        row_ref[...] = total.astype(BF16).reshape(row_ref.shape)
        out[...] = row_ref[pl.ds(core, cols)]
        side[corner] = row_ref[cols * (1 - core)]
    column = ds_ref[:, jnp.where(core == 0, cols + 1, 2)]
    above, level, below = [
        weight_back(column, ws_ref, 3 * row_tap + 2 - 2 * core, width) for row_tap in range(3)
    ]
    empty = jnp.zeros((cell, width), F32)
    total = level + jnp.concatenate([above[cell:], empty]) + jnp.concatenate([empty, below[:-cell]])
    side[1 : rows + 1] = total.astype(BF16).reshape(rows, cell, width)


def spatial_grad_kernel(ds_ref, ws_ref, grad_ref):
    rows, cols, cell = ds_ref.shape[0], ds_ref.shape[1] - 4, ds_ref.shape[2]
    width = grad_ref.shape[1]
    for row in range(rows):
        total = None
        for row_tap in range(3):
            if not 0 <= row + 1 - row_tap < rows:
                continue
            for col_tap in range(3):
                window = ds_ref[row + 1 - row_tap, 3 - col_tap : 3 - col_tap + cols]
                term = weight_back(window, ws_ref, 3 * row_tap + col_tap, width)
                total = term if total is None else total + term
        grad_ref[row * cols * cell : (row + 1) * cols * cell, :] = total


def add_halo(place_ref, grad_ref, out_ref, halo_refs):
    up, down, side = halo_refs
    rows, cols = side.shape[0] - 2, up.shape[0]
    edge = jnp.where(place_ref[0] == 0, cols - 1, 0)
    out_ref[...] = grad_ref[...]
    last = (rows - 1) * cols
    for c in range(cols):
        out_ref[cell_rows(c), :] += up[c].astype(F32)
        out_ref[cell_rows(last + c), :] += down[c].astype(F32)
    for r in range(rows):
        out_ref[cell_rows(r * cols + edge), :] += side[r + 1].astype(F32)


def spatial_weight_kernel(padded_ref, ds_ref, grad_ref):
    rows, cols, cell, middle = ds_ref.shape
    cols = cols - 4
    width = padded_ref.shape[-1]
    grads = ds_ref[:, 2 : cols + 2].reshape(rows * cols * cell, middle)
    for row_tap in range(3):
        for col_tap in range(3):
            window = padded_ref[row_tap : row_tap + rows, col_tap : col_tap + cols]
            tap = 3 * row_tap + col_tap
            grad_ref[tap * width : (tap + 1) * width, :] = lax.dot_general(
                window.reshape(rows * cols * cell, width),
                grads,
                (((0,), (0,)), ((), ())),
                preferred_element_type=F32,
            )


def between_kernel(
    place_ref, valid_ref, grad_ref, up, down, side, t_ref, stats_ref, gb_ref,
    e_ref, msg_ref, *, index,
):
    rows, width = e_ref.shape
    add_halo(place_ref, grad_ref, e_ref, (up, down, side))
    mean, rstd = stats_ref[0:1, :], stats_ref[1:2, :]
    gain, bias = gb_ref[2 * index : 2 * index + 1, :width], gb_ref[2 * index + 1 : 2 * index + 2, :width]

    def one_cell(c, carry):
        bias_sum, gain_sum = carry
        normal = (t_ref[cell_rows(c), :] - mean) * rstd
        value = normal * gain + bias
        sigma = sigmoid(value)
        e = e_ref[cell_rows(c), :] * valid_ref[c] * (sigma * (1.0 + value * (1.0 - sigma)))
        e_ref[cell_rows(c), :] = e
        return (bias_sum + fold8(e), gain_sum + fold8(e * normal))

    start = jnp.zeros((8, width), F32)
    bias_sum, gain_sum = lax.fori_loop(0, rows // CELL, one_cell, (start, start))
    send_sums(bias_sum, gain_sum, msg_ref)


def input_grad_kernel(
    place_ref, valid_ref, grad_ref, up, down, side, dpre_ref, out_ref
):
    add_halo(place_ref, grad_ref, out_ref, (up, down, side))

    def one_cell(c, carry):
        rows = cell_rows(c)
        out_ref[rows, :] = (out_ref[rows, :] + dpre_ref[rows, :]) * valid_ref[c]
        return carry

    lax.fori_loop(0, out_ref.shape[0] // CELL, one_cell, 0)


def temporal_kernel(
    valid_ref, s_ref, msg_ref, gb_ref, wt_ref, columns_ref, t_ref, stats_ref, out_ref, *, index
):
    rows, middle = s_ref.shape
    mean, rstd, count = receive_stats(msg_ref)
    keep_stats(stats_ref, mean, rstd, count)
    gain, bias = gb_ref[2 * index : 2 * index + 1, :], gb_ref[2 * index + 1 : 2 * index + 2, :]

    def one_cell(c, _):
        value = (s_ref[cell_rows(c), :] - mean) * rstd * gain + bias
        inner = value * sigmoid(value) * valid_ref[c]
        columns_ref[cell_rows(c), 0:middle] = earlier_frame(inner).astype(BF16)
        columns_ref[cell_rows(c), middle : 2 * middle] = inner.astype(BF16)
        columns_ref[cell_rows(c), 2 * middle : 3 * middle] = later_frame(inner).astype(BF16)
        return 0

    lax.fori_loop(0, rows // CELL, one_cell, 0)

    def one_block(i, _):
        t_ref[block_rows(i, 320), :] = jnp.dot(
            columns_ref[block_rows(i, 320), :], wt_ref[...], preferred_element_type=F32
        )
        return 0

    lax.fori_loop(0, rows // 320, one_block, 0)
    send_stats(t_ref, valid_ref, out_ref)


def middle_kernel(
    place_ref, valid_ref, t_ref, msg_ref, gb_ref, stats_ref, tile_ref, top, bottom, side, *, index,
):
    width = t_ref.shape[1]
    rows, cols = tile_ref.shape[:2]
    mean, rstd, count = receive_stats(msg_ref)
    keep_stats(stats_ref, mean, rstd, count)
    gain, bias = gb_ref[2 * index : 2 * index + 1, :width], gb_ref[2 * index + 1 : 2 * index + 2, :width]
    for r in range(rows):
        for c in range(cols):
            number = r * cols + c
            value = (t_ref[number * CELL : (number + 1) * CELL, :] - mean) * rstd * gain + bias
            tile_ref[r, c] = (value * sigmoid(value) * valid_ref[number]).astype(BF16)
    write_edges(place_ref, tile_ref, (top, bottom, side))


def top_kernel(
    valid_ref, t_ref, msg_ref, gb_ref, x_ref, cot_ref, stats_ref, out_ref, dpre_ref, msg_out, *, index
):
    rows, width = t_ref.shape
    mean, rstd, count = receive_stats(msg_ref)
    keep_stats(stats_ref, mean, rstd, count)
    gain, bias = gb_ref[2 * index : 2 * index + 1, :width], gb_ref[2 * index + 1 : 2 * index + 2, :width]

    def one_cell(c, carry):
        bias_sum, gain_sum = carry
        normal = (t_ref[cell_rows(c), :] - mean) * rstd
        pre = normal * gain + bias + x_ref[cell_rows(c), :].astype(F32)
        sigma = sigmoid(pre)
        valid = valid_ref[c]
        out_ref[cell_rows(c), :] = pre * sigma * valid
        dpre = cot_ref[cell_rows(c), :].astype(F32) * valid * (sigma * (1.0 + pre * (1.0 - sigma)))
        dpre_ref[cell_rows(c), :] = dpre
        return (bias_sum + fold8(dpre), gain_sum + fold8(dpre * normal))

    start = jnp.zeros((8, width), F32)
    bias_sum, gain_sum = lax.fori_loop(0, rows // CELL, one_cell, (start, start))
    send_sums(bias_sum, gain_sum, msg_out)


def temporal_grad_kernel(
    valid_ref, e_ref, t_ref, tstats_ref, msg_ref, s_ref, sstats_ref, gb_ref, wt_ref,
    dt_ref, en_ref, sums_ref, msg_out, columns_ref, *, index,
):
    rows, width = e_ref.shape
    middle = s_ref.shape[1]
    bias_grad, gain_grad = receive_sums(msg_ref)
    sums_ref[0:1, :] = gain_grad
    sums_ref[1:2, :] = bias_grad
    mean, rstd, count = tstats_ref[0:1, :], tstats_ref[1:2, :], tstats_ref[2:3, :]
    gain = gb_ref[2 * index + 2 : 2 * index + 3, :width]

    def one_cell(c, _):
        normal = (t_ref[cell_rows(c), :] - mean) * rstd
        dt = (rstd * gain) * (
            e_ref[cell_rows(c), :] - valid_ref[c] * ((bias_grad + normal * gain_grad) / count)
        )
        dt_ref[cell_rows(c), :] = dt.astype(BF16)
        columns_ref[cell_rows(c), 0:width] = later_frame(dt).astype(BF16)
        columns_ref[cell_rows(c), width : 2 * width] = dt.astype(BF16)
        columns_ref[cell_rows(c), 2 * width : 3 * width] = earlier_frame(dt).astype(BF16)
        return 0

    lax.fori_loop(0, rows // CELL, one_cell, 0)

    def one_block(i, _):
        total = None
        for tap in range(3):
            term = lax.dot_general(
                columns_ref[block_rows(i, 320), tap * width : (tap + 1) * width],
                wt_ref[tap * middle : (tap + 1) * middle, :],
                (((1,), (1,)), ((), ())),
                preferred_element_type=F32,
            )
            total = term if total is None else total + term
        en_ref[block_rows(i, 320), :] = total
        return 0

    lax.fori_loop(0, rows // 320, one_block, 0)
    mean_s, rstd_s = sstats_ref[0:1, :], sstats_ref[1:2, :]
    gain_s, bias_s = gb_ref[2 * index : 2 * index + 1, :], gb_ref[2 * index + 1 : 2 * index + 2, :]

    def one_mid_cell(c, carry):
        bias_sum, gain_sum = carry
        normal = (s_ref[cell_rows(c), :] - mean_s) * rstd_s
        value = normal * gain_s + bias_s
        sigma = sigmoid(value)
        e = en_ref[cell_rows(c), :] * valid_ref[c] * (sigma * (1.0 + value * (1.0 - sigma)))
        en_ref[cell_rows(c), :] = e
        return (bias_sum + fold8(e), gain_sum + fold8(e * normal))

    start = jnp.zeros((8, middle), F32)
    bias_sum, gain_sum = lax.fori_loop(0, rows // CELL, one_mid_cell, (start, start))
    send_sums(bias_sum, gain_sum, msg_out)


def temporal_weight_kernel(columns_ref, dt_ref, grad_ref):
    middle = columns_ref.shape[1] // 3
    for tap in range(3):
        grad_ref[tap * middle : (tap + 1) * middle, :] = lax.dot_general(
            columns_ref[:, tap * middle : (tap + 1) * middle],
            dt_ref[...],
            (((0,), (0,)), ((), ())),
            preferred_element_type=F32,
        )


def ds_kernel(
    place_ref, valid_ref, en_ref, s_ref, stats_ref, msg_ref, gb_ref, ws_ref,
    sums_ref, ds_ref, top, bottom, side, row_ref, *, index,
):
    rows, cols = ds_ref.shape[0], ds_ref.shape[1] - 4
    bias_grad, gain_grad = receive_sums(msg_ref)
    sums_ref[0:1, :] = gain_grad
    sums_ref[1:2, :] = bias_grad
    mean, rstd, count = stats_ref[0:1, :], stats_ref[1:2, :], stats_ref[2:3, :]
    scale = rstd * gb_ref[2 * index : 2 * index + 1, :]
    for r in range(rows):
        for c in (0, 1, cols + 2, cols + 3):
            ds_ref[r, c] = jnp.zeros(ds_ref.shape[2:], BF16)
        for c in range(cols):
            number = r * cols + c
            block = slice(number * CELL, (number + 1) * CELL)
            normal = (s_ref[block, :] - mean) * rstd
            ds_ref[r, c + 2] = (
                scale
                * (en_ref[block, :] - valid_ref[number] * ((bias_grad + normal * gain_grad) / count))
            ).astype(BF16)
    edge_grads(place_ref, ds_ref, ws_ref, (top, bottom, side), row_ref)


def run(
    kernel, ins, outs, scratch=(), scalars=0, us=1.0, extra=8, loose=(), spec=VMEM, aliases=(), **settings
):
    held = sum(
        math.prod(x.shape) * jnp.dtype(x.dtype).itemsize
        for x in scratch
        if x.memory_space == pltpu.VMEM
    )
    return pl.pallas_call(
        functools.partial(kernel, **settings),
        out_shape=[
            jax.ShapeDtypeStruct(shape, dtype) if i in loose else pltpu.VMEM(shape, dtype)
            for i, (shape, dtype) in enumerate(outs)
        ],
        in_specs=[SMEM] * scalars + [spec] * (len(ins) - scalars),
        out_specs=[VMEM] * len(outs),
        scratch_shapes=list(scratch),
        input_output_aliases=dict(aliases),
        cost_estimate=pl.CostEstimate(
            flops=int(us * 1.1e9), bytes_accessed=1000, transcendentals=0
        ),
        compiler_params=pltpu.CompilerParams(vmem_limit_bytes=held + extra * 2**20),
    )(*ins)


def ranks_of_pieces(owner_ids, devices):
    block = 64
    onehot = (owner_ids.reshape(-1, block, 1) == jnp.arange(devices, dtype=jnp.int32)).astype(BF16)
    earlier = jnp.tril(jnp.ones((block, block), BF16), -1)
    within = jnp.einsum("ij,bjd->bid", earlier, onehot, preferred_element_type=F32)
    sums = jnp.sum(onehot.astype(F32), axis=1)
    blocks = jnp.tril(jnp.ones((sums.shape[0],) * 2, F32), -1)
    before = jnp.sum(blocks[:, :, None] * sums[None], axis=1)
    ranking = jnp.sum(onehot.astype(F32) * (within + before[:, None, :]), axis=-1)
    return ranking.reshape(-1).astype(jnp.int32)


def moved_by(step, size):
    return [(i, (i + step) % size) for i in range(size)]


def mirrored(bit, size):
    return [(i, i ^ bit) for i in range(size)]


def gather_batch(own):
    batches = lax.axis_size("batch")
    return [own] + [lax.ppermute(own, "batch", moved_by(k, batches)) for k in range(1, batches)]


def gather_chips_first(steps):
    heights, half = lax.axis_size("ha"), len(steps) // 2
    one, two = jnp.concatenate(steps[:half]), jnp.concatenate(steps[half:])
    one = jnp.concatenate([one, lax.ppermute(one, "ha", mirrored(1, heights))])
    two = jnp.concatenate([two, lax.ppermute(two, "ha", mirrored(2, heights))])
    return one, two


def gather_chips_second(one, two, beside):
    heights = lax.axis_size("ha")
    across = mirrored(1, 2)
    one_next = lax.ppermute(one, "ha", mirrored(2, heights))
    two_next = lax.ppermute(two, "ha", mirrored(1, heights))
    others = [lax.ppermute(one, "wa", across), lax.ppermute(two, "wa", across)]
    one_next, two_next, beside = together(one_next, two_next, beside)
    others = [
        others[0],
        lax.ppermute(one_next, "wa", across),
        others[1],
        lax.ppermute(two_next, "wa", across),
    ]
    return [one, one_next, two, two_next] + others, beside


def part_position(owner_ids, place):
    batches, heights, cores = (lax.axis_size(axis) for axis in AXES)
    z, h, w = place
    core = (owner_ids % cores) ^ w
    turn = (owner_ids // cores % heights) ^ h
    step = (z - owner_ids // (cores * heights)) % batches
    half = batches // 2
    swapped = jnp.where(turn == 1, 2, jnp.where(turn == 2, 1, turn))
    block = jnp.where(
        step < half, turn * half + step, heights * half + swapped * half + step - half
    )
    return core * batches * heights + block


def target_position(owner_ids, place):
    batches, heights, cores = (lax.axis_size(axis) for axis in AXES)
    z, h, w = place
    core = (owner_ids % cores) ^ w
    turn = (owner_ids // cores % heights) ^ h
    step = (owner_ids // (cores * heights) - z) % batches
    return (core * heights + turn) * batches + step


def add_low(a, b):
    return (a.astype(F32) + b.astype(F32)).astype(BF16)


def sum_cores(packed):
    sent, kept = packed
    return [kept, lax.ppermute(sent, "wa", mirrored(1, 2))]


def added(terms, block, part, rows):
    half = rows // 2
    start = block * rows + part * half
    return add_low(*[t[start : start + half] for t in terms])


def move_chips_first(terms, rows):
    heights = lax.axis_size("ha")
    one = jnp.stack([added(terms, 1, 0, rows), added(terms, 3, 0, rows)])
    two = jnp.stack([added(terms, 2, 1, rows), added(terms, 3, 1, rows)])
    return (
        lax.ppermute(one, "ha", mirrored(1, heights)),
        lax.ppermute(two, "ha", mirrored(2, heights)),
    )


def add_chips_first(terms, moved, rows):
    one, two = moved
    return [
        add_low(added(terms, 0, 0, rows), one[0]),
        add_low(added(terms, 2, 0, rows), one[1]),
        add_low(added(terms, 0, 1, rows), two[0]),
        add_low(added(terms, 1, 1, rows), two[1]),
    ]


def move_chips_second(sums):
    heights = lax.axis_size("ha")
    return (
        lax.ppermute(sums[1], "ha", mirrored(2, heights)),
        lax.ppermute(sums[3], "ha", mirrored(1, heights)),
    )


def add_chips_second(sums, moved):
    own = jnp.concatenate([add_low(sums[0], moved[0]), add_low(sums[2], moved[1])])
    return own.reshape(lax.axis_size("batch"), -1, LANES)


def move_batch(own):
    batches = own.shape[0]
    return [lax.ppermute(own[k], "batch", moved_by(k, batches)) for k in range(1, batches)]


def add_batch(own, moved):
    total = own[0].astype(F32)
    for block in moved:
        total = total + block.astype(F32)
    return total


def scatter_sums(packed, rows):
    terms = sum_cores(packed)
    sums = add_chips_first(terms, move_chips_first(terms, rows), rows)
    own = add_chips_second(sums, move_chips_second(sums))
    return add_batch(own, move_batch(own))


def together(*values):
    return lax.optimization_barrier(values)


def exchange(message):
    return lax.all_to_all(message, AXES, 0, 0, tiled=True)


def swap_side(side):
    return lax.ppermute(side, "wa", mirrored(1, 2))


def swap_rows(top, bottom):
    count = lax.axis_size("ha")
    forward = [(i, i + 1) for i in range(count - 1)]
    backward = [(i + 1, i) for i in range(count - 1)]
    return [lax.ppermute(bottom, "ha", forward), lax.ppermute(top, "ha", backward)]


def swap_values(edges, side):
    top, bottom, _ = edges
    rows = swap_rows(
        jnp.concatenate([top, side[:1]]), jnp.concatenate([bottom, side[-1:]])
    )
    return rows + [side]


def with_ends(at_edge, edges, side):
    top, bottom, _ = edges
    return [
        jnp.where(at_edge[:, None, None], add_low(row, side[end][None]), row)
        for row, end in ((top, 0), (bottom, -1))
    ]


def per_device(
    block_input,
    cotangent,
    frame_sides,
    owner_list,
    master_slots,
    first_slots,
    second_slots,
    norm_gains,
    norm_biases,
    norm_first,
    norm_second,
):
    clip_count, frames, tile_rows, tile_cols, width = block_input.shape
    devices = lax.axis_size(AXES)
    slot_count, piece_len = master_slots.shape
    middle = norm_gains.shape[0] // 2 - width
    middle_pad = -(-middle // LANES) * LANES
    rows = clip_count * frames * tile_rows * tile_cols

    low_slots = master_slots.astype(BF16).reshape(slot_count * PIECE_ROWS, LANES)

    steps = gather_batch(low_slots)

    own_side = frame_sides[0]
    row_ids = lax.axis_index("ha") * tile_rows + jnp.arange(tile_rows, dtype=jnp.int32)
    col_ids = lax.axis_index("wa") * tile_cols + jnp.arange(tile_cols, dtype=jnp.int32)
    grid_rows = tile_rows * lax.axis_size("ha")
    grid_cols = tile_cols * lax.axis_size("wa")
    valid = (
        (row_ids[:, None] >= grid_rows - own_side) & (col_ids[None, :] >= grid_cols - own_side)
    ).astype(F32)
    valid_flat = valid.reshape(-1)
    place = lax.axis_index("wa").reshape(1)
    def to_tile(array):
        return jnp.transpose(array, (2, 3, 1, 0, 4)).reshape(tile_rows, tile_cols, CELL, width)

    x_tile = to_tile(block_input) * valid[:, :, None, None].astype(BF16)
    edge = jnp.where(place[0] == 0, tile_cols - 1, 0)
    x_side = lax.dynamic_index_in_dim(x_tile, edge, axis=1, keepdims=False)
    x_halo = swap_values((x_tile[0], x_tile[-1], x_side), swap_side(x_side))
    steps, x_tile, x_halo, cotangent, owner_list, norm_gains, norm_biases = together(
        steps, x_tile, x_halo, cotangent, owner_list, norm_gains, norm_biases
    )
    one, two = gather_chips_first(steps)

    cot_tile = to_tile(cotangent)
    owner_ids = owner_list[:, 0]
    ranking = ranks_of_pieces(owner_ids, devices)
    here = [lax.axis_index(axis) for axis in AXES]
    slot_index = (part_position(owner_ids, here) * slot_count + ranking) * PIECE_ROWS
    half = owner_list.shape[0] // 2
    kept = min(slot_count, int(slot_count / 2 + 1.7 * math.sqrt(slot_count)))
    rest = max(slot_count - kept, 1)
    target = target_position(owner_ids, here)
    fits = jnp.all(ranking[:half] < kept)

    def spare_rows(slots):
        return -(-(devices // 2 * slots + 1) * PIECE_ROWS // 128) * 128

    def by_core(number, rank, slots, here):
        spare = devices // 2 * slots * PIECE_ROWS
        place = (number * slots + rank) * PIECE_ROWS
        return (
            jnp.where(here & (place >= spare), place - spare, spare),
            jnp.where(here & (place < spare), place, spare),
        )

    late_two = fits & (ranking[half:] < kept)
    places1 = by_core(target[:half], ranking[:half], kept, fits)
    places2 = by_core(target[half:], ranking[half:], kept, late_two) + by_core(
        target[half:], ranking[half:] - (slot_count - rest), rest, fits & ~late_two
    )

    bounds = [0, middle, middle + width, 2 * middle + width, 2 * middle + 2 * width]
    gb = []
    for i in range(4):
        for vector in (norm_gains, norm_biases):
            part = vector[bounds[i] : bounds[i + 1]]
            gb.append(jnp.pad(part, (0, middle_pad - part.shape[0])))
    gb = jnp.stack(gb)

    at_edge = jnp.arange(tile_cols) == edge
    prepared = (at_edge, x_tile, x_halo, cot_tile, valid_flat, gb, slot_index, places1, places2, fits)
    parts, prepared = gather_chips_second(one, two, prepared)
    at_edge, x_tile, x_halo, cot_tile, valid_flat, gb, slot_index, places1, places2, fits = prepared

    tap_rows = 9 * width
    stage = [pltpu.VMEM((UNROLL, 144, LANES), F32), pltpu.VMEM((UNROLL, 5, 32, LANES), F32)]
    weight_shapes = [((tap_rows, middle_pad), BF16), ((3 * middle_pad, width), BF16)]
    (all_weights,) = run(
        gather_weights_kernel,
        parts,
        [((devices * slot_count * PIECE_ROWS, LANES), BF16)],
        [pltpu.SemaphoreType.DMA((len(parts),))],
        us=3.0,
        spec=pl.BlockSpec(memory_space=pl.ANY),
    )

    def unpack(all_weights, unit):
        return run(
            unpack_weights_kernel,
            [slot_index, all_weights],
            weight_shapes,
            stage,
            1,
            4.3,
            base=unit * (owner_list.shape[0] // 2),
        )

    tile_shape = (tile_rows, tile_cols, CELL, width)
    padded_tile = (tile_rows + 2, tile_cols + 2, CELL, width)
    ds_shape = (tile_rows, tile_cols + 4, CELL, middle_pad)
    stats_mid = (devices, 1, 2 * middle_pad + LANES)
    stats_wide = (devices, 1, 2 * width + LANES)

    def edge_shapes(lanes, beside=0):
        row, col = (tile_cols, CELL, lanes), (tile_rows + beside, CELL, lanes)
        return [(row, BF16), (row, BF16), (col, BF16)]

    def unit_forward(tile, halo, ws, wt, index):
        padded, s, msg = run(
            spatial_kernel,
            [place, valid_flat, tile, *halo, ws],
            [(padded_tile, BF16), ((rows, middle_pad), F32), (stats_mid, F32)],
            us=5.5,
            scalars=2,
        )
        columns, t, s_stats, msg = run(
            temporal_kernel,
            [valid_flat, s, exchange(msg), gb, wt],
            [
                ((rows, 3 * middle_pad), BF16),
                ((rows, width), F32),
                ((8, middle_pad), F32),
                (stats_wide, F32),
            ],
            scalars=1,
            us=4.2,
            index=index,
        )
        return padded, s, s_stats, columns, t, exchange(msg)

    ws1, wt1 = unpack(all_weights, 0)
    padded1, s1, s_stats1, columns1, t1, msg = unit_forward(x_tile, x_halo, ws1, wt1, 0)
    t_stats1, y_tile, *edges = run(
        middle_kernel,
        [place, valid_flat, t1, msg, gb],
        [((8, width), F32), (tile_shape, BF16)] + edge_shapes(width),
        scalars=2,
        index=1,
    )
    y_in, all_weights = together(swap_side(edges[2]), all_weights)
    halo = swap_values(edges, y_in)
    ws2, wt2 = unpack(all_weights, 1)
    ws2, wt2, halo = together(ws2, wt2, halo)
    padded2, s2, s_stats2, columns2, t2, msg = unit_forward(y_tile, halo, ws2, wt2, 2)
    t_stats2, block_output, dpre, msg = run(
        top_kernel,
        [valid_flat, t2, msg, gb, x_tile.reshape(rows, width), cot_tile.reshape(rows, width)],
        [((8, width), F32), ((rows, width), F32), ((rows, width), F32), ((devices, 1, 2 * width), F32)],
        scalars=1,
        loose=(1,),
        index=3,
    )

    batch_rows = lax.axis_size("batch") * PIECE_ROWS

    def pack(grads, places, slots, begun=()):
        shapes = [((spare_rows(n), LANES), BF16) for n in slots for _ in range(2)]
        first = len(places) + 2
        return run(
            pack_grads_kernel,
            [*places, *grads, *begun],
            shapes,
            stage,
            scalars=len(places),
            us=0.1,
            aliases={first + i: i for i in range(len(begun))},
            places=len(places),
            begun=len(begun),
        )

    def unit_backward(e, msg, t, t_stats, s, s_stats, columns, padded, ws, wt, index, aside=None):
        dt, en, t_sums, msg = run(
            temporal_grad_kernel,
            [valid_flat, e, t, t_stats, exchange(msg), s, s_stats, gb, wt],
            [
                ((rows, width), BF16),
                ((rows, middle_pad), F32),
                ((2, width), F32),
                ((devices, 1, 2 * middle_pad), F32),
            ],
            [pltpu.VMEM((rows, 3 * width), BF16)],
            scalars=1,
            us=4.5,
            index=index,
        )
        if aside is not None:
            msg, aside = together(msg, sum_cores(aside))
        msg = exchange(msg)
        if aside is not None:
            msg, aside = together(msg, aside)
            moved = move_chips_first(aside, batch_rows * rest)
        s_sums, ds, *edges = run(
            ds_kernel,
            [place, valid_flat, en, s, s_stats, msg, gb, ws],
            [((2, middle_pad), F32), (ds_shape, BF16)] + edge_shapes(width, 2),
            [pltpu.VMEM((tile_cols + 1, CELL, width), BF16)],
            scalars=2,
            us=4.0,
            index=index,
        )
        edges, columns, dt = together(edges, columns, dt)
        (wt_grad,) = run(temporal_weight_kernel, [columns, dt], [((3 * middle_pad, width), F32)], us=0.1)
        wt_grad, padded = together(wt_grad, padded)
        (ws_grad,) = run(spatial_weight_kernel, [padded, ds], [((tap_rows, middle_pad), F32)], us=0.1)
        return ds, edges, (ws_grad, wt_grad), s_sums, t_sums, aside and (aside, moved)

    def inner_grad(ds, ws):
        return run(spatial_grad_kernel, [ds, ws], [((rows, width), F32)], us=0.1)[0]

    ds, edges, grads2, s_sums2, t_sums2, _ = unit_backward(
        dpre, msg, t2, t_stats2, s2, s_stats2, columns2, padded2, ws2, wt2, 2
    )
    side = swap_side(edges[2])
    halo = swap_rows(*with_ends(at_edge, edges, side)) + [side]
    inner, halo, grads2 = together(inner_grad(ds, ws2), halo, grads2)
    *begun, sent2, kept2 = pack(grads2, places2, (kept, rest))
    packed2 = sent2, kept2
    inner, packed2 = together(inner, packed2)
    e1, msg = run(
        between_kernel,
        [place, valid_flat, inner, *halo, t1, t_stats1, gb],
        [((rows, width), F32), ((devices, 1, 2 * width), F32)],
        scalars=2,
        us=2.0,
        index=1,
    )
    ds, edges, grads1, s_sums1, t_sums1, moving2 = unit_backward(
        e1, msg, t1, t_stats1, s1, s_stats1, columns1, padded1, ws1, wt1, 0, packed2
    )
    packed1, moving2, edges, ds = together(
        pack(grads1, places1, (kept,), begun), moving2, edges, ds
    )
    first2 = add_chips_first(*moving2, batch_rows * rest)
    side, ds = together(swap_side(edges[2]), ds)
    terms1, moved2, side, inner, first2 = together(
        sum_cores(packed1), move_chips_second(first2), side, inner_grad(ds, ws1), first2
    )
    own2 = add_chips_second(first2, moved2)
    moved1, moved2, ends, block_output, terms1, own2 = together(
        move_chips_first(terms1, batch_rows * kept),
        move_batch(own2),
        with_ends(at_edge, edges, side),
        block_output,
        terms1,
        own2,
    )
    first1 = add_chips_first(terms1, moved1, batch_rows * kept)
    sums = (own2, moved2, s_sums1, t_sums1, s_sums2, t_sums2)
    moved1, ends, sums, first1 = together(move_chips_second(first1), ends, sums, first1)
    own2, moved2, s_sums1, t_sums1, s_sums2, t_sums2 = sums
    own1 = add_chips_second(first1, moved1)
    moved1, rows_in, own1 = together(move_batch(own1), swap_rows(*ends), own1)
    (input_grad,) = run(
        input_grad_kernel,
        [place, valid_flat, inner, *rows_in, side, dpre],
        [((rows, width), F32)],
        scalars=2,
        us=2.0,
        loose=(0,),
    )
    sums1, sums2 = add_batch(own1, moved1), add_batch(own2, moved2)

    def joined(first, last):
        after, before = [(slot_count - n) * PIECE_ROWS for n in (kept, rest)]
        return jnp.pad(first, ((0, after), (0, 0))) + jnp.pad(last, ((before, 0), (0, 0)))

    def whole(grads1, grads2):
        packed = [
            pack(grads, by_core(target[part], ranking[part], slot_count, True), (slot_count,))
            for grads, part in ((grads1, slice(0, half)), (grads2, slice(half, None)))
        ]
        return scatter_sums([a + b for a, b in zip(*packed)], batch_rows * slot_count)

    if kept == slot_count:
        grad_mine = joined(sums1, sums2)
    else:
        grad_mine = lax.cond(
            fits,
            lambda early, late, *_: joined(early, late),
            lambda early, late, ones, twos: whole(ones, twos),
            sums1,
            sums2,
            grads1,
            grads2,
        )

    def from_tile(array):
        array = array.reshape(tile_rows, tile_cols, frames, clip_count, width)
        return jnp.transpose(array, (3, 2, 0, 1, 4))

    grad_mine = grad_mine.reshape(slot_count, piece_len)
    correction = 1.0 - 0.5**STEP
    step_rate = 1.8 / math.sqrt(9.0 * width)
    first_new = 0.5 * first_slots + 0.5 * grad_mine
    second_new = 0.5 * second_slots + 0.5 * grad_mine * grad_mine
    master_new = master_slots - step_rate * (
        first_new / correction / (jnp.sqrt(second_new / correction) + ADAM_EPSILON)
        + DECAY_RATE * master_slots
    )
    weight_copy = master_new.astype(BF16)
    norm_grad = jnp.concatenate([s_sums1[:, :middle], t_sums1, s_sums2[:, :middle], t_sums2], axis=1)
    norm_pair = jnp.stack([norm_gains, norm_biases])
    norm_first_new = 0.5 * norm_first + 0.5 * norm_grad
    norm_second_new = 0.5 * norm_second + 0.5 * norm_grad * norm_grad
    norm_new = norm_pair - NORM_RATE * (norm_first_new / correction) / (
        jnp.sqrt(norm_second_new / correction) + ADAM_EPSILON
    )
    return (
        from_tile(block_output),
        from_tile(input_grad),
        master_new,
        first_new,
        second_new,
        weight_copy,
        norm_first_new,
        norm_second_new,
        norm_new,
    )


def solution(mesh):
    wide = P("batch", None, "ha", "wa", None)
    owned = P(AXES, None)
    return jax.shard_map(
        per_device,
        mesh=mesh,
        in_specs=(wide, wide, P("batch"), P(), owned, owned, owned, P(), P(), P(), P()),
        out_specs=(wide, wide, owned, owned, owned, owned, P(), P(), P()),
        check_vma=False,
    )
```
